32 devices in a mesh: dp: 8 (over z, y), mp: 4 (over x, core).
Axes of the slice: x: 2, y: 2, z: 4, core: 2. Of those that a mesh axis runs over, the one named last changes fastest.
Arguments:
- latents: float32 [64, 256, 1152], P('dp', None, 'mp'), may hold values from -6 to 6
- condition: float32 [64, 1152], P('dp', 'mp'), may hold values from -6 to 6
- cotangent: float32 [64, 256, 1152], P('dp', None, 'mp'), may hold values from -6 to 6
- noise_bins: int32 [64], P('dp'), may hold values from 0 to 7
- image_counts: int32 [8], P('dp'), may hold values from 0 to 8, as said below
- ada_weight: bfloat16 [1152, 6, 1152], P(None, None, 'mp'), may hold values from -0.1875 to 0.1875
- ada_bias: bfloat16 [6, 1152], P(None, 'mp'), may hold values from -3 to 3
- qkv_weight: bfloat16 [1152, 3, 1152], P(None, None, 'mp'), may hold values from -0.1875 to 0.1875
- norm_gains: bfloat16 [2, 72], replicated, may hold values from 0.796875 to 1.59375
- proj_weight: bfloat16 [1152, 1152], P('mp'), may hold values from -0.5 to 0.5
- gate_up_weight: bfloat16 [1152, 2, 3072], P(None, None, 'mp'), may hold values from -0.1875 to 0.1875
- down_weight: bfloat16 [3072, 1152], P('mp'), may hold values from -0.109375 to 0.109375
Outputs:
- output: float32 [64, 256, 1152], P('dp', None, 'mp')
- grad_latents: float32 [64, 256, 1152], P('dp', None, 'mp')
- grad_condition: float32 [64, 1152], P('dp', 'mp')
- grad_ada_weight: float32 [1152, 6, 1152], P(None, None, 'mp')
- grad_ada_bias: float32 [6, 1152], P(None, 'mp')
- grad_qkv_weight: float32 [1152, 3, 1152], P(None, None, 'mp')
- grad_norm_gains: float32 [2, 72], replicated
- grad_proj_weight: float32 [1152, 1152], P('mp')
- grad_gate_up_weight: float32 [1152, 2, 3072], P(None, None, 'mp')
- grad_down_weight: float32 [3072, 1152], P('mp')
The draws below stay inside these ranges and needn't reach their ends.
Inputs may be any that keep to these rules, and one draw needn't show every extreme that they name: The live slots of a device are its first image_counts ones; the counts sum to 32. Numbering all live images in the order of devices and then slots, from 0, every image's number lies in its own device's block of 4 numbers (device index times 4 onwards) or in the next device's block.
All inputs are finite; a program needn't handle non-finite values.
Results may differ from the reference program's by a relative error of at most 0.013.
Values may be sent and summed in bfloat16 or wider, within the bound.
No kernel may reach another device: no remote copies, remote signals or barrier semaphores. Data moves between devices by JAX's collectives and lax.ppermute only.
A program may use at most 192 MiB of HBM per device.

```python
import math
import jax
import jax.numpy as jnp
import numpy as np
from jax import lax

D = 1152
HEADS = 16
HEAD = 72
FF = 3072
P_SIZE = 256
GRID = 16
IMG_DEV = 4
NBINS = 8
SLOTS = 8
ALL_SLOTS = 64
IMAGES = 32
N_DP = 8


def draw_image_counts(key, part):
    key = jax.random.fold_in(key, 7)
    key_one, key_two, key_three = jax.random.split(key, 3)
    excess = jnp.minimum(jax.random.randint(key_one, (N_DP,), 0, IMG_DEV + 1), jax.random.randint(key_two, (N_DP,), 0, IMG_DEV + 1))
    fullest = jax.random.randint(key_three, (), 1, N_DP - 1)
    device_ids = jnp.arange(N_DP)
    excess = jnp.where(device_ids == fullest - 1, 0, excess)
    excess = jnp.where(device_ids == fullest, IMG_DEV, excess)
    excess = jnp.where((device_ids == fullest + 1) | (device_ids == N_DP - 1), 0, excess)
    before = jnp.concatenate([jnp.zeros((1,), jnp.int32), excess[:-1].astype(jnp.int32)])
    return (IMG_DEV + excess - before).astype(jnp.int32)


def place_ends(result, stream_key, smallest, high):
    place = [jax.random.randint(jax.random.fold_in(stream_key, axis), (), 0, length) for axis, length in enumerate(result.shape)]
    longest = result.shape.index(max(result.shape))
    neighbour = place[:longest] + [(place[longest] + 1) % result.shape[longest]] + place[longest + 1:]
    return result.at[tuple(place)].set(smallest).at[tuple(neighbour)].set(high)


def levels(own_key, dims, pieces, low, top_value):
    level = 1.0
    for dim, blocks in pieces:
        heights = jax.random.uniform(jax.random.fold_in(jax.random.fold_in(own_key, 6), dim), (blocks,), jnp.float32, low / len(pieces), top_value / len(pieces))
        level = level * jnp.repeat(jnp.exp(heights), dims[dim] // blocks).reshape((-1,) + (1,) * (len(dims) - 1 - dim))
    return level


def rank_table(amount, slope):
    loads = [(1 << 20) // math.isqrt(grade ** slope) + 1 for grade in range(1, amount + 1)]
    deviation = 1 + sum(loads) // (1 << 30)
    return np.cumsum(np.array([max(1, weight // deviation) for weight in loads]))


def ranked_ids(stream_key, dims, number_of, lean):
    table = rank_table(number_of, lean)
    lot = jax.random.randint(jax.random.fold_in(stream_key, 1), dims, 0, int(table[number_of - 1]))
    grade = jnp.searchsorted(jnp.asarray(table, jnp.int32), lot, side="right")
    return jax.random.permutation(jax.random.fold_in(stream_key, 2), number_of)[grade].astype(jnp.int32)


def centred(rng, extent, deviation, most, shards=(), kind=jnp.bfloat16):
    values = jax.random.normal(rng, extent, jnp.float32) * deviation
    if len(shards) > 0:
        values = levels(rng, extent, shards, -0.22, 0.18) * values
    return jnp.clip(values, min=-most, max=most).astype(kind)


def setup_inputs(seed: int = 0) -> dict:
    splits = jax.random.split(jax.random.key(seed), 13)
    return {
        "latents": centred(splits[0], (ALL_SLOTS, P_SIZE, D), 1.0, 6.0, ((0, 8), (2, 4)), jnp.float32),
        "condition": centred(splits[1], (ALL_SLOTS, D), 1.0, 6.0, ((0, 8), (1, 4)), jnp.float32),
        "cotangent": centred(splits[2], (ALL_SLOTS, P_SIZE, D), 1.0, 6.0, ((0, 8), (2, 4)), jnp.float32),
        "noise_bins": place_ends(ranked_ids(splits[3], (ALL_SLOTS,), NBINS, 2), jax.random.fold_in(splits[3], 3), 0, NBINS - 1).astype(jnp.int32),
        "image_counts": draw_image_counts(jax.random.fold_in(splits[12], 71), 0),
        "ada_weight": centred(splits[5], (D, 6, D), D ** -0.5, 0.1875, ((2, 4),)),
        "ada_bias": centred(splits[6], (6, D), 0.5, 3.0, ((1, 4),)),
        "qkv_weight": centred(splits[7], (D, 3, D), D ** -0.5, 0.1875, ((2, 4),)),
        "norm_gains": jnp.clip(jax.random.uniform(splits[8], (2, HEAD), jnp.float32, 0.796875, 1.59375), 0.796875, 1.59375).astype(jnp.bfloat16),
        "proj_weight": centred(splits[9], (D, D), (D // 8) ** -0.5, 0.5, ((0, 4),)),
        "gate_up_weight": centred(splits[10], (D, 2, FF), D ** -0.5, 0.1875, ((2, 4),)),
        "down_weight": centred(splits[11], (FF, D), FF ** -0.5, 0.109375, ((0, 4),)),
    }


EPSILON = 1e-06
PRECISE = lax.Precision.HIGHEST

@jax.custom_vjp
def low(v):
    return lax.optimization_barrier(v.astype(jnp.bfloat16)).astype(jnp.float32)

@jax.custom_vjp
def low_back(v):
    return v

def low_keep(v):
    return (low(v), None)

def low_pass(kept, grad):
    return (grad,)

def back_keep(v):
    return (v, None)

def back_low(kept, grad):
    return (low(grad),)
low.defvjp(low_keep, low_pass)
low_back.defvjp(back_keep, back_low)

def rope_tables():
    quarter = HEAD // 4
    frequency = 10000.0 ** (-jnp.arange(quarter, dtype=jnp.float32) / quarter)
    patches = jnp.arange(P_SIZE, dtype=jnp.int32)
    row_angle = (patches // GRID).astype(jnp.float32)[:, None, None] * frequency
    col_angle = (patches % GRID).astype(jnp.float32)[:, None, None] * frequency
    return (jnp.cos(row_angle), jnp.sin(row_angle), jnp.cos(col_angle), jnp.sin(col_angle))

def rotate(tensor, rotary_tables, direction):
    cos_row, sin_row, cos_col, sin_col = rotary_tables
    part_a, part_b, part_c, part_d = jnp.split(tensor, 4, axis=-1)
    return jnp.concatenate([part_a * cos_row - direction * part_b * sin_row, part_b * cos_row + direction * part_a * sin_row, part_c * cos_col - direction * part_d * sin_col, part_d * cos_col + direction * part_c * sin_col], axis=-1)

def rms_norm(tensor):
    return tensor * lax.rsqrt(lax.optimization_barrier(jnp.mean(tensor * tensor, axis=-1, keepdims=True)) + EPSILON)

def diffusion_transformer_block(latent_row_block, condition_row_block, block_parameters, rotary_tables):
    ada_weight, ada_bias, qkv_weight, norm_gains, proj_weight, gate_up_weight, down_weight = block_parameters
    images = latent_row_block.shape[0]
    silu_cond = low(jax.nn.silu(condition_row_block))
    modulation = low_back(jnp.einsum('bd,dkf->bkf', silu_cond, ada_weight, precision=PRECISE) + ada_bias)
    shift_one, scale_one, gate_one, shift_two, scale_two, gate_two = jnp.split(modulation, 6, axis=1)
    attn_input = low(rms_norm(latent_row_block) * (1.0 + scale_one) + shift_one)
    projected = low_back(jnp.einsum('bpd,dkf->bpkf', attn_input, qkv_weight, precision=PRECISE))
    projected = projected.reshape(images, P_SIZE, 3, HEADS, HEAD)
    queries = low(rotate(rms_norm(projected[:, :, 0]) * norm_gains[0], rotary_tables, 1.0))
    keys_rot = low(rotate(rms_norm(projected[:, :, 1]) * norm_gains[1], rotary_tables, 1.0))
    values = low(projected[:, :, 2])
    scores = low_back(jnp.einsum('bphe,bqhe->bhpq', queries, keys_rot, precision=PRECISE) * HEAD ** (-0.5))
    attention = low(jax.nn.softmax(scores, axis=-1))
    heads_out = low(low_back(jnp.einsum('bhpq,bqhe->bphe', attention, values, precision=PRECISE)))
    heads_out = heads_out.reshape(images, P_SIZE, D)
    branch_one = low_back(jnp.einsum('bpe,ed->bpd', heads_out, proj_weight, precision=PRECISE))
    middle = latent_row_block + gate_one * branch_one
    mlp_input = low(rms_norm(middle) * (1.0 + scale_two) + shift_two)
    gate_up = low_back(jnp.einsum('bpd,dkf->bpkf', mlp_input, gate_up_weight, precision=PRECISE))
    hidden = low(jax.nn.silu(gate_up[:, :, 0]) * gate_up[:, :, 1])
    branch_two = low_back(jnp.einsum('bpf,fd->bpd', hidden, down_weight, precision=PRECISE))
    return middle + gate_two * branch_two

def reference(latents, condition, cotangent, noise_bins, image_counts, ada_weight, ada_bias, qkv_weight, norm_gains, proj_weight, gate_up_weight, down_weight):
    slot_total = latents.shape[0]
    slot_ids = jnp.arange(slot_total, dtype=jnp.int32)
    live_mask = (slot_ids % SLOTS < image_counts[slot_ids // SLOTS]).astype(jnp.float32)
    onehot = (noise_bins[:, None] == jnp.arange(NBINS, dtype=jnp.int32)[None, :]).astype(jnp.float32)
    histogram = lax.optimization_barrier(jnp.sum(onehot * live_mask[:, None], axis=0))
    bin_load = lax.optimization_barrier(jnp.sum(onehot * histogram[None, :], axis=1))
    scaling = live_mask * IMAGES / (NBINS * (bin_load + 1.0 - live_mask))
    block_parameters = (ada_weight.astype(jnp.float32), ada_bias.astype(jnp.float32), qkv_weight.astype(jnp.float32), norm_gains.astype(jnp.float32), proj_weight.astype(jnp.float32), gate_up_weight.astype(jnp.float32), down_weight.astype(jnp.float32))
    rotary_tables = rope_tables()
    groups = slot_total // 16

    def forward(latent_all, cond_all, *bin_weights):

        def one_group(group_members):
            return diffusion_transformer_block(group_members[0], group_members[1], bin_weights, rotary_tables)
        outputs = lax.map(jax.checkpoint(one_group), (latent_all.reshape(groups, 16, P_SIZE, D), cond_all.reshape(groups, 16, D)))
        return outputs.reshape(slot_total, P_SIZE, D) * live_mask[:, None, None]
    output, pullback = jax.vjp(forward, latents, condition, *block_parameters)
    grad_latents, grad_condition, grad_ada, grad_bias, grad_qkv, grad_gains, grad_proj, grad_gate_up, grad_down = pullback(cotangent * scaling[:, None, None])
    return (output, grad_latents, grad_condition, grad_ada, grad_bias, grad_qkv, grad_gains, grad_proj, grad_gate_up, grad_down)
```

```python
import jax
import jax.numpy as jnp
from jax import lax
from jax.sharding import PartitionSpec as P

D = 1152
HEAD = 72
P_SIZE = 256
GRID = 16
IMG_DEV = 4
NBINS = 8

EPSILON = 1e-06
F32 = jnp.float32
BF16 = jnp.bfloat16


def exchange(value, axis, bit):
    pairs = [(i, i ^ bit) for i in range(lax.axis_size(axis))]
    return lax.ppermute(value, axis, pairs)


def shifted(value, axis, by):
    devices = lax.axis_size(axis)
    pairs = [(i, i + by) for i in range(devices) if 0 <= i + by < devices]
    return lax.ppermute(value, axis, pairs)


def bits_of(axis):
    bits, bit = [], 1
    while bit < lax.axis_size(axis):
        bits.append(bit)
        bit *= 2
    return bits


def has_bit(axis, bit):
    return (lax.axis_index(axis) & bit) != 0


def in_order(mine, other, later, axis, join):
    return jnp.where(later, join([other, mine], axis=axis), join([mine, other], axis=axis))


def gather_small(value, axis, dim):
    for bit in bits_of(axis):
        other = exchange(value, axis, bit)
        value = in_order(value, other, has_bit(axis, bit), dim, jnp.concatenate)
    return value


def sum_small(value, axis):
    for bit in bits_of(axis):
        value = value + exchange(value, axis, bit)
    return value


def spread(piece):
    pair = in_order(piece, exchange(piece, "mp", 2), has_bit("mp", 2), 1, jnp.stack)
    full = in_order(pair, exchange(pair, "mp", 1), has_bit("mp", 1), 2, jnp.stack)
    return full.reshape(piece.shape[0], -1, piece.shape[2])


def pick(value, index, dim):
    return lax.dynamic_index_in_dim(value, index, dim, keepdims=False)


def reduce_parts(partial):
    images, features, patches = partial.shape
    high = has_bit("mp", 2).astype(jnp.int32)
    low = has_bit("mp", 1).astype(jnp.int32)
    value = partial.reshape(images, 2, 2, features // 4, patches)
    received = exchange(pick(value, 1 - low, 2).astype(BF16), "mp", 1)
    value = pick(value, low, 2) + received.astype(F32)
    received = exchange(pick(value, 1 - high, 1).astype(BF16), "mp", 2)
    return pick(value, high, 1) + received.astype(F32)


def reduce_images(total, dim):
    steps = []
    for bit in bits_of("dp"):
        later = has_bit("dp", bit)
        rows = total.shape[dim]
        if rows % 2:
            total = total + exchange(total.astype(BF16), "dp", bit).astype(F32)
            continue
        halves = total.reshape(total.shape[:dim] + (2, rows // 2) + total.shape[dim + 1 :])
        index = later.astype(jnp.int32)
        received = exchange(pick(halves, 1 - index, dim).astype(BF16), "dp", bit)
        total = pick(halves, index, dim) + received.astype(F32)
        steps.append((bit, later))
    total = total.astype(BF16)
    for bit, later in reversed(steps):
        total = in_order(total, exchange(total, "dp", bit), later, dim, jnp.concatenate)
    return total.astype(F32)


def rope_tables():
    quarter = HEAD // 4
    frequency = 10000.0 ** (-jnp.arange(quarter, dtype=F32) / quarter)
    patches = jnp.arange(P_SIZE, dtype=jnp.int32)
    row_angle = (patches // GRID).astype(F32)[None, :] * frequency[:, None]
    col_angle = (patches % GRID).astype(F32)[None, :] * frequency[:, None]
    return (jnp.cos(row_angle), jnp.sin(row_angle), jnp.cos(col_angle), jnp.sin(col_angle))


def rotate(tensor, rotary_tables, direction):
    cos_row, sin_row, cos_col, sin_col = rotary_tables
    part_a, part_b, part_c, part_d = jnp.split(tensor, 4, axis=-2)
    return jnp.concatenate(
        [
            part_a * cos_row - direction * part_b * sin_row,
            part_b * cos_row + direction * part_a * sin_row,
            part_c * cos_col - direction * part_d * sin_col,
            part_d * cos_col + direction * part_c * sin_col,
        ],
        axis=-2,
    )


def inverse_rms(rows, dim):
    return lax.rsqrt(jnp.mean(rows * rows, axis=dim, keepdims=True) + EPSILON)


def einsum(spec, *operands):
    return jnp.einsum(spec, *operands, preferred_element_type=F32)


def local(
    latents,
    condition,
    cotangent,
    noise_bins,
    image_counts,
    ada_weight,
    ada_bias,
    qkv_weight,
    norm_gains,
    proj_weight,
    gate_up_weight,
    down_weight,
):
    slots = latents.shape[0]
    devices = lax.axis_size("dp")
    device = lax.axis_index("dp")
    part = lax.axis_index("mp")
    width = latents.shape[2]
    rows_in = latents.transpose(0, 2, 1)
    cot_in = cotangent.transpose(0, 2, 1)
    tables = rope_tables()
    gains = norm_gains.astype(F32)

    own_count = image_counts[0]
    last_slots = (own_count - IMG_DEV + jnp.arange(IMG_DEV)) % slots
    rows_came = shifted(jnp.take(rows_in, last_slots, axis=0).astype(BF16), "dp", 1)
    cot_came = shifted(jnp.take(cot_in, last_slots, axis=0).astype(BF16), "dp", 1)

    facts = jnp.zeros((1, width), F32)
    facts = facts.at[0, :slots].set(noise_bins.astype(F32)).at[0, slots].set(own_count.astype(F32))
    message = jnp.concatenate([jax.nn.silu(condition), facts]).astype(BF16)[None]
    message = gather_small(message, "dp", 0)
    facts = message[:, slots, : slots + 1].astype(jnp.int32)
    silu_all = gather_small(message[:, :slots], "mp", 2).reshape(devices * slots, -1)
    bins, counts = facts[:, :slots].reshape(-1), facts[:, slots]

    slot_ids = jnp.arange(devices * slots)
    live = (slot_ids % slots < counts[slot_ids // slots]).astype(F32)
    onehot = (bins[:, None] == jnp.arange(NBINS)[None, :]).astype(F32)
    histogram = jnp.sum(onehot * live[:, None], axis=0)
    bin_load = jnp.sum(onehot * histogram[None, :], axis=1)
    scaling = live * (IMG_DEV * devices) / (NBINS * (bin_load + 1.0 - live))

    ids = jnp.arange(devices)
    excess = jnp.cumsum(counts) - IMG_DEV * (ids + 1)
    came = jnp.concatenate([jnp.zeros((1,), excess.dtype), excess[:-1]])
    before = jnp.concatenate([jnp.zeros((1,), counts.dtype), counts[:-1]])
    places = jnp.arange(IMG_DEV)[None, :]
    from_before = places >= IMG_DEV - came[:, None]
    share_ids = jnp.where(
        from_before,
        (ids[:, None] - 1) * slots + (before[:, None] - IMG_DEV + places) % slots,
        ids[:, None] * slots + places,
    ).reshape(-1)
    silu_share = jnp.take(silu_all, share_ids, axis=0)
    silu_own = lax.dynamic_slice_in_dim(silu_share, device * IMG_DEV, IMG_DEV, 0)
    scale_share = jnp.take(scaling, share_ids)
    scale_own = lax.dynamic_slice_in_dim(scale_share, device * IMG_DEV, IMG_DEV, 0)
    came_here = pick(came, device, 0)
    mask = pick(from_before, device, 0)[:, None, None]

    modulation = einsum("bd,dkf->kbf", silu_own, ada_weight) + ada_bias.astype(F32)[:, None, :]
    everywhere = jnp.stack([modulation[0], modulation[1], modulation[3], modulation[4]])
    everywhere = gather_small(everywhere, "mp", 2)[..., None]
    shift_one_all, scale_one_all, shift_two_all, scale_two_all = everywhere
    modulation = modulation[..., None]
    shift_one, scale_one, gate_one, shift_two, scale_two, gate_two = modulation

    rows = jnp.where(mask, rows_came.astype(F32), rows_in[:IMG_DEV])
    rows_full = spread(jnp.where(mask, rows_came, rows_in[:IMG_DEV].astype(BF16))).astype(F32)
    inverse_one = inverse_rms(rows_full, 1)
    normed_full = rows_full * inverse_one
    attn_full = (normed_full * (1.0 + scale_one_all) + shift_one_all).astype(BF16)
    projected = einsum("dkf,bdp->bkfp", qkv_weight, attn_full)
    projected = projected.reshape(IMG_DEV, 3, -1, HEAD, P_SIZE)
    inverse_heads = inverse_rms(projected[:, :2], 3)
    hats = projected[:, :2] * inverse_heads
    gain_column = gains[None, :, None, :, None]
    rotated = rotate(hats * gain_column, tables, 1.0).astype(BF16)
    queries, keys = rotated[:, 0], rotated[:, 1]
    values = projected[:, 2].astype(BF16)
    scores = einsum("bheq,bhep->bhqp", keys, queries) * HEAD ** (-0.5)
    highest = jnp.max(scores, axis=2, keepdims=True)
    lse = highest + jnp.log(jnp.sum(jnp.exp(scores - highest), axis=2, keepdims=True))
    probability = jnp.exp(scores - lse)
    attention = probability.astype(BF16)
    heads_out = einsum("bheq,bhqp->bhep", values, attention).astype(BF16)
    heads_out = heads_out.reshape(IMG_DEV, -1, P_SIZE)
    branch_one = reduce_parts(einsum("ed,bep->bdp", proj_weight, heads_out))
    middle = rows + gate_one * branch_one

    middle_full = spread(middle.astype(BF16)).astype(F32)
    inverse_two = inverse_rms(middle_full, 1)
    normed_two_full = middle_full * inverse_two
    mlp_full = (normed_two_full * (1.0 + scale_two_all) + shift_two_all).astype(BF16)
    gate_up = einsum("dkf,bdp->kbfp", gate_up_weight, mlp_full)
    gate_part, up_part = gate_up
    sigmoid_gate = jax.nn.sigmoid(gate_part)
    silu_gate = gate_part * sigmoid_gate
    hidden = (silu_gate * up_part).astype(BF16)
    branch_two = reduce_parts(einsum("fd,bfp->bdp", down_weight, hidden))
    result = middle + gate_two * branch_two
    result_back = shifted(result.astype(BF16), "dp", -1)

    grad_out = jnp.where(mask, cot_came.astype(F32), cot_in[:IMG_DEV]) * scale_own[:, None, None]
    grad_gate_two = jnp.sum(grad_out * branch_two, axis=2)
    grad_branch_two = spread((grad_out * gate_two).astype(BF16))
    grad_down = reduce_images(einsum("bfp,bdp->fd", hidden, grad_branch_two), 0)
    grad_hidden = einsum("fd,bdp->bfp", down_weight, grad_branch_two)
    grad_gate = grad_hidden * up_part * sigmoid_gate * (1.0 + gate_part * (1.0 - sigmoid_gate))
    grad_up = grad_hidden * silu_gate
    grad_gu_rows = jnp.stack([grad_gate, grad_up]).astype(BF16)
    grad_gate_weight = reduce_images(einsum("bdp,bfp->df", mlp_full, grad_gu_rows[0]), 0)
    grad_up_weight = reduce_images(einsum("bdp,bfp->df", mlp_full, grad_gu_rows[1]), 0)
    grad_gate_up = jnp.stack([grad_gate_weight, grad_up_weight], axis=1)
    partial = einsum("dkf,kbfp->bdp", gate_up_weight, grad_gu_rows)
    inner = jnp.sum(partial * (1.0 + scale_two_all) * normed_two_full, axis=1, keepdims=True)
    inner = sum_small(inner, "mp") / D
    grad_mlp_in = reduce_parts(partial)
    normed_two = middle * inverse_two
    grad_shift_two = jnp.sum(grad_mlp_in, axis=2)
    grad_scale_two = jnp.sum(grad_mlp_in * normed_two, axis=2)
    grad_middle = grad_out + inverse_two * (grad_mlp_in * (1.0 + scale_two) - normed_two * inner)
    grad_gate_one = jnp.sum(grad_middle * branch_one, axis=2)
    grad_branch_one = spread((grad_middle * gate_one).astype(BF16))
    grad_proj = reduce_images(einsum("bep,bdp->ed", heads_out, grad_branch_one), 0)
    grad_heads = einsum("ed,bdp->bep", proj_weight, grad_branch_one).astype(BF16)
    grad_heads = grad_heads.reshape(IMG_DEV, -1, HEAD, P_SIZE)
    grad_attention = einsum("bheq,bhep->bhqp", values, grad_heads)
    grad_values = einsum("bhqp,bhep->bheq", attention, grad_heads)
    inner = jnp.sum(probability * grad_attention, axis=2, keepdims=True)
    grad_scores = (probability * (grad_attention - inner)).astype(BF16)
    score_scale = HEAD ** (-0.5)
    grad_rotated = jnp.stack(
        [
            einsum("bhqp,bheq->bhep", grad_scores, keys),
            einsum("bhqp,bhep->bheq", grad_scores, queries),
        ],
        axis=1,
    )
    grad_scaled = rotate(grad_rotated * score_scale, tables, -1.0)
    grad_gains = jnp.sum(grad_scaled * hats, axis=(0, 2, 4))
    grad_hats = grad_scaled * gain_column
    inner = jnp.mean(grad_hats * hats, axis=3, keepdims=True)
    grad_raw = inverse_heads * (grad_hats - hats * inner)
    grad_rows = jnp.concatenate([grad_raw, grad_values[:, None]], axis=1).astype(BF16)
    grad_rows = grad_rows.reshape(IMG_DEV, 3, -1, P_SIZE)
    grad_qkv = reduce_images(einsum("bkfp,bdp->kfd", grad_rows, attn_full), 1)
    partial = einsum("dkf,bkfp->bdp", qkv_weight, grad_rows)
    inner = jnp.sum(partial * (1.0 + scale_one_all) * normed_full, axis=1, keepdims=True)
    inner = sum_small(inner, "mp") / D
    grad_attn_in = reduce_parts(partial)
    normed_one = rows * inverse_one
    grad_shift_one = jnp.sum(grad_attn_in, axis=2)
    grad_scale_one = jnp.sum(grad_attn_in * normed_one, axis=2)
    grad_latent = grad_middle + inverse_one * (
        grad_attn_in * (1.0 + scale_one) - normed_one * inner
    )
    latent_back = shifted(grad_latent.astype(BF16), "dp", -1)

    grad_mod = jnp.stack(
        [
            grad_shift_one,
            grad_scale_one,
            grad_gate_one,
            grad_shift_two,
            grad_scale_two,
            grad_gate_two,
        ]
    ).astype(BF16)
    mod_share = gather_small(grad_mod, "dp", 1)
    grad_ada = einsum("kbf,bd->kfd", mod_share, silu_share)
    grad_bias = jnp.sum(mod_share.astype(F32), axis=1)
    grad_gains_total = sum_small(sum_small(grad_gains, "mp"), "dp")

    slot = jnp.arange(slots)
    stays = slot < IMG_DEV - came_here
    live_here = slot < own_count
    away_place = jnp.clip(slot - own_count + IMG_DEV, 0, IMG_DEV - 1)
    share_place = jnp.where(
        stays, device * IMG_DEV + slot, (device + 1) * IMG_DEV + away_place
    )
    share_place = jnp.clip(share_place, 0, devices * IMG_DEV - 1)
    mod_slots = jnp.take(mod_share, share_place, axis=1) * live_here.astype(BF16)[None, :, None]
    grad_silu = sum_small(einsum("kbf,dkf->bd", mod_slots, ada_weight), "mp")
    grad_silu = lax.dynamic_slice_in_dim(grad_silu, part * width, width, 1)
    sigmoid_cond = jax.nn.sigmoid(condition)
    grad_cond = grad_silu * sigmoid_cond * (1.0 + condition * (1.0 - sigmoid_cond))

    def home(here, back):
        kept = jnp.take(here, jnp.clip(slot, 0, IMG_DEV - 1), axis=0)
        away = jnp.take(back, away_place, axis=0).astype(F32)
        chosen = jnp.where(stays[:, None, None], kept, away)
        return jnp.where(live_here[:, None, None], chosen, 0.0).transpose(0, 2, 1)

    return (
        home(result, result_back),
        home(grad_latent, latent_back),
        grad_cond,
        grad_ada.transpose(2, 0, 1),
        grad_bias,
        grad_qkv.transpose(2, 0, 1),
        grad_gains_total,
        grad_proj,
        grad_gate_up,
        grad_down,
    )


def solution(mesh):
    return jax.shard_map(
        local,
        mesh=mesh,
        in_specs=(
            P("dp", None, "mp"),
            P("dp", "mp"),
            P("dp", None, "mp"),
            P("dp"),
            P("dp"),
            P(None, None, "mp"),
            P(None, "mp"),
            P(None, None, "mp"),
            P(),
            P("mp", None),
            P(None, None, "mp"),
            P("mp", None),
        ),
        out_specs=(
            P("dp", None, "mp"),
            P("dp", None, "mp"),
            P("dp", "mp"),
            P(None, None, "mp"),
            P(None, "mp"),
            P(None, None, "mp"),
            P(),
            P("mp", None),
            P(None, None, "mp"),
            P("mp", None),
        ),
        check_vma=False,
    )
```

```python
import functools
import types

import jax
import jax.numpy as jnp
import numpy as np
from jax import lax
from jax.experimental import pallas as pl
from jax.experimental.pallas import tpu as pltpu
from jax.sharding import PartitionSpec as P

HEAD = 72
P_SIZE = 256
GRID = 16
IMG_DEV = 4
NBINS = 8

EPSILON = 1e-06
F32 = jnp.float32
BF16 = jnp.bfloat16
MIB = 1 << 20
WEIGHT = 0.1 * 1e9


def exchange(value, axis, bit):
    pairs = [(i, i ^ bit) for i in range(lax.axis_size(axis))]
    return lax.ppermute(value, axis, pairs)


def shifted(value, axis, by):
    devices = lax.axis_size(axis)
    pairs = [(i, i + by) for i in range(devices) if 0 <= i + by < devices]
    return lax.ppermute(value, axis, pairs)


def bits_of(axis):
    bits, bit = [], 1
    while bit < lax.axis_size(axis):
        bits.append(bit)
        bit *= 2
    return bits


def has_bit(axis, bit):
    return (lax.axis_index(axis) & bit) != 0


def in_order(mine, other, later, axis, join):
    return jnp.where(later, join([other, mine], axis=axis), join([mine, other], axis=axis))


def gather_small(value, axis, dim):
    for bit in bits_of(axis):
        other = exchange(value, axis, bit)
        value = in_order(value, other, has_bit(axis, bit), dim, jnp.concatenate)
    return value


def sum_small(value, axis):
    for bit in bits_of(axis):
        value = value + exchange(value, axis, bit)
    return value


def pick(value, index, dim):
    return lax.dynamic_index_in_dim(value, index, dim, keepdims=False)


def spread(piece):
    core = exchange(piece, "mp", 1)
    over = exchange(piece, "mp", 2)
    both = exchange(over, "mp", 1)
    return [piece, core, over, both]


def call(kernel, grid, scalars, ins, outs, scratch=(), vmem=48, us=3.0):
    in_specs = [
        pl.BlockSpec(block, index, pipeline_mode=pl.Buffered(1)) if whole else pl.BlockSpec(block, index)
        for _, block, index, whole in ins
    ]
    return pl.pallas_call(
        kernel,
        grid_spec=pltpu.PrefetchScalarGridSpec(
            num_scalar_prefetch=1,
            grid=grid,
            in_specs=in_specs,
            out_specs=[pl.BlockSpec(block, index) for _, _, block, index in outs],
            scratch_shapes=list(scratch),
        ),
        out_shape=[jax.ShapeDtypeStruct(shape, kind) for shape, kind, _, _ in outs],
        compiler_params=pltpu.CompilerParams(
            dimension_semantics=("arbitrary",) * len(grid), vmem_limit_bytes=vmem * MIB
        ),
        cost_estimate=pl.CostEstimate(flops=int(us * WEIGHT), bytes_accessed=1000, transcendentals=0),
    )(scalars, *(a for a, _, _, _ in ins))


def by_image(array):
    rest = array.shape[1:]
    return (array, (1,) + rest, lambda i, s: (i,) + (0,) * len(rest), False)


def entire(array):
    return (array, array.shape, lambda i, s: (0,) * array.ndim, True)


def image_out(images, rest, kind):
    return ((images,) + rest, kind, (1,) + rest, lambda i, s: (i,) + (0,) * len(rest))


def flat_out(images, rows):
    return ((rows, images * P_SIZE), BF16, (rows, P_SIZE), lambda i, s: (0, i))


def dot(a, b, over=(1, 0)):
    return lax.dot_general(a, b, (((over[0],), (over[1],)), ((), ())), preferred_element_type=F32)


def span(me, relative, width):
    return pl.ds(pl.multiple_of((me ^ relative) * width, 32), width)


def assemble(pieces, full, me):
    width = pieces[0].shape[1]
    for relative, piece in enumerate(pieces):
        full[span(me, relative, width), :] = piece[0]


def inverse_rms(rows):
    return lax.rsqrt(jnp.mean(rows * rows, axis=0, keepdims=True) + EPSILON)


def swap_quarters(v):
    rows = lax.broadcasted_iota(jnp.int32, v.shape, 0)
    quarter = HEAD // 4
    first = (rows % (2 * quarter)) < quarter
    return jnp.where(first, pltpu.roll(v, HEAD - quarter, 0), pltpu.roll(v, quarter, 0))


def head_parts(raw, gain, cos, sin):
    inverse = inverse_rms(raw)
    hat = raw * inverse
    scaled = hat * gain
    return hat, inverse, (scaled * cos + swap_quarters(scaled) * sin).astype(BF16)


def probabilities(queries, keys):
    scores = dot(keys, queries, (0, 0)) * HEAD ** (-0.5)
    weights = jnp.exp(scores - jnp.max(scores, axis=0, keepdims=True))
    return weights * (1.0 / jnp.sum(weights, axis=0, keepdims=True))


def split_out(me, weight, rows, width, near, far, keep, over, weights=None):
    inner = 0.0
    for relative, out in ((3, far), (1, near), (0, keep), (2, over)):
        product = dot(weight[span(me, relative, width), :], rows)
        out[0, :width] = product.astype(out.dtype)
        if weights is not None:
            inner += jnp.sum(product * weights(relative), axis=0, keepdims=True)
    if weights is not None:
        far[0, width:] = two_parts(jnp.broadcast_to(inner, (8, inner.shape[1])))


def two_parts(values):
    high = values.astype(BF16)
    return jnp.concatenate([high.astype(F32), values - high.astype(F32)], axis=0).astype(BF16)


def attention_kernel(
    me_ref, p0, p1, p2, p3, mods, wqkv, wproj, gains, cos_ref, sin_ref,
    near, far, keep, over, attn_out, raw_out, heads_out, inverse_out,
    full, heads,
):
    me = me_ref[0]
    width = p0.shape[1]
    assemble((p0, p1, p2, p3), full, me)
    rows = full[...].astype(F32)
    inverse = inverse_rms(rows)
    inverse_out[0] = inverse
    columns_in = mods[0].T
    attn = (rows * inverse * (1.0 + columns_in[:, 1:2]) + columns_in[:, 0:1]).astype(BF16)
    attn_out[...] = attn
    raw_out[0] = dot(wqkv[...], attn)
    cos, sin = cos_ref[...], sin_ref[...]
    for head in range(width // HEAD):
        low = head * HEAD
        _, _, queries = head_parts(raw_out[0, low : low + HEAD], gains[:, 0:1], cos, sin)
        low += width
        _, _, keys = head_parts(raw_out[0, low : low + HEAD], gains[:, 1:2], cos, sin)
        low += width
        values = raw_out[0, low : low + HEAD].astype(BF16)
        attention = probabilities(queries, keys).astype(BF16)
        heads[head * HEAD : (head + 1) * HEAD] = dot(values, attention)
    out = heads[...].astype(BF16)
    heads_out[...] = out
    split_out(me, wproj, out, width, near, far, keep, over)


def mlp_kernel(
    me_ref, p0, p1, p2, p3, g0, g1, g2, g3, mods, wup_t, wup, wdown_t, wdown,
    near_a, far_a, keep_a, over_a, near_b, far_b, keep_b, over_b, mlp_out, hidden_out, rows_out, grad_out, inverse_out,
    full, modulated,
):
    me = me_ref[0]
    width = p0.shape[1]
    units = wdown.shape[0]
    assemble((p0, p1, p2, p3), full, me)
    rows = full[...].astype(F32)
    inverse = inverse_rms(rows)
    inverse_out[0] = inverse
    columns_in = mods[0].T
    scaled = rows * inverse * (1.0 + columns_in[:, 3:4])
    modulated[...] = scaled
    mlp = (scaled + columns_in[:, 2:3]).astype(BF16)
    mlp_out[...] = mlp
    gate = dot(wup_t[:units], mlp)
    up = dot(wup_t[units:], mlp)
    sigmoid = jax.nn.sigmoid(gate)
    silu = gate * sigmoid
    hidden = (silu * up).astype(BF16)
    hidden_out[...] = hidden
    assemble((g0, g1, g2, g3), full, me)
    grad_out[...] = full[...]
    grad_hidden = dot(wdown[...], full[...])
    rows_out[:units] = (grad_hidden * up * sigmoid * (1.0 + gate * (1.0 - sigmoid))).astype(BF16)
    rows_out[units:] = (grad_hidden * silu).astype(BF16)
    split_out(
        me, wup, rows_out[...], width, near_b, far_b, keep_b, over_b, lambda r: modulated[span(me, r, width), :]
    )
    split_out(me, wdown_t, hidden, width, near_a, far_a, keep_a, over_a)


def attention_back_kernel(
    me_ref, p0, p1, p2, p3, r0, r1, r2, r3, inverse_ref, mods, raw, wproj, wqkv_t, gains, cos_ref, sin_ref,
    near, far, keep, over, rows_out, grad_out, gains_out,
    full, heads, rows, scales, gains_sum,
):
    me = me_ref[0]
    width = p0.shape[1]
    assemble((p0, p1, p2, p3), full, me)
    grad_out[...] = full[...]
    heads[...] = dot(wproj[...], full[...])
    cos, sin = cos_ref[...], sin_ref[...]
    scale = HEAD ** (-0.5)

    @pl.when(pl.program_id(0) == 0)
    def _():
        gains_sum[...] = jnp.zeros_like(gains_sum)

    for head in range(width // HEAD):
        low = head * HEAD
        gain_q, gain_k = gains[:, 0:1], gains[:, 1:2]
        hat_q, inverse_q, queries = head_parts(raw[0, low : low + HEAD], gain_q, cos, sin)
        hat_k, inverse_k, keys = head_parts(raw[0, width + low : width + low + HEAD], gain_k, cos, sin)
        values = raw[0, 2 * width + low : 2 * width + low + HEAD].astype(BF16)
        grad_heads = heads[low : low + HEAD].astype(BF16)
        probability = probabilities(queries, keys)
        grad_attention = dot(values, grad_heads, (0, 0))
        rows[2 * width + low : 2 * width + low + HEAD] = dot(grad_heads, probability.astype(BF16), (1, 1))
        inner = jnp.sum(probability * grad_attention, axis=0, keepdims=True)
        grad_scores = (probability * (grad_attention - inner)).astype(BF16)
        grad_q = dot(keys, grad_scores) * scale
        grad_k = dot(queries, grad_scores, (1, 1)) * scale
        for index, grad, hat, inverse, gain in (
            (0, grad_q, hat_q, inverse_q, gain_q),
            (1, grad_k, hat_k, inverse_k, gain_k),
        ):
            grad = grad * cos - swap_quarters(grad) * sin
            product = grad * hat
            gains_sum[index] += product
            grad = grad * gain
            middle = jnp.mean(product * gain, axis=0, keepdims=True)
            start = index * width + low
            rows[start : start + HEAD] = inverse * (grad - hat * middle)
    rows_out[...] = rows[...].astype(BF16)
    inverse = inverse_ref[0]
    pieces = (r0, r1, r2, r3)
    scales[...] = mods[0].T

    def weights(relative):
        scale = 1.0 + scales[span(me, relative, width), 1:2]
        return pieces[relative][0].astype(F32) * inverse * scale

    split_out(me, wqkv_t, rows_out[...], width, near, far, keep, over, weights)

    @pl.when(pl.program_id(0) == pl.num_programs(0) - 1)
    def _():
        for index in range(2):
            gains_out[index : index + 1] = jnp.sum(gains_sum[index].T, axis=0, keepdims=True)


def columns_of(mods, width):
    return mods[0].T[:width]


def columns(values):
    lanes = lax.broadcasted_iota(jnp.int32, (values[0].shape[0], 128), 1)
    out = jnp.zeros((values[0].shape[0], 128), F32)
    for index, value in enumerate(values):
        out = jnp.where(lanes == index, value, out)
    return out


def sum_parts(values, width):
    return values[0, width : width + 1].astype(F32) + values[0, width + 8 : width + 9].astype(F32)


def total_inner(far, far_core, across, width):
    return (sum_parts(far, width) + sum_parts(far_core, width) + sum_parts(across, width)) / (4 * width)


def middle_back_kernel(
    s_ref, far, far_core, keep, core, across, cot, middle, branch, inverse_ref, mods,
    grad_out, piece_out, sums_out,
):
    width = keep.shape[1]
    modulation = columns_of(mods, width)
    inverse = inverse_ref[0]
    grad = keep[0] + core[0].astype(F32) + across[0, :width].astype(F32)
    normed = middle[0] * inverse
    inner = total_inner(far, far_core, across, width)
    grad_middle = cot[0] + inverse * (grad * (1.0 + modulation[:, 4:5]) - normed * inner)
    grad_out[0] = grad_middle
    piece_out[0] = (grad_middle * modulation[:, 2:3]).astype(BF16)
    sums_out[0] = columns(
        [
            jnp.sum(grad_middle * branch[0], axis=1, keepdims=True),
            jnp.sum(grad, axis=1, keepdims=True),
            jnp.sum(grad * normed, axis=1, keepdims=True),
        ]
    )


def last_kernel(
    s_ref, far, far_core, keep, core, across, grad_middle, latents, inverse_ref, mods,
    grad_out, back_out, sums_out,
):
    width = keep.shape[1]
    modulation = columns_of(mods, width)
    inverse = inverse_ref[0]
    grad = keep[0] + core[0].astype(F32) + across[0, :width].astype(F32)
    normed = latents[0] * inverse
    inner = total_inner(far, far_core, across, width)
    result = grad_middle[0] + inverse * (grad * (1.0 + modulation[:, 1:2]) - normed * inner)
    grad_out[0] = result
    back_out[0] = result.astype(BF16)
    sums_out[0] = columns(
        [jnp.sum(grad, axis=1, keepdims=True), jnp.sum(grad * normed, axis=1, keepdims=True)]
    )


def relay_kernel(s_ref, far, far_core, over, out):
    width = over.shape[1]
    out[0, :width] = (over[0] + far_core[0, :width].astype(F32)).astype(BF16)
    if out.shape[1] > width:
        inner = sum_parts(far, width) + sum_parts(far_core, width)
        out[0, width:] = two_parts(jnp.broadcast_to(inner, (8, inner.shape[1])))


def relay(scalars, far, far_core, over):
    images = over.shape[0]
    return call(
        relay_kernel, (images,), scalars,
        [by_image(far), by_image(far_core), by_image(over)],
        [image_out(images, far.shape[1:], BF16)],
    )[0]


def accumulate(lefts, rights, out):
    total = dot(lefts[0][...], rights[0][...], (1, 1))
    for left, right in zip(lefts[1:], rights[1:]):
        total += dot(left[...], right[...], (1, 1))
    out[...] = total.astype(out.dtype).reshape(out.shape)


def half_kernel(s_ref, *refs):
    parts = len(refs) // 2 - 1
    lefts, rights, out, kept = refs[:parts], refs[parts : 2 * parts], refs[-2], refs[-1]

    @pl.when(pl.program_id(0) == 0)
    def _():
        accumulate(lefts, rights, out)

    @pl.when(pl.program_id(0) == 1)
    def _():
        accumulate(lefts, rights, kept)


def weight_halves(index, lefts, rights, first, rows):
    half = rows // 2
    outer = rights[0].shape[0]
    place = lambda b, s: (first // half + b * s[0] + (1 - b) * (1 - s[0]), 0)
    ins = [(left, (half, left.shape[1]), place, False) for left in lefts] + [entire(right) for right in rights]
    block = (1, half, outer)
    outs = [(block, kind, block, lambda b, s: (0, 0, 0)) for kind in (BF16, F32)]
    return call(half_kernel, (2,), index, ins, outs)


def attention_weight_kernel(s_ref, *refs):
    parts = len(refs) // 4 - 1
    rows, heads, inputs, grads = (refs[i * parts : (i + 1) * parts] for i in range(4))
    out1, kept1, out2, kept2, total = refs[4 * parts :]
    group = pl.program_id(0)
    half = total.shape[0] // 2

    @pl.when(group < 3)
    def _():
        accumulate(rows, inputs, total)

    @pl.when(group == 3)
    def _():
        accumulate(heads, grads, total)

    def store(index, out, kept):
        out[0] = total[pl.ds(pl.multiple_of((1 - index) * half, 16), half)].astype(BF16)
        kept[0] = total[pl.ds(pl.multiple_of(index * half, 16), half)]

    @pl.when(group < 2)
    def _():
        store(s_ref[0], out1, kept1)

    @pl.when(group >= 2)
    def _():
        store(s_ref[1], out2, kept2)


def attention_weight_halves(indices, rows, heads, inputs, grads):
    size = heads[0].shape[0]
    outer = inputs[0].shape[0]
    ins = [(left, (size, left.shape[1]), lambda g, s: (jnp.minimum(g, 2), 0), False) for left in rows]
    ins += [entire(array) for array in heads + inputs + grads]
    shape, block = (2, size // 2, outer), (1, size // 2, outer)
    outs = []
    for place in (lambda g, s: (jnp.minimum(g, 1), 0, 0), lambda g, s: (jnp.maximum(g - 2, 0), 0, 0)):
        outs += [(shape, BF16, block, place), (shape, F32, block, place)]
    return call(attention_weight_kernel, (4,), indices, ins, outs, scratch=[pltpu.VMEM((size, outer), F32)])


def paired_kernel(s_ref, *refs):
    out = refs[-1]
    blocks = pl.num_programs(0) // 4
    units = out.shape[2]
    for index, source in enumerate(refs[:-1]):

        @pl.when(pl.program_id(0) // blocks == index)
        def _():
            values = source[0].astype(F32)
            for pair in range(out.shape[1]):
                out[:, pair, :] = values[:, pair * units : (pair + 1) * units]


def paired(indices, sources, pairs, size):
    _, half, outer = sources[0].shape
    blocks = half // size
    ins = [
        (a, (1, size, outer), lambda b, s, f=i * blocks: (0, jnp.clip(b - f, 0, blocks - 1), 0), False)
        for i, a in enumerate(sources)
    ]
    shape = (4 * half, pairs, outer // pairs)

    def place(b, s):
        chunk, within = b // (2 * blocks), b % (2 * blocks)
        own = jnp.where(chunk == 0, s[0], s[1])
        return (chunk * 2 * blocks + ((within // blocks) ^ own) * blocks + within % blocks, 0, 0)

    return call(paired_kernel, (4 * blocks,), indices, ins, [(shape, F32, (size,) + shape[1:], place)])[0]


def add_split_kernel(s_ref, own_a, got_a, own_b, got_b, out, kept):
    out[...] = (own_a[...] + got_a[...].astype(F32)).astype(BF16)
    kept[...] = own_b[...] + got_b[...].astype(F32)


def add_split(index, own, received, axis):
    groups, rows, outer = own.shape
    cut = 3 if outer % 384 == 0 else 1
    size = outer // cut
    if axis == 1:
        shape = (groups, rows // 2, outer)
        block = (1, rows // 2, size)
        here = lambda g, c, s: (g, s[0], c)
        there = lambda g, c, s: (g, 1 - s[0], c)
    else:
        half = groups // 2
        shape = (half, rows, outer)
        block = (1, rows, size)
        here = lambda g, c, s: (s[0] * half + g, 0, c)
        there = lambda g, c, s: ((1 - s[0]) * half + g, 0, c)
    plain = lambda g, c, s: (g, 0, c)
    ins = [
        (own, block, there, False),
        (received, block, there, False),
        (own, block, here, False),
        (received, block, here, False),
    ]
    outs = [(shape, BF16, block, plain), (shape, F32, block, plain)]
    return call(add_split_kernel, (shape[0], cut), index, ins, outs)


def unfold_kernel(s_ref, *refs):
    out = refs[-1]
    blocks = pl.num_programs(0) // (len(refs) - 1)
    for index, source in enumerate(refs[:-1]):

        @pl.when(pl.program_id(0) // blocks == index)
        def _():
            out[0] = source[0].astype(F32)


def unfold(index, segments):
    rows, outer = segments[0][0].shape[1:]
    ins = []
    for mine, other, group in segments:
        for half in (mine, other):
            ins.append((half, (1, rows, outer), lambda b, s, g=group: (g, 0, 0), False))
    place = lambda b, s: (b // 2, (b % 2) ^ s[0], 0)
    outs = [((len(segments), 2 * rows, outer), F32, (1, rows, outer), place)]
    return call(unfold_kernel, (len(ins),), index, ins, outs)[0]


def unfold_pair_kernel(s_ref, mine1, other1, mine2, other2, qkv, proj):
    step = pl.program_id(0)
    for index, source in enumerate((mine1, other1, mine2, other2)):

        @pl.when((step // 4) * 2 + step % 2 == index)
        def _():
            values = source[0].astype(F32)

            @pl.when(step < 6)
            def _():
                qkv[0] = values

            @pl.when(step >= 6)
            def _():
                proj[...] = values


def unfold_pair(indices, sources):
    _, half, outer = sources[0].shape
    block = (1, half, outer)
    first = lambda b, s: (jnp.minimum(b // 2, 1), 0, 0)
    second = lambda b, s: (jnp.maximum(b // 2 - 2, 0), 0, 0)
    ins = [(a, block, first if i < 2 else second, False) for i, a in enumerate(sources)]

    def row(b, s):
        return (b % 2) ^ jnp.where(b < 4, s[0], s[1])

    outs = [
        (
            (3, 2 * half, outer), F32, block,
            lambda b, s: (jnp.minimum(b // 2, 2), row(jnp.minimum(b, 5), s), 0),
        ),
        ((2 * half, outer), F32, block[1:], lambda b, s: (row(jnp.maximum(b, 6), s), 0)),
    ]
    return call(unfold_pair_kernel, (8,), indices, ins, outs)


class Order:
    def __init__(self):
        self.last = None

    def __call__(self, step, *args):
        if self.last is not None:
            args = lax.optimization_barrier((self.last, *args))[1:]
        result = step(*args)
        self.last = jax.tree.leaves(result)
        return result


class Reduction:
    def __init__(self, order, second_first=False):
        self.order = order
        self.bits = bits_of("dp")
        if second_first and len(self.bits) > 1:
            self.bits[:2] = self.bits[1::-1]
        self.levels = []

    def index(self, bit):
        return has_bit("dp", bit).astype(jnp.int32)[None]

    def first(self):
        return self.index(self.bits[0])

    def begin(self, out, own):
        self.own = own
        self.received = exchange(out, "dp", self.bits[0])

    def halve(self, level):
        if level >= len(self.bits):
            return
        bit = self.bits[level]
        groups, rows, _ = self.own.shape
        if rows % 16 == 0:
            axis = 1
        elif groups % 2 == 0:
            axis = 0
        else:
            axis = None
        if axis is None:
            self.own = self.order(lambda a, b: a + b.astype(F32), self.own, self.received)
            self.received = exchange(self.own.astype(BF16), "dp", bit)
            return
        index = self.index(bit)
        out, self.own = self.order(lambda a, b: add_split(index, a, b, axis), self.own, self.received)
        self.received = exchange(out, "dp", bit)
        self.levels.append((bit, axis))

    def join(self):
        self.own = self.order(lambda a, b: (a + b.astype(F32)).astype(BF16), self.own, self.received)
        bit = self.levels[-1][0] if self.levels else self.bits[0]
        self.received = exchange(self.own, "dp", bit)

    def double(self, level):
        if level >= len(self.levels):
            return
        bit, axis = self.levels[-1 - level]
        later = has_bit("dp", bit)
        self.own = self.order(lambda a, b: in_order(a, b, later, axis, jnp.concatenate), self.own, self.received)
        outer = self.levels[-2 - level][0] if level + 1 < len(self.levels) else self.bits[0]
        self.received = exchange(self.own, "dp", outer)


def rope_tables():
    quarter = HEAD // 4
    frequency = 10000.0 ** (-np.arange(quarter, dtype=np.float32) / quarter)
    patches = np.arange(P_SIZE)
    row = (patches // GRID).astype(np.float32)[None, :] * frequency[:, None]
    col = (patches % GRID).astype(np.float32)[None, :] * frequency[:, None]
    cos = np.concatenate([np.cos(row), np.cos(row), np.cos(col), np.cos(col)])
    sin = np.concatenate([-np.sin(row), np.sin(row), -np.sin(col), np.sin(col)])
    return jnp.asarray(cos, F32), jnp.asarray(sin, F32)


def einsum(spec, *operands):
    return jnp.einsum(spec, *operands, preferred_element_type=F32)


PARTS = ((0, 4),)


def pack_kernel(s_ref, rows, out):
    out[...] = rows[...].astype(BF16)


def last_slots(count, rows):
    slots = rows.shape[0]
    place = lambda i, s: (lax.rem(s[0] - IMG_DEV + i + slots, slots), 0, 0)
    ins = [(rows, (1,) + rows.shape[1:], place, False)]
    return call(pack_kernel, (IMG_DEV,), count, ins, [image_out(IMG_DEV, rows.shape[1:], BF16)])[0]


def transpose_kernel(s_ref, values, out):
    out[...] = values[...].T


def transposed(scalars, array):
    rows, outer = array.shape
    ins = [(array, (rows, 128), lambda i, s: (0, i), False)]
    return call(transpose_kernel, (outer // 128,), scalars, ins, [((outer, rows), array.dtype, (128, rows), lambda i, s: (i, 0))])[0]


def share_kernel(device_ref, facts, ids_out, own_out, load_out, histogram):
    devices, slots = facts.shape[0], facts.shape[1] - 1
    for b in range(NBINS):
        histogram[b] = 0

    def count(i, carry):
        for j in range(slots):
            b = facts[i, j]
            histogram[b] = histogram[b] + jnp.where(j < facts[i, slots], 1, 0)
        return carry

    lax.fori_loop(0, devices, count, 0)

    def place(i, carry):
        came, before = carry
        for k in range(IMG_DEV):
            moved = (i - 1) * slots + lax.rem(before - IMG_DEV + k + slots, slots)
            ids_out[i * IMG_DEV + k] = jnp.where(k >= IMG_DEV - came, moved, i * slots + k)

        @pl.when(i == device_ref[0])
        def _():
            own_out[0] = came

        return came + facts[i, slots] - IMG_DEV, facts[i, slots]

    lax.fori_loop(0, devices, place, (0, 0))
    for k in range(IMG_DEV):
        slot = ids_out[device_ref[0] * IMG_DEV + k]
        owner, j = lax.div(slot, slots), lax.rem(slot, slots)
        load_out[k] = histogram[facts[owner, j]]
        load_out[IMG_DEV + k] = jnp.where(j < facts[owner, slots], 1, 0)


def share(device, facts):
    smem = pl.BlockSpec(memory_space=pltpu.SMEM)
    return pl.pallas_call(
        share_kernel,
        grid_spec=pltpu.PrefetchScalarGridSpec(
            num_scalar_prefetch=1, grid=(), in_specs=[smem], out_specs=[smem] * 3,
            scratch_shapes=[pltpu.SMEM((NBINS,), jnp.int32)],
        ),
        out_shape=[jax.ShapeDtypeStruct((n,), jnp.int32) for n in (facts.shape[0] * IMG_DEV, 8, 2 * IMG_DEV)],
        cost_estimate=pl.CostEstimate(flops=1000, bytes_accessed=1000, transcendentals=0),
    )(device, facts)


def choose(s_ref, start, own, came):
    moved = pl.program_id(0) + start >= IMG_DEV - s_ref[0]
    return jnp.where(moved, came[0].astype(F32), own[0])


def rows_kernel(start, s_ref, own, came, rows_out, piece_out):
    rows = choose(s_ref, start, own, came)
    rows_out[0] = rows
    piece_out[0] = rows.astype(BF16)


def cot_kernel(start, s_ref, own, came, mods, rows_out, piece_out):
    modulation = columns_of(mods, own.shape[1])
    rows = choose(s_ref, start, own, came) * modulation[:, 6:7]
    rows_out[0] = rows
    piece_out[0] = (rows * modulation[:, 5:6]).astype(BF16)


def from_image(array, start):
    rest = array.shape[1:]
    return (array, (1,) + rest, lambda i, s: (i + start,) + (0,) * len(rest), False)


def middle_kernel(s_ref, keep, core, across, rows, mods, branch_out, middle_out, piece_out):
    branch = keep[0] + core[0].astype(F32) + across[0].astype(F32)
    branch_out[0] = branch
    middle = rows[0] + columns_of(mods, rows.shape[1])[:, 2:3] * branch
    middle_out[0] = middle
    piece_out[0] = middle.astype(BF16)


def result_kernel(s_ref, keep, core, across, middle, cot, mods, result_out, back_out, sums_out):
    branch = keep[0] + core[0].astype(F32) + across[0].astype(F32)
    result = middle[0] + columns_of(mods, middle.shape[1])[:, 5:6] * branch
    result_out[0] = result
    back_out[0] = result.astype(BF16)
    sums_out[0] = columns([jnp.sum(cot[0] * branch, axis=1, keepdims=True)])


def home_kernel(starts, s_ref, *refs):
    out = refs[-1]
    parts = len(starts)
    slot = pl.program_id(0)
    came, count = s_ref[0], s_ref[1]
    kept, away = refs[0][0], refs[parts][0].astype(F32)
    for part in range(1, parts):
        kept = jnp.where(slot >= starts[part], refs[part][0], kept)
        place = slot - count + IMG_DEV
        away = jnp.where(place >= starts[part], refs[parts + part][0].astype(F32), away)
    chosen = jnp.where(slot < IMG_DEV - came, kept, away)
    out[0] = jnp.where(slot < count, chosen, 0.0)


def home(scalars, slots, here, back):
    starts, start = [], 0
    for part in here:
        starts.append(start)
        start += part.shape[0]
    block = (1,) + here[0].shape[1:]
    ins = []
    for part, first in zip(here, starts):
        end = part.shape[0] - 1
        ins.append((part, block, lambda i, s, f=first, e=end: (jnp.clip(i - f, 0, e), 0, 0), False))
    for part, first in zip(back, starts):
        end = part.shape[0] - 1
        ins.append(
            (part, block, lambda i, s, f=first, e=end: (jnp.clip(i - s[1] + IMG_DEV - f, 0, e), 0, 0), False)
        )
    outs = [image_out(slots, block[1:], F32)]
    return call(functools.partial(home_kernel, starts), (slots,), scalars, ins, outs)[0]


def local(
    latents,
    condition,
    cotangent,
    noise_bins,
    image_counts,
    ada_weight,
    ada_bias,
    qkv_weight,
    norm_gains,
    proj_weight,
    gate_up_weight,
    down_weight,
):
    slots = latents.shape[0]
    devices = lax.axis_size("dp")
    device = lax.axis_index("dp").astype(jnp.int32)
    part = lax.axis_index("mp")
    me = part.astype(jnp.int32)[None]
    width = latents.shape[2]
    features = qkv_weight.shape[0]
    units = down_weight.shape[0]
    rows_in = latents.transpose(0, 2, 1)
    cot_in = cotangent.transpose(0, 2, 1)
    cos, sin = rope_tables()
    gains = norm_gains.astype(F32).T
    order = Order()

    own_count = image_counts[0]
    silu = jax.nn.silu(condition)
    facts = jnp.concatenate([noise_bins, image_counts]).astype(F32)
    facts = jnp.pad(facts, (0, width - slots - 1))[None]
    message = jnp.concatenate([silu, facts]).astype(BF16)[None]
    latest = (own_count - IMG_DEV + jnp.arange(IMG_DEV)) % slots
    silu_came = shifted(jnp.take(silu, latest, axis=0).astype(BF16), "dp", 1)
    message = gather_small(message, "dp", 0)
    facts = message[:, slots, : slots + 1].astype(jnp.int32)
    rows_last = order(last_slots, image_counts, rows_in)
    share_ids, own_facts, loads = order(lambda f: share(device[None], f), facts)
    came_here = own_facts[:1]
    home_facts = jnp.concatenate([came_here, image_counts])
    rows_last, _ = lax.optimization_barrier((rows_last, own_facts))
    rows_came = shifted(rows_last, "dp", 1)
    came = types.SimpleNamespace()

    silu_near = jnp.concatenate([silu[:IMG_DEV].astype(BF16), silu_came])
    silu_near = gather_small(silu_near, "mp", 1)
    modulation = einsum("bd,dkf->bkf", silu_near, ada_weight) + ada_bias.astype(F32)
    spread_mods = jnp.concatenate([modulation[:, 0:2], modulation[:, 3:5]], axis=1)
    spread_mods = gather_small(spread_mods, "mp", 2)

    parts = PARTS
    count = len(parts)
    state = [types.SimpleNamespace() for _ in parts]
    wqkv = qkv_weight.transpose(1, 2, 0).reshape(3 * width, features)
    weights = types.SimpleNamespace()

    def prepare():
        up = order(lambda w: w.reshape(features, 2 * units), gate_up_weight)
        weights.up = up
        weights.proj_t, weights.qkv_t, weights.down_t = (
            order(lambda w: transposed(me, w), array) for array in (proj_weight, wqkv, down_weight)
        )
        cot_last = order(last_slots, image_counts, cot_in)
        cot_ready, _ = lax.optimization_barrier((cot_last, weights.down_t))
        came.cot = shifted(cot_ready, "dp", 1)

    def prepare_up():
        weights.up_t = order(lambda w: transposed(me, w), weights.up)

    def choose_rows(p):
        start, images = parts[p]
        st = state[p]
        rest = rows_in.shape[1:]
        st.rows, piece = order(
            lambda own, came: call(
                functools.partial(rows_kernel, start), (images,), came_here,
                [from_image(own, start), from_image(came, start)],
                [image_out(images, rest, F32), image_out(images, rest, BF16)],
            ),
            rows_in, rows_came,
        )
        st.pieces_one = spread(piece)

    moved = (jnp.arange(IMG_DEV) >= IMG_DEV - came_here[0])[:, None, None]
    spread_mods = jnp.where(moved, spread_mods[IMG_DEV:], spread_mods[:IMG_DEV])
    spread_mods = jnp.pad(spread_mods, ((0, 0), (0, 4), (0, 0)))
    modulation = jnp.where(moved, modulation[IMG_DEV:], modulation[:IMG_DEV])
    load, live = loads[:IMG_DEV].astype(F32), loads[IMG_DEV:].astype(F32)
    scaling = live * (IMG_DEV * devices) / (NBINS * (load + 1.0 - live))
    scaling = jnp.broadcast_to(scaling[:, None, None], (IMG_DEV, 2, width))
    mods_all = jnp.concatenate([modulation, scaling], axis=1)
    mods_all = jnp.pad(mods_all, ((0, 0), (0, 0), (0, -width % 128)))
    for p, (start, images) in enumerate(parts):
        state[p].mods_full = spread_mods[start : start + images]
        state[p].mods = mods_all[start : start + images]

    def attention(p):
        st = state[p]
        images = parts[p][1]
        st.near, st.far, st.keep, st.over, st.attn, st.raw, st.heads, st.inverse_one = order(
            lambda *a: call(
                attention_kernel, (images,), me,
                [by_image(x) for x in a[:5]] + [entire(x) for x in a[5:]],
                [
                    image_out(images, (width, P_SIZE), BF16),
                    image_out(images, (width, P_SIZE), BF16),
                    image_out(images, (width, P_SIZE), F32),
                    image_out(images, (width, P_SIZE), F32),
                    flat_out(images, features),
                    image_out(images, (3 * width, P_SIZE), F32),
                    flat_out(images, width),
                    image_out(images, (1, P_SIZE), F32),
                ],
                scratch=[pltpu.VMEM((features, P_SIZE), BF16), pltpu.VMEM((width, P_SIZE), F32)],
                us=4.5 * images,
                vmem=58,
            ),
            *st.pieces_one, st.mods_full, wqkv, weights.proj_t, gains, cos, sin,
        )
        st.far_core = exchange(st.far, "mp", 1)
        st.core = exchange(st.near, "mp", 1)

    def choose_cot(p):
        start, images = parts[p]
        st = state[p]
        rest = rows_in.shape[1:]
        st.cot, piece = order(
            lambda own, came, mods: call(
                functools.partial(cot_kernel, start), (images,), came_here,
                [from_image(own, start), from_image(came, start), by_image(mods)],
                [image_out(images, rest, F32), image_out(images, rest, BF16)],
            ),
            cot_in, came.cot, st.mods,
        )
        st.pieces_grad_two = spread(piece)

    def relay_one(p):
        st = state[p]
        out = order(lambda *a: relay(me, *a), st.far, st.far_core, st.over)
        st.across = exchange(out, "mp", 2)

    def middle(p):
        st = state[p]
        images = parts[p][1]
        rest = (width, P_SIZE)
        st.branch_one, st.middle, piece = order(
            lambda keep, core, *a: call(
                middle_kernel, (images,), me,
                [by_image(keep), by_image(core)] + [by_image(x) for x in a],
                [image_out(images, rest, F32), image_out(images, rest, F32), image_out(images, rest, BF16)],
            ),
            st.keep, st.core, st.across, st.rows, st.mods,
        )
        st.pieces_two = spread(piece)

    def mlp(p):
        st = state[p]
        images = parts[p][1]
        (
            st.near_a, st.far_a, st.keep_a, st.over_a,
            st.near_b, st.far_b, st.keep_b, st.over_b,
            st.mlp, st.hidden, st.grad_rows_two, st.grad_two, st.inverse_two,
        ) = order(
            lambda *a: call(
                mlp_kernel, (images,), me,
                [by_image(x) for x in a[:9]] + [entire(x) for x in a[9:]],
                [
                    image_out(images, (width, P_SIZE), BF16),
                    image_out(images, (width, P_SIZE), BF16),
                    image_out(images, (width, P_SIZE), F32),
                    image_out(images, (width, P_SIZE), F32),
                    image_out(images, (width, P_SIZE), BF16),
                    image_out(images, (width + 16, P_SIZE), BF16),
                    image_out(images, (width, P_SIZE), F32),
                    image_out(images, (width, P_SIZE), F32),
                    flat_out(images, features),
                    flat_out(images, units),
                    flat_out(images, 2 * units),
                    flat_out(images, features),
                    image_out(images, (1, P_SIZE), F32),
                ],
                scratch=[pltpu.VMEM((features, P_SIZE), BF16), pltpu.VMEM((features, P_SIZE), F32)],
                us=6.0 * images,
                vmem=58,
            ),
            *st.pieces_two, *st.pieces_grad_two, st.mods_full,
            weights.up_t, weights.up, weights.down_t, down_weight,
        )
        st.far_core_b = exchange(st.far_b, "mp", 1)
        st.core_b = exchange(st.near_b, "mp", 1)

    def relay_three(p):
        st = state[p]
        out = order(lambda *a: relay(me, *a), st.far_b, st.far_core_b, st.over_b)
        st.across_b = exchange(out, "mp", 2)

    def middle_back(p):
        st = state[p]
        images = parts[p][1]
        st.grad_middle, piece, st.sums_two = order(
            lambda *a: call(
                middle_back_kernel, (images,), me, [by_image(x) for x in a],
                [
                    image_out(images, (width, P_SIZE), F32),
                    image_out(images, (width, P_SIZE), BF16),
                    image_out(images, (width, 128), F32),
                ],
            ),
            st.far_b, st.far_core_b, st.keep_b, st.core_b, st.across_b, st.cot, st.middle,
            st.branch_one, st.inverse_two, st.mods,
        )
        st.pieces_grad_one = spread(piece)

    def result_core(p):
        st = state[p]
        far, near, _ = lax.optimization_barrier((st.far_a, st.near_a, order.last))
        st.far_core_a = exchange(far, "mp", 1)
        st.core_a = exchange(near, "mp", 1)

    def relay_two(p):
        st = state[p]
        out = order(lambda *a: relay(me, *a), st.far_a, st.far_core_a, st.over_a)
        st.across_a = exchange(out, "mp", 2)

    def result(p):
        st = state[p]
        images = parts[p][1]
        st.result, back, st.sums_three = order(
            lambda keep, core, *a: call(
                result_kernel, (images,), me,
                [by_image(keep), by_image(core)] + [by_image(x) for x in a],
                [
                    image_out(images, (width, P_SIZE), F32),
                    image_out(images, (width, P_SIZE), BF16),
                    image_out(images, (width, 128), F32),
                ],
            ),
            st.keep_a, st.core_a, st.across_a, st.middle, st.cot, st.mods,
        )
        st.result_out = back

    def attention_back(p):
        st = state[p]
        images = parts[p][1]
        st.near_c, st.far_c, st.keep_c, st.over_c, st.grad_rows_one, st.grad_one, st.gain_sums = order(
            lambda *a: call(
                attention_back_kernel, (images,), me,
                [by_image(x) for x in a[:11]] + [entire(x) for x in a[11:]],
                [
                    image_out(images, (width, P_SIZE), BF16),
                    image_out(images, (width + 16, P_SIZE), BF16),
                    image_out(images, (width, P_SIZE), F32),
                    image_out(images, (width, P_SIZE), F32),
                    flat_out(images, 3 * width),
                    flat_out(images, features),
                    ((2, HEAD), F32, (2, HEAD), lambda i, s: (0, 0)),
                ],
                scratch=[
                    pltpu.VMEM((features, P_SIZE), BF16),
                    pltpu.VMEM((width, P_SIZE), F32),
                    pltpu.VMEM((3 * width, P_SIZE), F32),
                    pltpu.VMEM((features, 8), F32),
                    pltpu.VMEM((2, HEAD, P_SIZE), F32),
                ],
                us=4.5 * images,
                vmem=58,
            ),
            *st.pieces_grad_one, *st.pieces_one, st.inverse_one, st.mods_full, st.raw,
            proj_weight, weights.qkv_t, gains, cos, sin,
        )
        st.far_core_c = exchange(st.far_c, "mp", 1)
        st.core_c = exchange(st.near_c, "mp", 1)

    def relay_four(p):
        st = state[p]
        out = order(lambda *a: relay(me, *a), st.far_c, st.far_core_c, st.over_c)
        st.across_c = exchange(out, "mp", 2)

    def last(p):
        st = state[p]
        images = parts[p][1]
        st.grad_latent, back, st.sums_one = order(
            lambda *a: call(
                last_kernel, (images,), me, [by_image(x) for x in a],
                [
                    image_out(images, (width, P_SIZE), F32),
                    image_out(images, (width, P_SIZE), BF16),
                    image_out(images, (width, 128), F32),
                ],
            ),
            st.far_c, st.far_core_c, st.keep_c, st.core_c, st.across_c, st.grad_middle, st.rows,
            st.inverse_one, st.mods,
        )
        st.latent_out = back

    def each(field):
        return [field(st) for st in state]

    attn1 = Reduction(order)
    attn2 = Reduction(order, True)
    up1 = Reduction(order)
    up2 = Reduction(order, True)
    down = Reduction(order, False)

    def attention_weights():
        indices = jnp.concatenate([attn1.first(), attn2.first()])
        out1, own1, out2, own2 = order(
            lambda *a: attention_weight_halves(indices, *(a[i * count : (i + 1) * count] for i in range(4))),
            *each(lambda s: s.grad_rows_one), *each(lambda s: s.heads),
            *each(lambda s: s.attn), *each(lambda s: s.grad_one),
        )
        attn1.begin(out1, own1)
        attn2.begin(out2, own2)

    def begin(reduction):
        if reduction is down:
            lefts, rights, first, rows = each(lambda s: s.hidden), each(lambda s: s.grad_two), 0, units
        else:
            lefts, rights, rows = each(lambda s: s.mlp), each(lambda s: s.grad_rows_two), features // 2
            first = 0 if reduction is up1 else rows
        index = reduction.first()
        reduction.begin(
            *order(lambda *a: weight_halves(index, a[:count], a[count:], first, rows), *lefts, *rights)
        )

    def halve(reduction, level):
        reduction.halve(level)

    def join(reduction):
        for level in range(3, len(reduction.bits)):
            reduction.halve(level)
        reduction.join()
        for level in range(0, len(reduction.levels) - 2):
            reduction.double(level)

    def double(reduction, step):
        reduction.double(max(0, len(reduction.levels) - 2) + step)

    def unfolded(reduction, groups):
        index = reduction.first()
        return order(lambda a, b: unfold(index, [(a, b, g) for g in groups]), reduction.own, reduction.received)

    def finish_attention():
        done.qkv = order(
            lambda *a: unfold_pair(jnp.concatenate([attn1.first(), attn2.first()]), a),
            attn1.own, attn1.received, attn2.own, attn2.received,
        )

    def finish_down():
        done.down = unfolded(down, (0,))[0]

    def finish_up():
        indices = jnp.concatenate([up1.first(), up2.first()])
        done.up = order(
            lambda *a: paired(indices, a, 2, features // 8), up1.own, up1.received, up2.own, up2.received
        )

    done = types.SimpleNamespace()

    def send_back(p):
        st = state[p]
        result_out, latent_out, _ = lax.optimization_barrier((st.result_out, st.latent_out, order.last))
        st.result_back = shifted(result_out, "dp", -1)
        st.latent_back = shifted(latent_out, "dp", -1)

    def modulation_back():
        columns_one, columns_two, columns_three = (
            jnp.concatenate(each(field))
            for field in (lambda s: s.sums_one, lambda s: s.sums_two, lambda s: s.sums_three)
        )
        grad_mod = jnp.stack(
            [
                columns_one[..., 0],
                columns_one[..., 1],
                columns_two[..., 0],
                columns_two[..., 1],
                columns_two[..., 2],
                columns_three[..., 0],
            ]
        ).astype(BF16)
        gain_sums = sum(each(lambda s: s.gain_sums)).reshape(1, -1)
        high = gain_sums.astype(BF16)
        gain_row = jnp.concatenate([high, (gain_sums - high.astype(F32)).astype(BF16)], axis=1)
        sent = jnp.concatenate([grad_mod.reshape(6 * IMG_DEV, width), gain_row])[None]
        done.message = sent
        done.bits = bits_of("dp")
        modulation_send()

    def modulation_send():
        done.other = exchange(done.message, "dp", done.bits[0])

    def modulation_step():
        later = has_bit("dp", done.bits.pop(0))
        done.message = order(lambda a, b: in_order(a, b, later, 0, jnp.concatenate), done.message, done.other)
        if done.bits:
            modulation_send()

    def ada_back():
        while done.bits:
            modulation_step()
        sent = done.message
        mod_share = sent[:, : 6 * IMG_DEV].reshape(devices, 6, IMG_DEV, width).transpose(1, 0, 2, 3)
        mod_share = mod_share.reshape(6, devices * IMG_DEV, width)
        gain_sums = jnp.sum(sent[:, 6 * IMG_DEV].astype(F32), axis=0).reshape(2, 2, HEAD)
        done.gains = sum_small(gain_sums[0] + gain_sums[1], "mp")
        silu_all = gather_small(message[:, :slots], "mp", 2).reshape(devices * slots, -1)
        silu_share = jnp.take(silu_all, share_ids, axis=0)
        done.ada = order(lambda a, b: einsum("kbf,bd->kfd", a, b), mod_share, silu_share)
        done.bias = jnp.sum(mod_share.astype(F32), axis=1)

        slot = jnp.arange(slots)
        stays = slot < IMG_DEV - came_here[0]
        away_place = jnp.clip(slot - own_count + IMG_DEV, 0, IMG_DEV - 1)
        share_place = jnp.where(stays, device * IMG_DEV + slot, (device + 1) * IMG_DEV + away_place)
        share_place = jnp.clip(share_place, 0, devices * IMG_DEV - 1)
        live_here = (slot < own_count).astype(BF16)
        mod_slots = jnp.take(mod_share, share_place, axis=1) * live_here[None, :, None]
        grad_silu = sum_small(einsum("kbf,dkf->bd", mod_slots, ada_weight), "mp")
        grad_silu = lax.dynamic_slice_in_dim(grad_silu, part * width, width, 1)
        sigmoid_cond = jax.nn.sigmoid(condition)
        done.cond = grad_silu * sigmoid_cond * (1.0 + condition * (1.0 - sigmoid_cond))

    def home_result():
        done.output = order(
            lambda *a: home(home_facts, slots, a[:count], a[count:]), *each(lambda s: s.result), *each(lambda s: s.result_back)
        )

    def home_latent():
        done.latent = order(
            lambda *a: home(home_facts, slots, a[:count], a[count:]), *each(lambda s: s.grad_latent), *each(lambda s: s.latent_back)
        )

    prepare()
    choose_rows(0)
    prepare_up()
    choose_cot(0)
    attention(0)
    relay_one(0)
    middle(0)
    mlp(0)
    begin(down)
    relay_three(0)
    begin(up2)
    begin(up1)
    middle_back(0)
    halve(down, 1)
    result_core(0)
    halve(up2, 1)
    relay_two(0)
    halve(up1, 1)
    attention_back(0)
    halve(up2, 2)
    halve(up1, 2)
    attention_weights()
    halve(down, 2)
    relay_four(0)
    result(0)
    join(up1)
    join(up2)
    halve(attn1, 1)
    halve(attn2, 1)
    last(0)
    join(down)
    modulation_back()
    halve(attn2, 2)
    double(up1, 0)
    modulation_step()
    send_back(0)
    double(up2, 0)
    halve(attn1, 2)
    double(down, 0)
    join(attn2)
    double(up1, 1)
    modulation_step()
    home_result()
    home_latent()
    join(attn1)
    double(up2, 1)
    double(down, 1)
    double(attn2, 0)
    modulation_step()
    ada_back()
    double(attn1, 0)
    finish_up()
    finish_down()
    double(attn1, 1)
    double(attn2, 1)
    finish_attention()
    return (
        done.output.transpose(0, 2, 1),
        done.latent.transpose(0, 2, 1),
        done.cond,
        done.ada.transpose(2, 0, 1),
        done.bias,
        done.qkv[0].transpose(2, 0, 1),
        done.gains,
        done.qkv[1],
        done.up,
        done.down,
    )


def solution(mesh):
    return jax.shard_map(
        local,
        mesh=mesh,
        in_specs=(
            P("dp", None, "mp"),
            P("dp", "mp"),
            P("dp", None, "mp"),
            P("dp"),
            P("dp"),
            P(None, None, "mp"),
            P(None, "mp"),
            P(None, None, "mp"),
            P(),
            P("mp", None),
            P(None, None, "mp"),
            P("mp", None),
        ),
        out_specs=(
            P("dp", None, "mp"),
            P("dp", None, "mp"),
            P("dp", "mp"),
            P(None, None, "mp"),
            P(None, "mp"),
            P(None, None, "mp"),
            P(),
            P("mp", None),
            P(None, None, "mp"),
            P("mp", None),
        ),
        check_vma=False,
    )
```

```python
import functools
import types

import jax
import jax.numpy as jnp
import numpy as np
from jax import lax
from jax.experimental import pallas as pl
from jax.experimental.pallas import tpu as pltpu
from jax.sharding import PartitionSpec as P

HEAD = 72
P_SIZE = 256
GRID = 16
IMG_DEV = 4
NBINS = 8

EPSILON = 1e-06
F32 = jnp.float32
BF16 = jnp.bfloat16
MIB = 1 << 20
WEIGHT = 0.1 * 1e9


def exchange(value, axis, bit):
    pairs = [(i, i ^ bit) for i in range(lax.axis_size(axis))]
    return lax.ppermute(value, axis, pairs)


def shifted(value, axis, by):
    devices = lax.axis_size(axis)
    pairs = [(i, i + by) for i in range(devices) if 0 <= i + by < devices]
    return lax.ppermute(value, axis, pairs)


def bits_of(axis):
    bits, bit = [], 1
    while bit < lax.axis_size(axis):
        bits.append(bit)
        bit *= 2
    return bits


def has_bit(axis, bit):
    return (lax.axis_index(axis) & bit) != 0


def in_order(mine, other, later, axis, join):
    return jnp.where(later, join([other, mine], axis=axis), join([mine, other], axis=axis))


def gather_small(value, axis, dim):
    for bit in bits_of(axis):
        other = exchange(value, axis, bit)
        value = in_order(value, other, has_bit(axis, bit), dim, jnp.concatenate)
    return value


def sum_small(value, axis):
    for bit in bits_of(axis):
        value = value + exchange(value, axis, bit)
    return value


def pick(value, index, dim):
    return lax.dynamic_index_in_dim(value, index, dim, keepdims=False)


def spread(piece):
    core = exchange(piece, "mp", 1)
    over = exchange(piece, "mp", 2)
    both = exchange(over, "mp", 1)
    return [piece, core, over, both]


def call(kernel, grid, scalars, ins, outs, scratch=(), vmem=24, us=3.0):
    in_specs = [
        pl.BlockSpec(block, index, pipeline_mode=pl.Buffered(1)) if whole else pl.BlockSpec(block, index)
        for _, block, index, whole in ins
    ]
    return pl.pallas_call(
        kernel,
        grid_spec=pltpu.PrefetchScalarGridSpec(
            num_scalar_prefetch=1,
            grid=grid,
            in_specs=in_specs,
            out_specs=[pl.BlockSpec(block, index) for _, _, block, index in outs],
            scratch_shapes=list(scratch),
        ),
        out_shape=[jax.ShapeDtypeStruct(shape, kind) for shape, kind, _, _ in outs],
        compiler_params=pltpu.CompilerParams(
            dimension_semantics=("arbitrary",) * len(grid), vmem_limit_bytes=vmem * MIB
        ),
        cost_estimate=pl.CostEstimate(flops=int(us * WEIGHT), bytes_accessed=1000, transcendentals=0),
    )(scalars, *(a for a, _, _, _ in ins))


def by_image(array):
    rest = array.shape[1:]
    return (array, (1,) + rest, lambda i, s: (i,) + (0,) * len(rest), False)


def entire(array):
    return (array, array.shape, lambda i, s: (0,) * array.ndim, True)


def image_out(images, rest, kind):
    return ((images,) + rest, kind, (1,) + rest, lambda i, s: (i,) + (0,) * len(rest))


def flat_out(images, rows):
    return ((rows, images * P_SIZE), BF16, (rows, P_SIZE), lambda i, s: (0, i))


def dot(a, b, over=(1, 0)):
    return lax.dot_general(a, b, (((over[0],), (over[1],)), ((), ())), preferred_element_type=F32)


def span(me, relative, width):
    return pl.ds(pl.multiple_of((me ^ relative) * width, 32), width)


def assemble(pieces, full, me):
    width = pieces[0].shape[1]
    for relative, piece in enumerate(pieces):
        full[span(me, relative, width), :] = piece[0]


def inverse_rms(rows):
    return lax.rsqrt(jnp.mean(rows * rows, axis=0, keepdims=True) + EPSILON)


def swap_quarters(v):
    rows = lax.broadcasted_iota(jnp.int32, v.shape, 0)
    quarter = HEAD // 4
    first = (rows % (2 * quarter)) < quarter
    return jnp.where(first, pltpu.roll(v, HEAD - quarter, 0), pltpu.roll(v, quarter, 0))


def head_parts(raw, gain, cos, sin):
    inverse = inverse_rms(raw)
    hat = raw * inverse
    scaled = hat * gain
    return hat, inverse, (scaled * cos + swap_quarters(scaled) * sin).astype(BF16)


def probabilities(queries, keys):
    scores = dot(keys, queries, (0, 0)) * HEAD ** (-0.5)
    weights = jnp.exp(scores - jnp.max(scores, axis=0, keepdims=True))
    return weights * (1.0 / jnp.sum(weights, axis=0, keepdims=True))


def split_out(me, weight, rows, width, near, far, keep, over, weights=None):
    inner = 0.0
    for relative, out in ((3, far), (1, near), (0, keep), (2, over)):
        product = dot(weight[span(me, relative, width), :], rows)
        out[0, :width] = product.astype(out.dtype)
        if weights is not None:
            inner += jnp.sum(product * weights(relative), axis=0, keepdims=True)
    if weights is not None:
        far[0, width:] = two_parts(jnp.broadcast_to(inner, (8, inner.shape[1])))


def two_parts(values):
    high = values.astype(BF16)
    return jnp.concatenate([high.astype(F32), values - high.astype(F32)], axis=0).astype(BF16)


def attention_kernel(
    me_ref, p0, p1, p2, p3, mods, wqkv, wproj, gains, cos_ref, sin_ref,
    near, far, keep, over, attn_out, raw_out, heads_out, inverse_out,
    full, heads,
):
    me = me_ref[0]
    width = p0.shape[1]
    assemble((p0, p1, p2, p3), full, me)
    rows = full[...].astype(F32)
    inverse = inverse_rms(rows)
    inverse_out[0] = inverse
    columns_in = mods[0].T
    attn = (rows * inverse * (1.0 + columns_in[:, 1:2]) + columns_in[:, 0:1]).astype(BF16)
    attn_out[...] = attn
    raw_out[0] = dot(wqkv[...], attn)
    cos, sin = cos_ref[...], sin_ref[...]
    for head in range(width // HEAD):
        low = head * HEAD
        _, _, queries = head_parts(raw_out[0, low : low + HEAD], gains[:, 0:1], cos, sin)
        low += width
        _, _, keys = head_parts(raw_out[0, low : low + HEAD], gains[:, 1:2], cos, sin)
        low += width
        values = raw_out[0, low : low + HEAD].astype(BF16)
        attention = probabilities(queries, keys).astype(BF16)
        heads[head * HEAD : (head + 1) * HEAD] = dot(values, attention)
    out = heads[...].astype(BF16)
    heads_out[...] = out
    split_out(me, wproj, out, width, near, far, keep, over)


def mlp_kernel(
    me_ref, p0, p1, p2, p3, g0, g1, g2, g3, mods, wup_t, wup, wdown_t, wdown,
    near_a, far_a, keep_a, over_a, near_b, far_b, keep_b, over_b, mlp_out, hidden_out, rows_out, grad_out, inverse_out,
    full, modulated,
):
    me = me_ref[0]
    width = p0.shape[1]
    units = wdown.shape[0]
    assemble((p0, p1, p2, p3), full, me)
    rows = full[...].astype(F32)
    inverse = inverse_rms(rows)
    inverse_out[0] = inverse
    columns_in = mods[0].T
    scaled = rows * inverse * (1.0 + columns_in[:, 3:4])
    modulated[...] = scaled
    mlp = (scaled + columns_in[:, 2:3]).astype(BF16)
    mlp_out[...] = mlp
    gate = dot(wup_t[:units], mlp)
    up = dot(wup_t[units:], mlp)
    sigmoid = jax.nn.sigmoid(gate)
    silu = gate * sigmoid
    hidden = (silu * up).astype(BF16)
    hidden_out[...] = hidden
    assemble((g0, g1, g2, g3), full, me)
    grad_out[...] = full[...]
    grad_hidden = dot(wdown[...], full[...])
    rows_out[:units] = (grad_hidden * up * sigmoid * (1.0 + gate * (1.0 - sigmoid))).astype(BF16)
    rows_out[units:] = (grad_hidden * silu).astype(BF16)
    split_out(
        me, wup, rows_out[...], width, near_b, far_b, keep_b, over_b, lambda r: modulated[span(me, r, width), :]
    )
    split_out(me, wdown_t, hidden, width, near_a, far_a, keep_a, over_a)


def attention_back_kernel(
    me_ref, p0, p1, p2, p3, r0, r1, r2, r3, inverse_ref, mods, raw, wproj, wqkv_t, gains, cos_ref, sin_ref,
    near, far, keep, over, rows_out, grad_out, gains_out,
    full, heads, rows, scales, gains_sum,
):
    me = me_ref[0]
    width = p0.shape[1]
    assemble((p0, p1, p2, p3), full, me)
    grad_out[...] = full[...]
    heads[...] = dot(wproj[...], full[...])
    cos, sin = cos_ref[...], sin_ref[...]
    scale = HEAD ** (-0.5)

    @pl.when(pl.program_id(0) == 0)
    def _():
        gains_sum[...] = jnp.zeros_like(gains_sum)

    for head in range(width // HEAD):
        low = head * HEAD
        gain_q, gain_k = gains[:, 0:1], gains[:, 1:2]
        hat_q, inverse_q, queries = head_parts(raw[0, low : low + HEAD], gain_q, cos, sin)
        hat_k, inverse_k, keys = head_parts(raw[0, width + low : width + low + HEAD], gain_k, cos, sin)
        values = raw[0, 2 * width + low : 2 * width + low + HEAD].astype(BF16)
        grad_heads = heads[low : low + HEAD].astype(BF16)
        probability = probabilities(queries, keys)
        grad_attention = dot(values, grad_heads, (0, 0))
        rows[2 * width + low : 2 * width + low + HEAD] = dot(grad_heads, probability.astype(BF16), (1, 1))
        inner = jnp.sum(probability * grad_attention, axis=0, keepdims=True)
        grad_scores = (probability * (grad_attention - inner)).astype(BF16)
        grad_q = dot(keys, grad_scores) * scale
        grad_k = dot(queries, grad_scores, (1, 1)) * scale
        for index, grad, hat, inverse, gain in (
            (0, grad_q, hat_q, inverse_q, gain_q),
            (1, grad_k, hat_k, inverse_k, gain_k),
        ):
            grad = grad * cos - swap_quarters(grad) * sin
            product = grad * hat
            gains_sum[index] += product
            grad = grad * gain
            middle = jnp.mean(product * gain, axis=0, keepdims=True)
            start = index * width + low
            rows[start : start + HEAD] = inverse * (grad - hat * middle)
    rows_out[...] = rows[...].astype(BF16)
    inverse = inverse_ref[0]
    pieces = (r0, r1, r2, r3)
    scales[...] = mods[0].T

    def weights(relative):
        scale = 1.0 + scales[span(me, relative, width), 1:2]
        return pieces[relative][0].astype(F32) * inverse * scale

    split_out(me, wqkv_t, rows_out[...], width, near, far, keep, over, weights)

    @pl.when(pl.program_id(0) == pl.num_programs(0) - 1)
    def _():
        for index in range(2):
            gains_out[index : index + 1] = jnp.sum(gains_sum[index].T, axis=0, keepdims=True)


def columns_of(mods, width):
    return mods[0].T[:width]


def columns(values):
    lanes = lax.broadcasted_iota(jnp.int32, (values[0].shape[0], 128), 1)
    out = jnp.zeros((values[0].shape[0], 128), F32)
    for index, value in enumerate(values):
        out = jnp.where(lanes == index, value, out)
    return out


def sum_parts(values, width):
    return values[0, width : width + 1].astype(F32) + values[0, width + 8 : width + 9].astype(F32)


def total_inner(far, far_core, across, width):
    return (sum_parts(far, width) + sum_parts(far_core, width) + sum_parts(across, width)) / (4 * width)


def middle_back_kernel(
    s_ref, far, far_core, keep, core, across, cot, middle, branch, inverse_ref, mods,
    grad_out, piece_out, sums_out,
):
    width = keep.shape[1]
    modulation = columns_of(mods, width)
    inverse = inverse_ref[0]
    grad = keep[0] + core[0].astype(F32) + across[0, :width].astype(F32)
    normed = middle[0] * inverse
    inner = total_inner(far, far_core, across, width)
    grad_middle = cot[0] + inverse * (grad * (1.0 + modulation[:, 4:5]) - normed * inner)
    grad_out[0] = grad_middle
    piece_out[0] = (grad_middle * modulation[:, 2:3]).astype(BF16)
    sums_out[0] = columns(
        [
            jnp.sum(grad_middle * branch[0], axis=1, keepdims=True),
            jnp.sum(grad, axis=1, keepdims=True),
            jnp.sum(grad * normed, axis=1, keepdims=True),
        ]
    )


def last_kernel(
    s_ref, far, far_core, keep, core, across, grad_middle, latents, inverse_ref, mods,
    grad_out, back_out, sums_out,
):
    width = keep.shape[1]
    modulation = columns_of(mods, width)
    inverse = inverse_ref[0]
    grad = keep[0] + core[0].astype(F32) + across[0, :width].astype(F32)
    normed = latents[0] * inverse
    inner = total_inner(far, far_core, across, width)
    result = grad_middle[0] + inverse * (grad * (1.0 + modulation[:, 1:2]) - normed * inner)
    grad_out[0] = result
    back_out[0] = result.astype(BF16)
    sums_out[0] = columns(
        [jnp.sum(grad, axis=1, keepdims=True), jnp.sum(grad * normed, axis=1, keepdims=True)]
    )


def relay_kernel(s_ref, far, far_core, over, out):
    width = over.shape[1]
    out[0, :width] = (over[0] + far_core[0, :width].astype(F32)).astype(BF16)
    if out.shape[1] > width:
        inner = sum_parts(far, width) + sum_parts(far_core, width)
        out[0, width:] = two_parts(jnp.broadcast_to(inner, (8, inner.shape[1])))


def relay(scalars, far, far_core, over):
    images = over.shape[0]
    return call(
        relay_kernel, (images,), scalars,
        [by_image(far), by_image(far_core), by_image(over)],
        [image_out(images, far.shape[1:], BF16)],
    )[0]


def accumulate(lefts, rights, out):
    total = dot(lefts[0][...], rights[0][...], (1, 1))
    for left, right in zip(lefts[1:], rights[1:]):
        total += dot(left[...], right[...], (1, 1))
    out[...] = total.astype(out.dtype).reshape(out.shape)


def half_kernel(s_ref, *refs):
    parts = len(refs) // 2 - 1
    lefts, rights, out, kept = refs[:parts], refs[parts : 2 * parts], refs[-2], refs[-1]

    @pl.when(pl.program_id(0) == 0)
    def _():
        accumulate(lefts, rights, out)

    @pl.when(pl.program_id(0) == 1)
    def _():
        accumulate(lefts, rights, kept)


def weight_halves(index, lefts, rights, first, rows):
    half = rows // 2
    outer = rights[0].shape[0]
    place = lambda b, s: (first // half + b * s[0] + (1 - b) * (1 - s[0]), 0)
    ins = [(left, (half, left.shape[1]), place, False) for left in lefts] + [entire(right) for right in rights]
    block = (1, half, outer)
    outs = [(block, kind, block, lambda b, s: (0, 0, 0)) for kind in (BF16, F32)]
    return call(half_kernel, (2,), index, ins, outs)


def attention_weight_kernel(s_ref, *refs):
    parts = len(refs) // 4 - 1
    rows, heads, inputs, grads = (refs[i * parts : (i + 1) * parts] for i in range(4))
    out1, kept1, out2, kept2, total = refs[4 * parts :]
    group = pl.program_id(0)
    half = total.shape[0] // 2

    @pl.when(group < 3)
    def _():
        accumulate(rows, inputs, total)

    @pl.when(group == 3)
    def _():
        accumulate(heads, grads, total)

    def store(index, out, kept):
        out[0] = total[pl.ds(pl.multiple_of((1 - index) * half, 16), half)].astype(BF16)
        kept[0] = total[pl.ds(pl.multiple_of(index * half, 16), half)]

    @pl.when(group < 2)
    def _():
        store(s_ref[0], out1, kept1)

    @pl.when(group >= 2)
    def _():
        store(s_ref[1], out2, kept2)


def attention_weight_halves(indices, rows, heads, inputs, grads):
    size = heads[0].shape[0]
    outer = inputs[0].shape[0]
    ins = [(left, (size, left.shape[1]), lambda g, s: (jnp.minimum(g, 2), 0), False) for left in rows]
    ins += [entire(array) for array in heads + inputs + grads]
    shape, block = (2, size // 2, outer), (1, size // 2, outer)
    outs = []
    for place in (lambda g, s: (jnp.minimum(g, 1), 0, 0), lambda g, s: (jnp.maximum(g - 2, 0), 0, 0)):
        outs += [(shape, BF16, block, place), (shape, F32, block, place)]
    return call(attention_weight_kernel, (4,), indices, ins, outs, scratch=[pltpu.VMEM((size, outer), F32)])


def paired_kernel(s_ref, *refs):
    out = refs[-1]
    blocks = pl.num_programs(0) // 4
    units = out.shape[2]
    for index, source in enumerate(refs[:-1]):

        @pl.when(pl.program_id(0) // blocks == index)
        def _():
            values = source[0].astype(F32)
            for pair in range(out.shape[1]):
                out[:, pair, :] = values[:, pair * units : (pair + 1) * units]


def paired(indices, sources, pairs, size):
    _, half, outer = sources[0].shape
    blocks = half // size
    ins = [
        (a, (1, size, outer), lambda b, s, f=i * blocks: (0, jnp.clip(b - f, 0, blocks - 1), 0), False)
        for i, a in enumerate(sources)
    ]
    shape = (4 * half, pairs, outer // pairs)

    def place(b, s):
        chunk, within = b // (2 * blocks), b % (2 * blocks)
        own = jnp.where(chunk == 0, s[0], s[1])
        return (chunk * 2 * blocks + ((within // blocks) ^ own) * blocks + within % blocks, 0, 0)

    return call(paired_kernel, (4 * blocks,), indices, ins, [(shape, F32, (size,) + shape[1:], place)])[0]


def add_split_kernel(s_ref, own_a, got_a, own_b, got_b, out, kept):
    out[...] = (own_a[...] + got_a[...].astype(F32)).astype(BF16)
    kept[...] = own_b[...] + got_b[...].astype(F32)


def add_split(index, own, received, axis):
    groups, rows, outer = own.shape
    cut = 3 if outer % 384 == 0 else 1
    size = outer // cut
    if axis == 1:
        shape = (groups, rows // 2, outer)
        block = (1, rows // 2, size)
        here = lambda g, c, s: (g, s[0], c)
        there = lambda g, c, s: (g, 1 - s[0], c)
    else:
        half = groups // 2
        shape = (half, rows, outer)
        block = (1, rows, size)
        here = lambda g, c, s: (s[0] * half + g, 0, c)
        there = lambda g, c, s: ((1 - s[0]) * half + g, 0, c)
    plain = lambda g, c, s: (g, 0, c)
    ins = [
        (own, block, there, False),
        (received, block, there, False),
        (own, block, here, False),
        (received, block, here, False),
    ]
    outs = [(shape, BF16, block, plain), (shape, F32, block, plain)]
    return call(add_split_kernel, (shape[0], cut), index, ins, outs)


def unfold_kernel(s_ref, *refs):
    out = refs[-1]
    blocks = pl.num_programs(0) // (len(refs) - 1)
    for index, source in enumerate(refs[:-1]):

        @pl.when(pl.program_id(0) // blocks == index)
        def _():
            out[0] = source[0].astype(F32)


def unfold(index, segments):
    rows, outer = segments[0][0].shape[1:]
    ins = []
    for mine, other, group in segments:
        for half in (mine, other):
            ins.append((half, (1, rows, outer), lambda b, s, g=group: (g, 0, 0), False))
    place = lambda b, s: (b // 2, (b % 2) ^ s[0], 0)
    outs = [((len(segments), 2 * rows, outer), F32, (1, rows, outer), place)]
    return call(unfold_kernel, (len(ins),), index, ins, outs)[0]


def unfold_pair_kernel(s_ref, mine1, other1, mine2, other2, qkv, proj):
    step = pl.program_id(0)
    for index, source in enumerate((mine1, other1, mine2, other2)):

        @pl.when((step // 4) * 2 + step % 2 == index)
        def _():
            values = source[0].astype(F32)

            @pl.when(step < 6)
            def _():
                qkv[0] = values

            @pl.when(step >= 6)
            def _():
                proj[...] = values


def unfold_pair(indices, sources):
    _, half, outer = sources[0].shape
    block = (1, half, outer)
    first = lambda b, s: (jnp.minimum(b // 2, 1), 0, 0)
    second = lambda b, s: (jnp.maximum(b // 2 - 2, 0), 0, 0)
    ins = [(a, block, first if i < 2 else second, False) for i, a in enumerate(sources)]

    def row(b, s):
        return (b % 2) ^ jnp.where(b < 4, s[0], s[1])

    outs = [
        (
            (3, 2 * half, outer), F32, block,
            lambda b, s: (jnp.minimum(b // 2, 2), row(jnp.minimum(b, 5), s), 0),
        ),
        ((2 * half, outer), F32, block[1:], lambda b, s: (row(jnp.maximum(b, 6), s), 0)),
    ]
    return call(unfold_pair_kernel, (8,), indices, ins, outs)


class Order:
    def __init__(self):
        self.last = None

    def __call__(self, step, *args):
        if self.last is not None:
            args = lax.optimization_barrier((self.last, *args))[1:]
        result = step(*args)
        self.last = jax.tree.leaves(result)
        return result


class Reduction:
    def __init__(self, order, second_first=False):
        self.order = order
        self.bits = bits_of("dp")
        if second_first and len(self.bits) > 1:
            self.bits[:2] = self.bits[1::-1]
        self.levels = []

    def index(self, bit):
        return has_bit("dp", bit).astype(jnp.int32)[None]

    def first(self):
        return self.index(self.bits[0])

    def begin(self, out, own):
        self.own = own
        self.received = exchange(out, "dp", self.bits[0])

    def halve(self, level):
        if level >= len(self.bits):
            return
        bit = self.bits[level]
        groups, rows, _ = self.own.shape
        if rows % 16 == 0:
            axis = 1
        elif groups % 2 == 0:
            axis = 0
        else:
            axis = None
        if axis is None:
            self.own = self.order(lambda a, b: a + b.astype(F32), self.own, self.received)
            self.received = exchange(self.own.astype(BF16), "dp", bit)
            return
        index = self.index(bit)
        out, self.own = self.order(lambda a, b: add_split(index, a, b, axis), self.own, self.received)
        self.received = exchange(out, "dp", bit)
        self.levels.append((bit, axis))

    def join(self):
        self.own = self.order(lambda a, b: (a + b.astype(F32)).astype(BF16), self.own, self.received)
        bit = self.levels[-1][0] if self.levels else self.bits[0]
        self.received = exchange(self.own, "dp", bit)

    def double(self, level):
        if level >= len(self.levels):
            return
        bit, axis = self.levels[-1 - level]
        later = has_bit("dp", bit)
        self.own = self.order(lambda a, b: in_order(a, b, later, axis, jnp.concatenate), self.own, self.received)
        outer = self.levels[-2 - level][0] if level + 1 < len(self.levels) else self.bits[0]
        self.received = exchange(self.own, "dp", outer)


def rope_tables():
    quarter = HEAD // 4
    frequency = 10000.0 ** (-np.arange(quarter, dtype=np.float32) / quarter)
    patches = np.arange(P_SIZE)
    row = (patches // GRID).astype(np.float32)[None, :] * frequency[:, None]
    col = (patches % GRID).astype(np.float32)[None, :] * frequency[:, None]
    cos = np.concatenate([np.cos(row), np.cos(row), np.cos(col), np.cos(col)])
    sin = np.concatenate([-np.sin(row), np.sin(row), -np.sin(col), np.sin(col)])
    return jnp.asarray(cos, F32), jnp.asarray(sin, F32)


def einsum(spec, *operands):
    return jnp.einsum(spec, *operands, preferred_element_type=F32)


PARTS = ((0, 4),)


def pack_kernel(s_ref, rows, out):
    out[...] = rows[...].astype(BF16)


def last_slots(count, rows):
    slots = rows.shape[0]
    place = lambda i, s: (lax.rem(s[0] - IMG_DEV + i + slots, slots), 0, 0)
    ins = [(rows, (1,) + rows.shape[1:], place, False)]
    return call(pack_kernel, (IMG_DEV,), count, ins, [image_out(IMG_DEV, rows.shape[1:], BF16)])[0]


def transpose_kernel(s_ref, values, out):
    out[...] = values[...].T


def transposed(scalars, array):
    rows, outer = array.shape
    ins = [(array, (rows, 128), lambda i, s: (0, i), False)]
    return call(transpose_kernel, (outer // 128,), scalars, ins, [((outer, rows), array.dtype, (128, rows), lambda i, s: (i, 0))])[0]


def share_kernel(device_ref, facts, ids_out, own_out, load_out, histogram):
    devices, slots = facts.shape[0], facts.shape[1] - 1
    for b in range(NBINS):
        histogram[b] = 0

    def count(i, carry):
        for j in range(slots):
            b = facts[i, j]
            histogram[b] = histogram[b] + jnp.where(j < facts[i, slots], 1, 0)
        return carry

    lax.fori_loop(0, devices, count, 0)

    def place(i, carry):
        came, before = carry
        for k in range(IMG_DEV):
            moved = (i - 1) * slots + lax.rem(before - IMG_DEV + k + slots, slots)
            ids_out[i * IMG_DEV + k] = jnp.where(k >= IMG_DEV - came, moved, i * slots + k)

        @pl.when(i == device_ref[0])
        def _():
            own_out[0] = came

        return came + facts[i, slots] - IMG_DEV, facts[i, slots]

    lax.fori_loop(0, devices, place, (0, 0))
    for k in range(IMG_DEV):
        slot = ids_out[device_ref[0] * IMG_DEV + k]
        owner, j = lax.div(slot, slots), lax.rem(slot, slots)
        load_out[k] = histogram[facts[owner, j]]
        load_out[IMG_DEV + k] = jnp.where(j < facts[owner, slots], 1, 0)


def share(device, facts):
    smem = pl.BlockSpec(memory_space=pltpu.SMEM)
    return pl.pallas_call(
        share_kernel,
        grid_spec=pltpu.PrefetchScalarGridSpec(
            num_scalar_prefetch=1, grid=(), in_specs=[smem], out_specs=[smem] * 3,
            scratch_shapes=[pltpu.SMEM((NBINS,), jnp.int32)],
        ),
        out_shape=[jax.ShapeDtypeStruct((n,), jnp.int32) for n in (facts.shape[0] * IMG_DEV, 8, 2 * IMG_DEV)],
        cost_estimate=pl.CostEstimate(flops=1000, bytes_accessed=1000, transcendentals=0),
    )(device, facts)


def choose(s_ref, start, own, came):
    moved = pl.program_id(0) + start >= IMG_DEV - s_ref[0]
    return jnp.where(moved, came[0].astype(F32), own[0])


def rows_kernel(start, s_ref, own, came, rows_out, piece_out):
    rows = choose(s_ref, start, own, came)
    rows_out[0] = rows
    piece_out[0] = rows.astype(BF16)


def cot_kernel(start, s_ref, own, came, mods, rows_out, piece_out):
    modulation = columns_of(mods, own.shape[1])
    rows = choose(s_ref, start, own, came) * modulation[:, 6:7]
    rows_out[0] = rows
    piece_out[0] = (rows * modulation[:, 5:6]).astype(BF16)


def from_image(array, start):
    rest = array.shape[1:]
    return (array, (1,) + rest, lambda i, s: (i + start,) + (0,) * len(rest), False)


def middle_kernel(s_ref, keep, core, across, rows, mods, branch_out, middle_out, piece_out):
    branch = keep[0] + core[0].astype(F32) + across[0].astype(F32)
    branch_out[0] = branch
    middle = rows[0] + columns_of(mods, rows.shape[1])[:, 2:3] * branch
    middle_out[0] = middle
    piece_out[0] = middle.astype(BF16)


def result_kernel(s_ref, keep, core, across, middle, cot, mods, result_out, back_out, sums_out):
    branch = keep[0] + core[0].astype(F32) + across[0].astype(F32)
    result = middle[0] + columns_of(mods, middle.shape[1])[:, 5:6] * branch
    result_out[0] = result
    back_out[0] = result.astype(BF16)
    sums_out[0] = columns([jnp.sum(cot[0] * branch, axis=1, keepdims=True)])


def home_kernel(starts, s_ref, *refs):
    out = refs[-1]
    parts = len(starts)
    slot = pl.program_id(0)
    came, count = s_ref[0], s_ref[1]
    kept, away = refs[0][0], refs[parts][0].astype(F32)
    for part in range(1, parts):
        kept = jnp.where(slot >= starts[part], refs[part][0], kept)
        place = slot - count + IMG_DEV
        away = jnp.where(place >= starts[part], refs[parts + part][0].astype(F32), away)
    chosen = jnp.where(slot < IMG_DEV - came, kept, away)
    out[0] = jnp.where(slot < count, chosen, 0.0)


def home(scalars, slots, here, back):
    starts, start = [], 0
    for part in here:
        starts.append(start)
        start += part.shape[0]
    block = (1,) + here[0].shape[1:]
    ins = []
    for part, first in zip(here, starts):
        end = part.shape[0] - 1
        ins.append((part, block, lambda i, s, f=first, e=end: (jnp.clip(i - f, 0, e), 0, 0), False))
    for part, first in zip(back, starts):
        end = part.shape[0] - 1
        ins.append(
            (part, block, lambda i, s, f=first, e=end: (jnp.clip(i - s[1] + IMG_DEV - f, 0, e), 0, 0), False)
        )
    outs = [image_out(slots, block[1:], F32)]
    return call(functools.partial(home_kernel, starts), (slots,), scalars, ins, outs)[0]


def local(
    latents,
    condition,
    cotangent,
    noise_bins,
    image_counts,
    ada_weight,
    ada_bias,
    qkv_weight,
    norm_gains,
    proj_weight,
    gate_up_weight,
    down_weight,
):
    slots = latents.shape[0]
    devices = lax.axis_size("dp")
    device = lax.axis_index("dp").astype(jnp.int32)
    part = lax.axis_index("mp")
    me = part.astype(jnp.int32)[None]
    width = latents.shape[2]
    features = qkv_weight.shape[0]
    units = down_weight.shape[0]
    rows_in = latents.transpose(0, 2, 1)
    cot_in = cotangent.transpose(0, 2, 1)
    cos, sin = rope_tables()
    gains = norm_gains.astype(F32).T
    order = Order()

    own_count = image_counts[0]
    silu = jax.nn.silu(condition)
    facts = jnp.concatenate([noise_bins, image_counts]).astype(F32)
    facts = jnp.pad(facts, (0, width - slots - 1))[None]
    message = jnp.concatenate([silu, facts]).astype(BF16)[None]
    latest = (own_count - IMG_DEV + jnp.arange(IMG_DEV)) % slots
    silu_came = shifted(jnp.take(silu, latest, axis=0).astype(BF16), "dp", 1)
    message = gather_small(message, "dp", 0)
    facts = message[:, slots, : slots + 1].astype(jnp.int32)
    rows_last = order(last_slots, image_counts, rows_in)
    share_ids, own_facts, loads = order(lambda f: share(device[None], f), facts)
    came_here = own_facts[:1]
    home_facts = jnp.concatenate([came_here, image_counts])
    rows_last, _ = lax.optimization_barrier((rows_last, own_facts))
    rows_came = shifted(rows_last, "dp", 1)
    came = types.SimpleNamespace()

    silu_near = jnp.concatenate([silu[:IMG_DEV].astype(BF16), silu_came])
    silu_near = gather_small(silu_near, "mp", 1)
    modulation = einsum("bd,dkf->bkf", silu_near, ada_weight) + ada_bias.astype(F32)
    spread_mods = jnp.concatenate([modulation[:, 0:2], modulation[:, 3:5]], axis=1)
    spread_mods = gather_small(spread_mods, "mp", 2)

    parts = PARTS
    count = len(parts)
    state = [types.SimpleNamespace() for _ in parts]
    wqkv = qkv_weight.transpose(1, 2, 0).reshape(3 * width, features)
    weights = types.SimpleNamespace()

    def prepare():
        up = order(lambda w: w.reshape(features, 2 * units), gate_up_weight)
        weights.up = up
        weights.proj_t, weights.qkv_t, weights.down_t = (
            order(lambda w: transposed(me, w), array) for array in (proj_weight, wqkv, down_weight)
        )
        cot_last = order(last_slots, image_counts, cot_in)
        cot_ready, _ = lax.optimization_barrier((cot_last, weights.down_t))
        came.cot = shifted(cot_ready, "dp", 1)

    def prepare_up():
        weights.up_t = order(lambda w: transposed(me, w), weights.up)

    def choose_rows(p):
        start, images = parts[p]
        st = state[p]
        rest = rows_in.shape[1:]
        st.rows, piece = order(
            lambda own, came: call(
                functools.partial(rows_kernel, start), (images,), came_here,
                [from_image(own, start), from_image(came, start)],
                [image_out(images, rest, F32), image_out(images, rest, BF16)],
            ),
            rows_in, rows_came,
        )
        st.pieces_one = spread(piece)

    moved = (jnp.arange(IMG_DEV) >= IMG_DEV - came_here[0])[:, None, None]
    spread_mods = jnp.where(moved, spread_mods[IMG_DEV:], spread_mods[:IMG_DEV])
    spread_mods = jnp.pad(spread_mods, ((0, 0), (0, 4), (0, 0)))
    modulation = jnp.where(moved, modulation[IMG_DEV:], modulation[:IMG_DEV])
    load, live = loads[:IMG_DEV].astype(F32), loads[IMG_DEV:].astype(F32)
    scaling = live * (IMG_DEV * devices) / (NBINS * (load + 1.0 - live))
    scaling = jnp.broadcast_to(scaling[:, None, None], (IMG_DEV, 2, width))
    mods_all = jnp.concatenate([modulation, scaling], axis=1)
    mods_all = jnp.pad(mods_all, ((0, 0), (0, 0), (0, -width % 128)))
    for p, (start, images) in enumerate(parts):
        state[p].mods_full = spread_mods[start : start + images]
        state[p].mods = mods_all[start : start + images]

    def attention(p):
        st = state[p]
        images = parts[p][1]
        st.near, st.far, st.keep, st.over, st.attn, st.raw, st.heads, st.inverse_one = order(
            lambda *a: call(
                attention_kernel, (images,), me,
                [by_image(x) for x in a[:5]] + [entire(x) for x in a[5:]],
                [
                    image_out(images, (width, P_SIZE), BF16),
                    image_out(images, (width, P_SIZE), BF16),
                    image_out(images, (width, P_SIZE), F32),
                    image_out(images, (width, P_SIZE), F32),
                    flat_out(images, features),
                    image_out(images, (3 * width, P_SIZE), F32),
                    flat_out(images, width),
                    image_out(images, (1, P_SIZE), F32),
                ],
                scratch=[pltpu.VMEM((features, P_SIZE), BF16), pltpu.VMEM((width, P_SIZE), F32)],
                us=4.5 * images,
                vmem=58,
            ),
            *st.pieces_one, st.mods_full, wqkv, weights.proj_t, gains, cos, sin,
        )
        far, near, _ = lax.optimization_barrier((st.far, st.near, st.pieces_grad_two[2]))
        st.far_core = exchange(far, "mp", 1)
        st.core = exchange(near, "mp", 1)

    def choose_cot(p):
        start, images = parts[p]
        st = state[p]
        rest = rows_in.shape[1:]
        st.cot, piece = order(
            lambda own, came, mods: call(
                functools.partial(cot_kernel, start), (images,), came_here,
                [from_image(own, start), from_image(came, start), by_image(mods)],
                [image_out(images, rest, F32), image_out(images, rest, BF16)],
            ),
            cot_in, came.cot, st.mods,
        )
        st.pieces_grad_two = spread(piece)

    def relay_one(p):
        st = state[p]
        out = order(lambda *a: relay(me, *a), st.far, st.far_core, st.over)
        st.across = exchange(out, "mp", 2)

    def middle(p):
        st = state[p]
        images = parts[p][1]
        rest = (width, P_SIZE)
        st.branch_one, st.middle, piece = order(
            lambda keep, core, *a: call(
                middle_kernel, (images,), me,
                [by_image(keep), by_image(core)] + [by_image(x) for x in a],
                [image_out(images, rest, F32), image_out(images, rest, F32), image_out(images, rest, BF16)],
            ),
            st.keep, st.core, st.across, st.rows, st.mods,
        )
        st.pieces_two = spread(piece)

    def mlp(p):
        st = state[p]
        images = parts[p][1]
        (
            st.near_a, st.far_a, st.keep_a, st.over_a,
            st.near_b, st.far_b, st.keep_b, st.over_b,
            st.mlp, st.hidden, st.grad_rows_two, st.grad_two, st.inverse_two,
        ) = order(
            lambda *a: call(
                mlp_kernel, (images,), me,
                [by_image(x) for x in a[:9]] + [entire(x) for x in a[9:]],
                [
                    image_out(images, (width, P_SIZE), BF16),
                    image_out(images, (width, P_SIZE), BF16),
                    image_out(images, (width, P_SIZE), F32),
                    image_out(images, (width, P_SIZE), F32),
                    image_out(images, (width, P_SIZE), BF16),
                    image_out(images, (width + 16, P_SIZE), BF16),
                    image_out(images, (width, P_SIZE), F32),
                    image_out(images, (width, P_SIZE), F32),
                    flat_out(images, features),
                    flat_out(images, units),
                    flat_out(images, 2 * units),
                    flat_out(images, features),
                    image_out(images, (1, P_SIZE), F32),
                ],
                scratch=[pltpu.VMEM((features, P_SIZE), BF16), pltpu.VMEM((features, P_SIZE), F32)],
                us=6.0 * images,
                vmem=58,
            ),
            *st.pieces_two, *st.pieces_grad_two, st.mods_full,
            weights.up_t, weights.up, weights.down_t, down_weight,
        )
        st.far_core_b = exchange(st.far_b, "mp", 1)
        st.core_b = exchange(st.near_b, "mp", 1)

    def relay_three(p):
        st = state[p]
        out = order(lambda *a: relay(me, *a), st.far_b, st.far_core_b, st.over_b)
        st.across_b = exchange(out, "mp", 2)

    def middle_back(p):
        st = state[p]
        images = parts[p][1]
        st.grad_middle, piece, st.sums_two = order(
            lambda *a: call(
                middle_back_kernel, (images,), me, [by_image(x) for x in a],
                [
                    image_out(images, (width, P_SIZE), F32),
                    image_out(images, (width, P_SIZE), BF16),
                    image_out(images, (width, 128), F32),
                ],
            ),
            st.far_b, st.far_core_b, st.keep_b, st.core_b, st.across_b, st.cot, st.middle,
            st.branch_one, st.inverse_two, st.mods,
        )
        st.pieces_grad_one = spread(piece)

    def result_core(p):
        st = state[p]
        far, near, _ = lax.optimization_barrier((st.far_a, st.near_a, order.last))
        st.far_core_a = exchange(far, "mp", 1)
        st.core_a = exchange(near, "mp", 1)

    def relay_two(p):
        st = state[p]
        out = order(lambda *a: relay(me, *a), st.far_a, st.far_core_a, st.over_a)
        st.across_a = exchange(out, "mp", 2)

    def result(p):
        st = state[p]
        images = parts[p][1]
        st.result, back, st.sums_three = order(
            lambda keep, core, *a: call(
                result_kernel, (images,), me,
                [by_image(keep), by_image(core)] + [by_image(x) for x in a],
                [
                    image_out(images, (width, P_SIZE), F32),
                    image_out(images, (width, P_SIZE), BF16),
                    image_out(images, (width, 128), F32),
                ],
            ),
            st.keep_a, st.core_a, st.across_a, st.middle, st.cot, st.mods,
        )
        st.result_out = back

    def attention_back(p):
        st = state[p]
        images = parts[p][1]
        st.near_c, st.far_c, st.keep_c, st.over_c, st.grad_rows_one, st.grad_one, st.gain_sums = order(
            lambda *a: call(
                attention_back_kernel, (images,), me,
                [by_image(x) for x in a[:11]] + [entire(x) for x in a[11:]],
                [
                    image_out(images, (width, P_SIZE), BF16),
                    image_out(images, (width + 16, P_SIZE), BF16),
                    image_out(images, (width, P_SIZE), F32),
                    image_out(images, (width, P_SIZE), F32),
                    flat_out(images, 3 * width),
                    flat_out(images, features),
                    ((2, HEAD), F32, (2, HEAD), lambda i, s: (0, 0)),
                ],
                scratch=[
                    pltpu.VMEM((features, P_SIZE), BF16),
                    pltpu.VMEM((width, P_SIZE), F32),
                    pltpu.VMEM((3 * width, P_SIZE), F32),
                    pltpu.VMEM((features, 8), F32),
                    pltpu.VMEM((2, HEAD, P_SIZE), F32),
                ],
                us=4.5 * images,
                vmem=58,
            ),
            *st.pieces_grad_one, *st.pieces_one, st.inverse_one, st.mods_full, st.raw,
            proj_weight, weights.qkv_t, gains, cos, sin,
        )
        st.far_core_c = exchange(st.far_c, "mp", 1)
        st.core_c = exchange(st.near_c, "mp", 1)

    def relay_four(p):
        st = state[p]
        out = order(lambda *a: relay(me, *a), st.far_c, st.far_core_c, st.over_c)
        st.across_c = exchange(out, "mp", 2)

    def last(p):
        st = state[p]
        images = parts[p][1]
        st.grad_latent, back, st.sums_one = order(
            lambda *a: call(
                last_kernel, (images,), me, [by_image(x) for x in a],
                [
                    image_out(images, (width, P_SIZE), F32),
                    image_out(images, (width, P_SIZE), BF16),
                    image_out(images, (width, 128), F32),
                ],
            ),
            st.far_c, st.far_core_c, st.keep_c, st.core_c, st.across_c, st.grad_middle, st.rows,
            st.inverse_one, st.mods,
        )
        st.latent_out = back

    def each(field):
        return [field(st) for st in state]

    attn1 = Reduction(order, True)
    attn2 = Reduction(order, False)
    up1 = Reduction(order, False)
    up2 = Reduction(order, False)
    down = Reduction(order, True)

    def attention_weights():
        indices = jnp.concatenate([attn1.first(), attn2.first()])
        out1, own1, out2, own2 = order(
            lambda *a: attention_weight_halves(indices, *(a[i * count : (i + 1) * count] for i in range(4))),
            *each(lambda s: s.grad_rows_one), *each(lambda s: s.heads),
            *each(lambda s: s.attn), *each(lambda s: s.grad_one),
        )
        attn1.begin(out1, own1)
        attn2.begin(out2, own2)

    def begin(reduction):
        if reduction is down:
            lefts, rights, first, rows = each(lambda s: s.hidden), each(lambda s: s.grad_two), 0, units
        else:
            lefts, rights, rows = each(lambda s: s.mlp), each(lambda s: s.grad_rows_two), features // 2
            first = 0 if reduction is up1 else rows
        index = reduction.first()
        reduction.begin(
            *order(lambda *a: weight_halves(index, a[:count], a[count:], first, rows), *lefts, *rights)
        )

    def halve(reduction, level):
        reduction.halve(level)

    def join(reduction):
        for level in range(3, len(reduction.bits)):
            reduction.halve(level)
        reduction.join()
        for level in range(0, len(reduction.levels) - 2):
            reduction.double(level)

    def double(reduction, step):
        reduction.double(max(0, len(reduction.levels) - 2) + step)

    def unfolded(reduction, groups):
        index = reduction.first()
        return order(lambda a, b: unfold(index, [(a, b, g) for g in groups]), reduction.own, reduction.received)

    def finish_attention():
        done.qkv = order(
            lambda *a: unfold_pair(jnp.concatenate([attn1.first(), attn2.first()]), a),
            attn1.own, attn1.received, attn2.own, attn2.received,
        )

    def finish_down():
        done.down = unfolded(down, (0,))[0]

    def finish_up():
        indices = jnp.concatenate([up1.first(), up2.first()])
        done.up = order(
            lambda *a: paired(indices, a, 2, features // 8), up1.own, up1.received, up2.own, up2.received
        )

    done = types.SimpleNamespace()

    def send_result(p):
        out, _ = lax.optimization_barrier((state[p].result_out, order.last))
        state[p].result_back = shifted(out, "dp", -1)

    def send_latent(p):
        out, _ = lax.optimization_barrier((state[p].latent_out, order.last))
        state[p].latent_back = shifted(out, "dp", -1)

    def modulation_back():
        columns_one, columns_two, columns_three = (
            jnp.concatenate(each(field))
            for field in (lambda s: s.sums_one, lambda s: s.sums_two, lambda s: s.sums_three)
        )
        grad_mod = jnp.stack(
            [
                columns_one[..., 0],
                columns_one[..., 1],
                columns_two[..., 0],
                columns_two[..., 1],
                columns_two[..., 2],
                columns_three[..., 0],
            ]
        ).astype(BF16)
        gain_sums = sum(each(lambda s: s.gain_sums)).reshape(1, -1)
        high = gain_sums.astype(BF16)
        gain_row = jnp.concatenate([high, (gain_sums - high.astype(F32)).astype(BF16)], axis=1)
        sent = jnp.concatenate([grad_mod.reshape(6 * IMG_DEV, width), gain_row])[None]
        done.message = sent
        done.bits = bits_of("dp")
        modulation_send()

    def modulation_send():
        done.other = exchange(done.message, "dp", done.bits[0])

    def modulation_step():
        later = has_bit("dp", done.bits.pop(0))
        done.message = order(lambda a, b: in_order(a, b, later, 0, jnp.concatenate), done.message, done.other)
        if done.bits:
            modulation_send()

    def ada_back():
        while done.bits:
            modulation_step()
        sent = done.message
        mod_share = sent[:, : 6 * IMG_DEV].reshape(devices, 6, IMG_DEV, width).transpose(1, 0, 2, 3)
        mod_share = mod_share.reshape(6, devices * IMG_DEV, width)
        gain_sums = jnp.sum(sent[:, 6 * IMG_DEV].astype(F32), axis=0).reshape(2, 2, HEAD)
        done.gains = sum_small(gain_sums[0] + gain_sums[1], "mp")
        silu_all = gather_small(message[:, :slots], "mp", 2).reshape(devices * slots, -1)
        silu_share = jnp.take(silu_all, share_ids, axis=0)
        done.ada = order(lambda a, b: einsum("kbf,bd->kfd", a, b), mod_share, silu_share)
        done.bias = jnp.sum(mod_share.astype(F32), axis=1)

        slot = jnp.arange(slots)
        stays = slot < IMG_DEV - came_here[0]
        away_place = jnp.clip(slot - own_count + IMG_DEV, 0, IMG_DEV - 1)
        share_place = jnp.where(stays, device * IMG_DEV + slot, (device + 1) * IMG_DEV + away_place)
        share_place = jnp.clip(share_place, 0, devices * IMG_DEV - 1)
        live_here = (slot < own_count).astype(BF16)
        mod_slots = jnp.take(mod_share, share_place, axis=1) * live_here[None, :, None]
        grad_silu = sum_small(einsum("kbf,dkf->bd", mod_slots, ada_weight), "mp")
        grad_silu = lax.dynamic_slice_in_dim(grad_silu, part * width, width, 1)
        sigmoid_cond = jax.nn.sigmoid(condition)
        done.cond = grad_silu * sigmoid_cond * (1.0 + condition * (1.0 - sigmoid_cond))

    def home_result():
        done.output = order(
            lambda *a: home(home_facts, slots, a[:count], a[count:]), *each(lambda s: s.result), *each(lambda s: s.result_back)
        )

    def home_latent():
        done.latent = order(
            lambda *a: home(home_facts, slots, a[:count], a[count:]), *each(lambda s: s.grad_latent), *each(lambda s: s.latent_back)
        )

    prepare()
    choose_rows(0)
    choose_cot(0)
    attention(0)
    relay_one(0)
    prepare_up()
    middle(0)
    mlp(0)
    relay_three(0)
    begin(up1)
    begin(down)
    begin(up2)
    middle_back(0)
    halve(up1, 1)
    result_core(0)
    halve(down, 1)
    relay_two(0)
    halve(up2, 1)
    halve(up1, 2)
    attention_back(0)
    join(up1)
    halve(down, 2)
    attention_weights()
    halve(up2, 2)
    relay_four(0)
    double(up1, 0)
    result(0)
    send_result(0)
    join(down)
    halve(attn1, 1)
    halve(attn2, 1)
    last(0)
    send_latent(0)
    join(up2)
    double(up1, 1)
    modulation_back()
    home_result()
    halve(attn1, 2)
    double(down, 0)
    halve(attn2, 2)
    home_latent()
    double(up2, 0)
    join(attn1)
    modulation_step()
    join(attn2)
    double(down, 1)
    double(up2, 1)
    modulation_step()
    double(attn1, 0)
    double(attn2, 0)
    finish_down()
    finish_up()
    double(attn1, 1)
    double(attn2, 1)
    modulation_step()
    ada_back()
    finish_attention()
    return (
        done.output.transpose(0, 2, 1),
        done.latent.transpose(0, 2, 1),
        done.cond,
        done.ada.transpose(2, 0, 1),
        done.bias,
        done.qkv[0].transpose(2, 0, 1),
        done.gains,
        done.qkv[1],
        done.up,
        done.down,
    )


def solution(mesh):
    return jax.shard_map(
        local,
        mesh=mesh,
        in_specs=(
            P("dp", None, "mp"),
            P("dp", "mp"),
            P("dp", None, "mp"),
            P("dp"),
            P("dp"),
            P(None, None, "mp"),
            P(None, "mp"),
            P(None, None, "mp"),
            P(),
            P("mp", None),
            P(None, None, "mp"),
            P("mp", None),
        ),
        out_specs=(
            P("dp", None, "mp"),
            P("dp", None, "mp"),
            P("dp", "mp"),
            P(None, None, "mp"),
            P(None, "mp"),
            P(None, None, "mp"),
            P(),
            P("mp", None),
            P(None, None, "mp"),
            P("mp", None),
        ),
        check_vma=False,
    )
```

```python
import functools
import types

import jax
import jax.numpy as jnp
import numpy as np
from jax import lax
from jax.experimental import pallas as pl
from jax.experimental.pallas import tpu as pltpu
from jax.sharding import PartitionSpec as P

HEAD = 72
P_SIZE = 256
GRID = 16
IMG_DEV = 4
NBINS = 8

EPSILON = 1e-06
F32 = jnp.float32
BF16 = jnp.bfloat16
MIB = 1 << 20
WEIGHT = 0.1 * 1e9


def exchange(value, axis, bit):
    pairs = [(i, i ^ bit) for i in range(lax.axis_size(axis))]
    return lax.ppermute(value, axis, pairs)


def shifted(value, axis, by):
    devices = lax.axis_size(axis)
    pairs = [(i, i + by) for i in range(devices) if 0 <= i + by < devices]
    return lax.ppermute(value, axis, pairs)


def bits_of(axis):
    bits, bit = [], 1
    while bit < lax.axis_size(axis):
        bits.append(bit)
        bit *= 2
    return bits


def has_bit(axis, bit):
    return (lax.axis_index(axis) & bit) != 0


def in_order(mine, other, later, axis, join):
    return jnp.where(later, join([other, mine], axis=axis), join([mine, other], axis=axis))


def gather_small(value, axis, dim):
    for bit in bits_of(axis):
        other = exchange(value, axis, bit)
        value = in_order(value, other, has_bit(axis, bit), dim, jnp.concatenate)
    return value


def sum_small(value, axis):
    for bit in bits_of(axis):
        value = value + exchange(value, axis, bit)
    return value


def pick(value, index, dim):
    return lax.dynamic_index_in_dim(value, index, dim, keepdims=False)


def spread(piece):
    core = exchange(piece, "mp", 1)
    over = exchange(piece, "mp", 2)
    both = exchange(over, "mp", 1)
    return [piece, core, over, both]


def call(kernel, grid, scalars, ins, outs, scratch=(), vmem=24, us=3.0):
    in_specs = [
        pl.BlockSpec(block, index, pipeline_mode=pl.Buffered(1)) if whole else pl.BlockSpec(block, index)
        for _, block, index, whole in ins
    ]
    return pl.pallas_call(
        kernel,
        grid_spec=pltpu.PrefetchScalarGridSpec(
            num_scalar_prefetch=1,
            grid=grid,
            in_specs=in_specs,
            out_specs=[pl.BlockSpec(block, index) for _, _, block, index in outs],
            scratch_shapes=list(scratch),
        ),
        out_shape=[jax.ShapeDtypeStruct(shape, kind) for shape, kind, _, _ in outs],
        compiler_params=pltpu.CompilerParams(
            dimension_semantics=("arbitrary",) * len(grid), vmem_limit_bytes=vmem * MIB
        ),
        cost_estimate=pl.CostEstimate(flops=int(us * WEIGHT), bytes_accessed=1000, transcendentals=0),
    )(scalars, *(a for a, _, _, _ in ins))


def by_image(array):
    rest = array.shape[1:]
    return (array, (1,) + rest, lambda i, s: (i,) + (0,) * len(rest), False)


def entire(array):
    return (array, array.shape, lambda i, s: (0,) * array.ndim, True)


def image_out(images, rest, kind):
    return ((images,) + rest, kind, (1,) + rest, lambda i, s: (i,) + (0,) * len(rest))


def flat_out(images, rows):
    return ((rows, images * P_SIZE), BF16, (rows, P_SIZE), lambda i, s: (0, i))


def dot(a, b, over=(1, 0)):
    return lax.dot_general(a, b, (((over[0],), (over[1],)), ((), ())), preferred_element_type=F32)


def span(me, relative, width):
    return pl.ds(pl.multiple_of((me ^ relative) * width, 32), width)


def assemble(pieces, full, me):
    width = pieces[0].shape[1]
    for relative, piece in enumerate(pieces):
        full[span(me, relative, width), :] = piece[0]


def inverse_rms(rows):
    return lax.rsqrt(jnp.mean(rows * rows, axis=0, keepdims=True) + EPSILON)


def swap_quarters(v):
    rows = lax.broadcasted_iota(jnp.int32, v.shape, 0)
    quarter = HEAD // 4
    first = (rows % (2 * quarter)) < quarter
    return jnp.where(first, pltpu.roll(v, HEAD - quarter, 0), pltpu.roll(v, quarter, 0))


def head_parts(raw, gain, cos, sin):
    inverse = inverse_rms(raw)
    hat = raw * inverse
    scaled = hat * gain
    return hat, inverse, (scaled * cos + swap_quarters(scaled) * sin).astype(BF16)


def probabilities(queries, keys):
    scores = dot(keys, queries, (0, 0)) * HEAD ** (-0.5)
    weights = jnp.exp(scores - jnp.max(scores, axis=0, keepdims=True))
    return weights * (1.0 / jnp.sum(weights, axis=0, keepdims=True))


def split_out(me, weight, rows, width, near, far, keep, over, weights=None):
    inner = 0.0
    for relative, out in ((3, far), (1, near), (0, keep), (2, over)):
        product = dot(weight[span(me, relative, width), :], rows)
        out[0, :width] = product.astype(out.dtype)
        if weights is not None:
            inner += jnp.sum(product * weights(relative), axis=0, keepdims=True)
    if weights is not None:
        far[0, width:] = two_parts(jnp.broadcast_to(inner, (8, inner.shape[1])))


def two_parts(values):
    high = values.astype(BF16)
    return jnp.concatenate([high.astype(F32), values - high.astype(F32)], axis=0).astype(BF16)


def attention_kernel(
    me_ref, p0, p1, p2, p3, mods, wqkv, wproj, gains, cos_ref, sin_ref,
    near, far, keep, over, attn_out, raw_out, heads_out, inverse_out,
    full, heads,
):
    me = me_ref[0]
    width = p0.shape[1]
    assemble((p0, p1, p2, p3), full, me)
    rows = full[...].astype(F32)
    inverse = inverse_rms(rows)
    inverse_out[0] = inverse
    columns_in = mods[0].T
    attn = (rows * inverse * (1.0 + columns_in[:, 1:2]) + columns_in[:, 0:1]).astype(BF16)
    attn_out[...] = attn
    raw_out[0] = dot(wqkv[...], attn)
    cos, sin = cos_ref[...], sin_ref[...]
    for head in range(width // HEAD):
        low = head * HEAD
        _, _, queries = head_parts(raw_out[0, low : low + HEAD], gains[:, 0:1], cos, sin)
        low += width
        _, _, keys = head_parts(raw_out[0, low : low + HEAD], gains[:, 1:2], cos, sin)
        low += width
        values = raw_out[0, low : low + HEAD].astype(BF16)
        attention = probabilities(queries, keys).astype(BF16)
        heads[head * HEAD : (head + 1) * HEAD] = dot(values, attention)
    out = heads[...].astype(BF16)
    heads_out[...] = out
    split_out(me, wproj, out, width, near, far, keep, over)


def mlp_kernel(
    me_ref, p0, p1, p2, p3, g0, g1, g2, g3, mods, wup_t, wup, wdown_t, wdown,
    near_a, far_a, keep_a, over_a, near_b, far_b, keep_b, over_b, mlp_out, hidden_out, rows_out, grad_out, inverse_out,
    full, modulated,
):
    me = me_ref[0]
    width = p0.shape[1]
    units = wdown.shape[0]
    assemble((p0, p1, p2, p3), full, me)
    rows = full[...].astype(F32)
    inverse = inverse_rms(rows)
    inverse_out[0] = inverse
    columns_in = mods[0].T
    scaled = rows * inverse * (1.0 + columns_in[:, 3:4])
    modulated[...] = scaled
    mlp = (scaled + columns_in[:, 2:3]).astype(BF16)
    mlp_out[...] = mlp
    gate = dot(wup_t[:units], mlp)
    up = dot(wup_t[units:], mlp)
    sigmoid = jax.nn.sigmoid(gate)
    silu = gate * sigmoid
    hidden = (silu * up).astype(BF16)
    hidden_out[...] = hidden
    assemble((g0, g1, g2, g3), full, me)
    grad_out[...] = full[...]
    grad_hidden = dot(wdown[...], full[...])
    rows_out[:units] = (grad_hidden * up * sigmoid * (1.0 + gate * (1.0 - sigmoid))).astype(BF16)
    rows_out[units:] = (grad_hidden * silu).astype(BF16)
    split_out(
        me, wup, rows_out[...], width, near_b, far_b, keep_b, over_b, lambda r: modulated[span(me, r, width), :]
    )
    split_out(me, wdown_t, hidden, width, near_a, far_a, keep_a, over_a)


def attention_back_kernel(
    me_ref, p0, p1, p2, p3, r0, r1, r2, r3, inverse_ref, mods, raw, wproj, wqkv_t, gains, cos_ref, sin_ref,
    near, far, keep, over, rows_out, grad_out, gains_out,
    full, heads, rows, scales, gains_sum,
):
    me = me_ref[0]
    width = p0.shape[1]
    assemble((p0, p1, p2, p3), full, me)
    grad_out[...] = full[...]
    heads[...] = dot(wproj[...], full[...])
    cos, sin = cos_ref[...], sin_ref[...]
    scale = HEAD ** (-0.5)

    @pl.when(pl.program_id(0) == 0)
    def _():
        gains_sum[...] = jnp.zeros_like(gains_sum)

    for head in range(width // HEAD):
        low = head * HEAD
        gain_q, gain_k = gains[:, 0:1], gains[:, 1:2]
        hat_q, inverse_q, queries = head_parts(raw[0, low : low + HEAD], gain_q, cos, sin)
        hat_k, inverse_k, keys = head_parts(raw[0, width + low : width + low + HEAD], gain_k, cos, sin)
        values = raw[0, 2 * width + low : 2 * width + low + HEAD].astype(BF16)
        grad_heads = heads[low : low + HEAD].astype(BF16)
        probability = probabilities(queries, keys)
        grad_attention = dot(values, grad_heads, (0, 0))
        rows[2 * width + low : 2 * width + low + HEAD] = dot(grad_heads, probability.astype(BF16), (1, 1))
        inner = jnp.sum(probability * grad_attention, axis=0, keepdims=True)
        grad_scores = (probability * (grad_attention - inner)).astype(BF16)
        grad_q = dot(keys, grad_scores) * scale
        grad_k = dot(queries, grad_scores, (1, 1)) * scale
        for index, grad, hat, inverse, gain in (
            (0, grad_q, hat_q, inverse_q, gain_q),
            (1, grad_k, hat_k, inverse_k, gain_k),
        ):
            grad = grad * cos - swap_quarters(grad) * sin
            product = grad * hat
            gains_sum[index] += product
            grad = grad * gain
            middle = jnp.mean(product * gain, axis=0, keepdims=True)
            start = index * width + low
            rows[start : start + HEAD] = inverse * (grad - hat * middle)
    rows_out[...] = rows[...].astype(BF16)
    inverse = inverse_ref[0]
    pieces = (r0, r1, r2, r3)
    scales[...] = mods[0].T

    def weights(relative):
        scale = 1.0 + scales[span(me, relative, width), 1:2]
        return pieces[relative][0].astype(F32) * inverse * scale

    split_out(me, wqkv_t, rows_out[...], width, near, far, keep, over, weights)

    @pl.when(pl.program_id(0) == pl.num_programs(0) - 1)
    def _():
        for index in range(2):
            gains_out[index : index + 1] = jnp.sum(gains_sum[index].T, axis=0, keepdims=True)


def columns_of(mods, width):
    return mods[0].T[:width]


def columns(values):
    lanes = lax.broadcasted_iota(jnp.int32, (values[0].shape[0], 128), 1)
    out = jnp.zeros((values[0].shape[0], 128), F32)
    for index, value in enumerate(values):
        out = jnp.where(lanes == index, value, out)
    return out


def sum_parts(values, width):
    return values[0, width : width + 1].astype(F32) + values[0, width + 8 : width + 9].astype(F32)


def total_inner(far, far_core, across, width):
    return (sum_parts(far, width) + sum_parts(far_core, width) + sum_parts(across, width)) / (4 * width)


def middle_back_kernel(
    s_ref, far, far_core, keep, core, across, cot, middle, branch, inverse_ref, mods,
    grad_out, piece_out, sums_out,
):
    width = keep.shape[1]
    modulation = columns_of(mods, width)
    inverse = inverse_ref[0]
    grad = keep[0] + core[0].astype(F32) + across[0, :width].astype(F32)
    normed = middle[0] * inverse
    inner = total_inner(far, far_core, across, width)
    grad_middle = cot[0] + inverse * (grad * (1.0 + modulation[:, 4:5]) - normed * inner)
    grad_out[0] = grad_middle
    piece_out[0] = (grad_middle * modulation[:, 2:3]).astype(BF16)
    sums_out[0] = columns(
        [
            jnp.sum(grad_middle * branch[0], axis=1, keepdims=True),
            jnp.sum(grad, axis=1, keepdims=True),
            jnp.sum(grad * normed, axis=1, keepdims=True),
        ]
    )


def last_kernel(
    s_ref, far, far_core, keep, core, across, grad_middle, latents, inverse_ref, mods,
    grad_out, back_out, sums_out,
):
    width = keep.shape[1]
    modulation = columns_of(mods, width)
    inverse = inverse_ref[0]
    grad = keep[0] + core[0].astype(F32) + across[0, :width].astype(F32)
    normed = latents[0] * inverse
    inner = total_inner(far, far_core, across, width)
    result = grad_middle[0] + inverse * (grad * (1.0 + modulation[:, 1:2]) - normed * inner)
    grad_out[0] = result
    back_out[0] = result.astype(BF16)
    sums_out[0] = columns(
        [jnp.sum(grad, axis=1, keepdims=True), jnp.sum(grad * normed, axis=1, keepdims=True)]
    )


def relay_kernel(s_ref, far, far_core, over, out):
    width = over.shape[1]
    out[0, :width] = (over[0] + far_core[0, :width].astype(F32)).astype(BF16)
    if out.shape[1] > width:
        inner = sum_parts(far, width) + sum_parts(far_core, width)
        out[0, width:] = two_parts(jnp.broadcast_to(inner, (8, inner.shape[1])))


def relay(scalars, far, far_core, over):
    images = over.shape[0]
    return call(
        relay_kernel, (images,), scalars,
        [by_image(far), by_image(far_core), by_image(over)],
        [image_out(images, far.shape[1:], BF16)],
    )[0]


def accumulate(lefts, rights, out):
    total = dot(lefts[0][...], rights[0][...], (1, 1))
    for left, right in zip(lefts[1:], rights[1:]):
        total += dot(left[...], right[...], (1, 1))
    out[...] = total.astype(out.dtype).reshape(out.shape)


def half_kernel(s_ref, *refs):
    parts = len(refs) // 2 - 1
    lefts, rights, out, kept = refs[:parts], refs[parts : 2 * parts], refs[-2], refs[-1]

    @pl.when(pl.program_id(0) == 0)
    def _():
        accumulate(lefts, rights, out)

    @pl.when(pl.program_id(0) == 1)
    def _():
        accumulate(lefts, rights, kept)


def weight_halves(index, lefts, rights, first, rows):
    half = rows // 2
    outer = rights[0].shape[0]
    place = lambda b, s: (first // half + b * s[0] + (1 - b) * (1 - s[0]), 0)
    ins = [(left, (half, left.shape[1]), place, False) for left in lefts] + [entire(right) for right in rights]
    block = (1, half, outer)
    outs = [(block, kind, block, lambda b, s: (0, 0, 0)) for kind in (BF16, F32)]
    return call(half_kernel, (2,), index, ins, outs)


def attention_weight_kernel(s_ref, *refs):
    parts = len(refs) // 4 - 1
    rows, heads, inputs, grads = (refs[i * parts : (i + 1) * parts] for i in range(4))
    out1, kept1, out2, kept2, total = refs[4 * parts :]
    group = pl.program_id(0)
    half = total.shape[0] // 2

    @pl.when(group < 3)
    def _():
        accumulate(rows, inputs, total)

    @pl.when(group == 3)
    def _():
        accumulate(heads, grads, total)

    def store(index, out, kept):
        out[0] = total[pl.ds(pl.multiple_of((1 - index) * half, 16), half)].astype(BF16)
        kept[0] = total[pl.ds(pl.multiple_of(index * half, 16), half)]

    @pl.when(group < 2)
    def _():
        store(s_ref[0], out1, kept1)

    @pl.when(group >= 2)
    def _():
        store(s_ref[1], out2, kept2)


def attention_weight_halves(indices, rows, heads, inputs, grads):
    size = heads[0].shape[0]
    outer = inputs[0].shape[0]
    ins = [(left, (size, left.shape[1]), lambda g, s: (jnp.minimum(g, 2), 0), False) for left in rows]
    ins += [entire(array) for array in heads + inputs + grads]
    shape, block = (2, size // 2, outer), (1, size // 2, outer)
    outs = []
    for place in (lambda g, s: (jnp.minimum(g, 1), 0, 0), lambda g, s: (jnp.maximum(g - 2, 0), 0, 0)):
        outs += [(shape, BF16, block, place), (shape, F32, block, place)]
    return call(attention_weight_kernel, (4,), indices, ins, outs, scratch=[pltpu.VMEM((size, outer), F32)])


def paired_kernel(s_ref, *refs):
    out = refs[-1]
    blocks = pl.num_programs(0) // 4
    units = out.shape[2]
    for index, source in enumerate(refs[:-1]):

        @pl.when(pl.program_id(0) // blocks == index)
        def _():
            values = source[0].astype(F32)
            for pair in range(out.shape[1]):
                out[:, pair, :] = values[:, pair * units : (pair + 1) * units]


def paired(indices, sources, pairs, size):
    _, half, outer = sources[0].shape
    blocks = half // size
    ins = [
        (a, (1, size, outer), lambda b, s, f=i * blocks: (0, jnp.clip(b - f, 0, blocks - 1), 0), False)
        for i, a in enumerate(sources)
    ]
    shape = (4 * half, pairs, outer // pairs)

    def place(b, s):
        chunk, within = b // (2 * blocks), b % (2 * blocks)
        own = jnp.where(chunk == 0, s[0], s[1])
        return (chunk * 2 * blocks + ((within // blocks) ^ own) * blocks + within % blocks, 0, 0)

    return call(paired_kernel, (4 * blocks,), indices, ins, [(shape, F32, (size,) + shape[1:], place)])[0]


def add_split_kernel(s_ref, own_a, got_a, own_b, got_b, out, kept):
    out[...] = (own_a[...] + got_a[...].astype(F32)).astype(BF16)
    kept[...] = own_b[...] + got_b[...].astype(F32)


def add_split(index, own, received, axis):
    groups, rows, outer = own.shape
    cut = 3 if outer % 384 == 0 else 1
    size = outer // cut
    if axis == 1:
        shape = (groups, rows // 2, outer)
        block = (1, rows // 2, size)
        here = lambda g, c, s: (g, s[0], c)
        there = lambda g, c, s: (g, 1 - s[0], c)
    else:
        half = groups // 2
        shape = (half, rows, outer)
        block = (1, rows, size)
        here = lambda g, c, s: (s[0] * half + g, 0, c)
        there = lambda g, c, s: ((1 - s[0]) * half + g, 0, c)
    plain = lambda g, c, s: (g, 0, c)
    ins = [
        (own, block, there, False),
        (received, block, there, False),
        (own, block, here, False),
        (received, block, here, False),
    ]
    outs = [(shape, BF16, block, plain), (shape, F32, block, plain)]
    return call(add_split_kernel, (shape[0], cut), index, ins, outs)


def unfold_kernel(s_ref, *refs):
    out = refs[-1]
    blocks = pl.num_programs(0) // (len(refs) - 1)
    for index, source in enumerate(refs[:-1]):

        @pl.when(pl.program_id(0) // blocks == index)
        def _():
            out[0] = source[0].astype(F32)


def unfold(index, segments):
    rows, outer = segments[0][0].shape[1:]
    ins = []
    for mine, other, group in segments:
        for half in (mine, other):
            ins.append((half, (1, rows, outer), lambda b, s, g=group: (g, 0, 0), False))
    place = lambda b, s: (b // 2, (b % 2) ^ s[0], 0)
    outs = [((len(segments), 2 * rows, outer), F32, (1, rows, outer), place)]
    return call(unfold_kernel, (len(ins),), index, ins, outs)[0]


def unfold_pair_kernel(s_ref, mine1, other1, mine2, other2, qkv, proj):
    step = pl.program_id(0)
    for index, source in enumerate((mine1, other1, mine2, other2)):

        @pl.when((step // 4) * 2 + step % 2 == index)
        def _():
            values = source[0].astype(F32)

            @pl.when(step < 6)
            def _():
                qkv[0] = values

            @pl.when(step >= 6)
            def _():
                proj[...] = values


def unfold_pair(indices, sources):
    _, half, outer = sources[0].shape
    block = (1, half, outer)
    first = lambda b, s: (jnp.minimum(b // 2, 1), 0, 0)
    second = lambda b, s: (jnp.maximum(b // 2 - 2, 0), 0, 0)
    ins = [(a, block, first if i < 2 else second, False) for i, a in enumerate(sources)]

    def row(b, s):
        return (b % 2) ^ jnp.where(b < 4, s[0], s[1])

    outs = [
        (
            (3, 2 * half, outer), F32, block,
            lambda b, s: (jnp.minimum(b // 2, 2), row(jnp.minimum(b, 5), s), 0),
        ),
        ((2 * half, outer), F32, block[1:], lambda b, s: (row(jnp.maximum(b, 6), s), 0)),
    ]
    return call(unfold_pair_kernel, (8,), indices, ins, outs)


class Order:
    def __init__(self):
        self.last = None

    def __call__(self, step, *args):
        if self.last is not None:
            args = lax.optimization_barrier((self.last, *args))[1:]
        result = step(*args)
        self.last = jax.tree.leaves(result)
        return result


class Reduction:
    def __init__(self, order, second_first=False):
        self.order = order
        self.bits = bits_of("dp")
        if second_first and len(self.bits) > 1:
            self.bits[:2] = self.bits[1::-1]
        self.levels = []

    def index(self, bit):
        return has_bit("dp", bit).astype(jnp.int32)[None]

    def first(self):
        return self.index(self.bits[0])

    def begin(self, out, own):
        self.own = own
        self.received = exchange(out, "dp", self.bits[0])

    def halve(self, level):
        if level >= len(self.bits):
            return
        bit = self.bits[level]
        groups, rows, _ = self.own.shape
        if rows % 16 == 0:
            axis = 1
        elif groups % 2 == 0:
            axis = 0
        else:
            axis = None
        if axis is None:
            self.own = self.order(lambda a, b: a + b.astype(F32), self.own, self.received)
            self.received = exchange(self.own.astype(BF16), "dp", bit)
            return
        index = self.index(bit)
        out, self.own = self.order(lambda a, b: add_split(index, a, b, axis), self.own, self.received)
        self.received = exchange(out, "dp", bit)
        self.levels.append((bit, axis))

    def join(self):
        self.own = self.order(lambda a, b: (a + b.astype(F32)).astype(BF16), self.own, self.received)
        bit = self.levels[-1][0] if self.levels else self.bits[0]
        self.received = exchange(self.own, "dp", bit)

    def double(self, level):
        if level >= len(self.levels):
            return
        bit, axis = self.levels[-1 - level]
        later = has_bit("dp", bit)
        self.own = self.order(lambda a, b: in_order(a, b, later, axis, jnp.concatenate), self.own, self.received)
        outer = self.levels[-2 - level][0] if level + 1 < len(self.levels) else self.bits[0]
        self.received = exchange(self.own, "dp", outer)


def rope_tables():
    quarter = HEAD // 4
    frequency = 10000.0 ** (-np.arange(quarter, dtype=np.float32) / quarter)
    patches = np.arange(P_SIZE)
    row = (patches // GRID).astype(np.float32)[None, :] * frequency[:, None]
    col = (patches % GRID).astype(np.float32)[None, :] * frequency[:, None]
    cos = np.concatenate([np.cos(row), np.cos(row), np.cos(col), np.cos(col)])
    sin = np.concatenate([-np.sin(row), np.sin(row), -np.sin(col), np.sin(col)])
    return jnp.asarray(cos, F32), jnp.asarray(sin, F32)


def einsum(spec, *operands):
    return jnp.einsum(spec, *operands, preferred_element_type=F32)


PARTS = ((0, 4),)


def pack_kernel(s_ref, rows, out):
    out[...] = rows[...].astype(BF16)


def last_slots(count, rows):
    slots = rows.shape[0]
    place = lambda i, s: (lax.rem(s[0] - IMG_DEV + i + slots, slots), 0, 0)
    ins = [(rows, (1,) + rows.shape[1:], place, False)]
    return call(pack_kernel, (IMG_DEV,), count, ins, [image_out(IMG_DEV, rows.shape[1:], BF16)])[0]


def transpose_kernel(s_ref, values, out):
    out[...] = values[...].T


def transposed(scalars, array):
    rows, outer = array.shape
    ins = [(array, (rows, 128), lambda i, s: (0, i), False)]
    return call(transpose_kernel, (outer // 128,), scalars, ins, [((outer, rows), array.dtype, (128, rows), lambda i, s: (i, 0))])[0]


def share_kernel(device_ref, facts, ids_out, own_out, load_out, histogram):
    devices, slots = facts.shape[0], facts.shape[1] - 1
    for b in range(NBINS):
        histogram[b] = 0

    def count(i, carry):
        for j in range(slots):
            b = facts[i, j]
            histogram[b] = histogram[b] + jnp.where(j < facts[i, slots], 1, 0)
        return carry

    lax.fori_loop(0, devices, count, 0)

    def place(i, carry):
        came, before = carry
        for k in range(IMG_DEV):
            moved = (i - 1) * slots + lax.rem(before - IMG_DEV + k + slots, slots)
            ids_out[i * IMG_DEV + k] = jnp.where(k >= IMG_DEV - came, moved, i * slots + k)

        @pl.when(i == device_ref[0])
        def _():
            own_out[0] = came

        return came + facts[i, slots] - IMG_DEV, facts[i, slots]

    lax.fori_loop(0, devices, place, (0, 0))
    for k in range(IMG_DEV):
        slot = ids_out[device_ref[0] * IMG_DEV + k]
        owner, j = lax.div(slot, slots), lax.rem(slot, slots)
        load_out[k] = histogram[facts[owner, j]]
        load_out[IMG_DEV + k] = jnp.where(j < facts[owner, slots], 1, 0)


def share(device, facts):
    smem = pl.BlockSpec(memory_space=pltpu.SMEM)
    return pl.pallas_call(
        share_kernel,
        grid_spec=pltpu.PrefetchScalarGridSpec(
            num_scalar_prefetch=1, grid=(), in_specs=[smem], out_specs=[smem] * 3,
            scratch_shapes=[pltpu.SMEM((NBINS,), jnp.int32)],
        ),
        out_shape=[jax.ShapeDtypeStruct((n,), jnp.int32) for n in (facts.shape[0] * IMG_DEV, 8, 2 * IMG_DEV)],
        cost_estimate=pl.CostEstimate(flops=1000, bytes_accessed=1000, transcendentals=0),
    )(device, facts)


def choose(s_ref, start, own, came):
    moved = pl.program_id(0) + start >= IMG_DEV - s_ref[0]
    return jnp.where(moved, came[0].astype(F32), own[0])


def rows_kernel(start, s_ref, own, came, rows_out, piece_out):
    rows = choose(s_ref, start, own, came)
    rows_out[0] = rows
    piece_out[0] = rows.astype(BF16)


def cot_kernel(start, s_ref, own, came, mods, rows_out, piece_out):
    modulation = columns_of(mods, own.shape[1])
    rows = choose(s_ref, start, own, came) * modulation[:, 6:7]
    rows_out[0] = rows
    piece_out[0] = (rows * modulation[:, 5:6]).astype(BF16)


def from_image(array, start):
    rest = array.shape[1:]
    return (array, (1,) + rest, lambda i, s: (i + start,) + (0,) * len(rest), False)


def middle_kernel(s_ref, keep, core, across, rows, mods, branch_out, middle_out, piece_out):
    branch = keep[0] + core[0].astype(F32) + across[0].astype(F32)
    branch_out[0] = branch
    middle = rows[0] + columns_of(mods, rows.shape[1])[:, 2:3] * branch
    middle_out[0] = middle
    piece_out[0] = middle.astype(BF16)


def result_kernel(s_ref, keep, core, across, middle, cot, mods, result_out, back_out, sums_out):
    branch = keep[0] + core[0].astype(F32) + across[0].astype(F32)
    result = middle[0] + columns_of(mods, middle.shape[1])[:, 5:6] * branch
    result_out[0] = result
    back_out[0] = result.astype(BF16)
    sums_out[0] = columns([jnp.sum(cot[0] * branch, axis=1, keepdims=True)])


def home_kernel(starts, s_ref, *refs):
    out = refs[-1]
    parts = len(starts)
    slot = pl.program_id(0)
    came, count = s_ref[0], s_ref[1]
    kept, away = refs[0][0], refs[parts][0].astype(F32)
    for part in range(1, parts):
        kept = jnp.where(slot >= starts[part], refs[part][0], kept)
        place = slot - count + IMG_DEV
        away = jnp.where(place >= starts[part], refs[parts + part][0].astype(F32), away)
    chosen = jnp.where(slot < IMG_DEV - came, kept, away)
    out[0] = jnp.where(slot < count, chosen, 0.0)


def home(scalars, slots, here, back):
    starts, start = [], 0
    for part in here:
        starts.append(start)
        start += part.shape[0]
    block = (1,) + here[0].shape[1:]
    ins = []
    for part, first in zip(here, starts):
        end = part.shape[0] - 1
        ins.append((part, block, lambda i, s, f=first, e=end: (jnp.clip(i - f, 0, e), 0, 0), False))
    for part, first in zip(back, starts):
        end = part.shape[0] - 1
        ins.append(
            (part, block, lambda i, s, f=first, e=end: (jnp.clip(i - s[1] + IMG_DEV - f, 0, e), 0, 0), False)
        )
    outs = [image_out(slots, block[1:], F32)]
    return call(functools.partial(home_kernel, starts), (slots,), scalars, ins, outs)[0]


def local(
    latents,
    condition,
    cotangent,
    noise_bins,
    image_counts,
    ada_weight,
    ada_bias,
    qkv_weight,
    norm_gains,
    proj_weight,
    gate_up_weight,
    down_weight,
):
    slots = latents.shape[0]
    devices = lax.axis_size("dp")
    device = lax.axis_index("dp").astype(jnp.int32)
    part = lax.axis_index("mp")
    me = part.astype(jnp.int32)[None]
    width = latents.shape[2]
    features = qkv_weight.shape[0]
    units = down_weight.shape[0]
    rows_in = latents.transpose(0, 2, 1)
    cot_in = cotangent.transpose(0, 2, 1)
    cos, sin = rope_tables()
    gains = norm_gains.astype(F32).T
    order = Order()

    own_count = image_counts[0]
    silu = jax.nn.silu(condition)
    facts = jnp.concatenate([noise_bins, image_counts]).astype(F32)
    facts = jnp.pad(facts, (0, width - slots - 1))[None]
    message = jnp.concatenate([silu, facts]).astype(BF16)[None]
    latest = (own_count - IMG_DEV + jnp.arange(IMG_DEV)) % slots
    silu_came = shifted(jnp.take(silu, latest, axis=0).astype(BF16), "dp", 1)
    message = gather_small(message, "dp", 0)
    facts = message[:, slots, : slots + 1].astype(jnp.int32)
    rows_last = order(last_slots, image_counts, rows_in)
    share_ids, own_facts, loads = order(lambda f: share(device[None], f), facts)
    came_here = own_facts[:1]
    home_facts = jnp.concatenate([came_here, image_counts])
    rows_last, _ = lax.optimization_barrier((rows_last, own_facts))
    rows_came = shifted(rows_last, "dp", 1)
    came = types.SimpleNamespace()

    silu_near = jnp.concatenate([silu[:IMG_DEV].astype(BF16), silu_came])
    silu_near = gather_small(silu_near, "mp", 1)
    modulation = einsum("bd,dkf->bkf", silu_near, ada_weight) + ada_bias.astype(F32)
    spread_mods = jnp.concatenate([modulation[:, 0:2], modulation[:, 3:5]], axis=1)
    spread_mods = gather_small(spread_mods, "mp", 2)

    parts = PARTS
    count = len(parts)
    state = [types.SimpleNamespace() for _ in parts]
    wqkv = qkv_weight.transpose(1, 2, 0).reshape(3 * width, features)
    weights = types.SimpleNamespace()

    def prepare():
        up = order(lambda w: w.reshape(features, 2 * units), gate_up_weight)
        weights.up = up
        weights.proj_t, weights.qkv_t, weights.down_t = (
            order(lambda w: transposed(me, w), array) for array in (proj_weight, wqkv, down_weight)
        )
        cot_last = order(last_slots, image_counts, cot_in)
        cot_ready, _ = lax.optimization_barrier((cot_last, weights.down_t))
        came.cot = shifted(cot_ready, "dp", 1)

    def prepare_up():
        weights.up_t = order(lambda w: transposed(me, w), weights.up)

    def choose_rows(p):
        start, images = parts[p]
        st = state[p]
        rest = rows_in.shape[1:]
        st.rows, piece = order(
            lambda own, came: call(
                functools.partial(rows_kernel, start), (images,), came_here,
                [from_image(own, start), from_image(came, start)],
                [image_out(images, rest, F32), image_out(images, rest, BF16)],
            ),
            rows_in, rows_came,
        )
        st.pieces_one = spread(piece)

    moved = (jnp.arange(IMG_DEV) >= IMG_DEV - came_here[0])[:, None, None]
    spread_mods = jnp.where(moved, spread_mods[IMG_DEV:], spread_mods[:IMG_DEV])
    spread_mods = jnp.pad(spread_mods, ((0, 0), (0, 4), (0, 0)))
    modulation = jnp.where(moved, modulation[IMG_DEV:], modulation[:IMG_DEV])
    load, live = loads[:IMG_DEV].astype(F32), loads[IMG_DEV:].astype(F32)
    scaling = live * (IMG_DEV * devices) / (NBINS * (load + 1.0 - live))
    scaling = jnp.broadcast_to(scaling[:, None, None], (IMG_DEV, 2, width))
    mods_all = jnp.concatenate([modulation, scaling], axis=1)
    mods_all = jnp.pad(mods_all, ((0, 0), (0, 0), (0, -width % 128)))
    for p, (start, images) in enumerate(parts):
        state[p].mods_full = spread_mods[start : start + images]
        state[p].mods = mods_all[start : start + images]

    def attention(p):
        st = state[p]
        images = parts[p][1]
        st.near, st.far, st.keep, st.over, st.attn, st.raw, st.heads, st.inverse_one = order(
            lambda *a: call(
                attention_kernel, (images,), me,
                [by_image(x) for x in a[:5]] + [entire(x) for x in a[5:]],
                [
                    image_out(images, (width, P_SIZE), BF16),
                    image_out(images, (width, P_SIZE), BF16),
                    image_out(images, (width, P_SIZE), F32),
                    image_out(images, (width, P_SIZE), F32),
                    flat_out(images, features),
                    image_out(images, (3 * width, P_SIZE), F32),
                    flat_out(images, width),
                    image_out(images, (1, P_SIZE), F32),
                ],
                scratch=[pltpu.VMEM((features, P_SIZE), BF16), pltpu.VMEM((width, P_SIZE), F32)],
                us=4.5 * images,
                vmem=48,
            ),
            *st.pieces_one, st.mods_full, wqkv, weights.proj_t, gains, cos, sin,
        )
        far, near, _ = lax.optimization_barrier((st.far, st.near, st.pieces_grad_two[2]))
        st.far_core = exchange(far, "mp", 1)
        st.core = exchange(near, "mp", 1)

    def choose_cot(p):
        start, images = parts[p]
        st = state[p]
        rest = rows_in.shape[1:]
        st.cot, piece = order(
            lambda own, came, mods: call(
                functools.partial(cot_kernel, start), (images,), came_here,
                [from_image(own, start), from_image(came, start), by_image(mods)],
                [image_out(images, rest, F32), image_out(images, rest, BF16)],
            ),
            cot_in, came.cot, st.mods,
        )
        st.pieces_grad_two = spread(piece)

    def relay_one(p):
        st = state[p]
        out = order(lambda *a: relay(me, *a), st.far, st.far_core, st.over)
        st.across = exchange(out, "mp", 2)

    def middle(p):
        st = state[p]
        images = parts[p][1]
        rest = (width, P_SIZE)
        st.branch_one, st.middle, piece = order(
            lambda keep, core, *a: call(
                middle_kernel, (images,), me,
                [by_image(keep), by_image(core)] + [by_image(x) for x in a],
                [image_out(images, rest, F32), image_out(images, rest, F32), image_out(images, rest, BF16)],
            ),
            st.keep, st.core, st.across, st.rows, st.mods,
        )
        st.pieces_two = spread(piece)

    def mlp(p):
        st = state[p]
        images = parts[p][1]
        (
            st.near_a, st.far_a, st.keep_a, st.over_a,
            st.near_b, st.far_b, st.keep_b, st.over_b,
            st.mlp, st.hidden, st.grad_rows_two, st.grad_two, st.inverse_two,
        ) = order(
            lambda *a: call(
                mlp_kernel, (images,), me,
                [by_image(x) for x in a[:9]] + [entire(x) for x in a[9:]],
                [
                    image_out(images, (width, P_SIZE), BF16),
                    image_out(images, (width, P_SIZE), BF16),
                    image_out(images, (width, P_SIZE), F32),
                    image_out(images, (width, P_SIZE), F32),
                    image_out(images, (width, P_SIZE), BF16),
                    image_out(images, (width + 16, P_SIZE), BF16),
                    image_out(images, (width, P_SIZE), F32),
                    image_out(images, (width, P_SIZE), F32),
                    flat_out(images, features),
                    flat_out(images, units),
                    flat_out(images, 2 * units),
                    flat_out(images, features),
                    image_out(images, (1, P_SIZE), F32),
                ],
                scratch=[pltpu.VMEM((features, P_SIZE), BF16), pltpu.VMEM((features, P_SIZE), F32)],
                us=6.0 * images,
                vmem=48,
            ),
            *st.pieces_two, *st.pieces_grad_two, st.mods_full,
            weights.up_t, weights.up, weights.down_t, down_weight,
        )
        st.far_core_b = exchange(st.far_b, "mp", 1)
        st.core_b = exchange(st.near_b, "mp", 1)

    def relay_three(p):
        st = state[p]
        out = order(lambda *a: relay(me, *a), st.far_b, st.far_core_b, st.over_b)
        st.across_b = exchange(out, "mp", 2)

    def middle_back(p):
        st = state[p]
        images = parts[p][1]
        st.grad_middle, piece, st.sums_two = order(
            lambda *a: call(
                middle_back_kernel, (images,), me, [by_image(x) for x in a],
                [
                    image_out(images, (width, P_SIZE), F32),
                    image_out(images, (width, P_SIZE), BF16),
                    image_out(images, (width, 128), F32),
                ],
            ),
            st.far_b, st.far_core_b, st.keep_b, st.core_b, st.across_b, st.cot, st.middle,
            st.branch_one, st.inverse_two, st.mods,
        )
        st.pieces_grad_one = spread(piece)

    def result_core(p):
        st = state[p]
        far, near, _ = lax.optimization_barrier((st.far_a, st.near_a, order.last))
        st.far_core_a = exchange(far, "mp", 1)
        st.core_a = exchange(near, "mp", 1)

    def relay_two(p):
        st = state[p]
        out = order(lambda *a: relay(me, *a), st.far_a, st.far_core_a, st.over_a)
        st.across_a = exchange(out, "mp", 2)

    def result(p):
        st = state[p]
        images = parts[p][1]
        st.result, back, st.sums_three = order(
            lambda keep, core, *a: call(
                result_kernel, (images,), me,
                [by_image(keep), by_image(core)] + [by_image(x) for x in a],
                [
                    image_out(images, (width, P_SIZE), F32),
                    image_out(images, (width, P_SIZE), BF16),
                    image_out(images, (width, 128), F32),
                ],
            ),
            st.keep_a, st.core_a, st.across_a, st.middle, st.cot, st.mods,
        )
        st.result_out = back

    def attention_back(p):
        st = state[p]
        images = parts[p][1]
        st.near_c, st.far_c, st.keep_c, st.over_c, st.grad_rows_one, st.grad_one, st.gain_sums = order(
            lambda *a: call(
                attention_back_kernel, (images,), me,
                [by_image(x) for x in a[:11]] + [entire(x) for x in a[11:]],
                [
                    image_out(images, (width, P_SIZE), BF16),
                    image_out(images, (width + 16, P_SIZE), BF16),
                    image_out(images, (width, P_SIZE), F32),
                    image_out(images, (width, P_SIZE), F32),
                    flat_out(images, 3 * width),
                    flat_out(images, features),
                    ((2, HEAD), F32, (2, HEAD), lambda i, s: (0, 0)),
                ],
                scratch=[
                    pltpu.VMEM((features, P_SIZE), BF16),
                    pltpu.VMEM((width, P_SIZE), F32),
                    pltpu.VMEM((3 * width, P_SIZE), F32),
                    pltpu.VMEM((features, 8), F32),
                    pltpu.VMEM((2, HEAD, P_SIZE), F32),
                ],
                us=4.5 * images,
                vmem=48,
            ),
            *st.pieces_grad_one, *st.pieces_one, st.inverse_one, st.mods_full, st.raw,
            proj_weight, weights.qkv_t, gains, cos, sin,
        )
        st.far_core_c = exchange(st.far_c, "mp", 1)
        st.core_c = exchange(st.near_c, "mp", 1)

    def relay_four(p):
        st = state[p]
        out = order(lambda *a: relay(me, *a), st.far_c, st.far_core_c, st.over_c)
        st.across_c = exchange(out, "mp", 2)

    def last(p):
        st = state[p]
        images = parts[p][1]
        st.grad_latent, back, st.sums_one = order(
            lambda *a: call(
                last_kernel, (images,), me, [by_image(x) for x in a],
                [
                    image_out(images, (width, P_SIZE), F32),
                    image_out(images, (width, P_SIZE), BF16),
                    image_out(images, (width, 128), F32),
                ],
            ),
            st.far_c, st.far_core_c, st.keep_c, st.core_c, st.across_c, st.grad_middle, st.rows,
            st.inverse_one, st.mods,
        )
        st.latent_out = back

    def each(field):
        return [field(st) for st in state]

    attn1 = Reduction(order, True)
    attn2 = Reduction(order, False)
    up1 = Reduction(order, False)
    up2 = Reduction(order, False)
    down = Reduction(order, True)

    def attention_weights():
        indices = jnp.concatenate([attn1.first(), attn2.first()])
        out1, own1, out2, own2 = order(
            lambda *a: attention_weight_halves(indices, *(a[i * count : (i + 1) * count] for i in range(4))),
            *each(lambda s: s.grad_rows_one), *each(lambda s: s.heads),
            *each(lambda s: s.attn), *each(lambda s: s.grad_one),
        )
        attn1.begin(out1, own1)
        attn2.begin(out2, own2)

    def begin(reduction):
        if reduction is down:
            lefts, rights, first, rows = each(lambda s: s.hidden), each(lambda s: s.grad_two), 0, units
        else:
            lefts, rights, rows = each(lambda s: s.mlp), each(lambda s: s.grad_rows_two), features // 2
            first = 0 if reduction is up1 else rows
        index = reduction.first()
        reduction.begin(
            *order(lambda *a: weight_halves(index, a[:count], a[count:], first, rows), *lefts, *rights)
        )

    def halve(reduction, level):
        reduction.halve(level)

    def join(reduction):
        for level in range(3, len(reduction.bits)):
            reduction.halve(level)
        reduction.join()
        for level in range(0, len(reduction.levels) - 2):
            reduction.double(level)

    def double(reduction, step):
        reduction.double(max(0, len(reduction.levels) - 2) + step)

    def unfolded(reduction, groups):
        index = reduction.first()
        return order(lambda a, b: unfold(index, [(a, b, g) for g in groups]), reduction.own, reduction.received)

    def finish_attention():
        done.qkv = order(
            lambda *a: unfold_pair(jnp.concatenate([attn1.first(), attn2.first()]), a),
            attn1.own, attn1.received, attn2.own, attn2.received,
        )

    def finish_down():
        done.down = unfolded(down, (0,))[0]

    def finish_up():
        indices = jnp.concatenate([up1.first(), up2.first()])
        done.up = order(
            lambda *a: paired(indices, a, 2, features // 8), up1.own, up1.received, up2.own, up2.received
        )

    done = types.SimpleNamespace()

    def send_result(p):
        out, _ = lax.optimization_barrier((state[p].result_out, order.last))
        state[p].result_back = shifted(out, "dp", -1)

    def send_latent(p):
        out, _ = lax.optimization_barrier((state[p].latent_out, order.last))
        state[p].latent_back = shifted(out, "dp", -1)

    def modulation_back():
        columns_one, columns_two, columns_three = (
            jnp.concatenate(each(field))
            for field in (lambda s: s.sums_one, lambda s: s.sums_two, lambda s: s.sums_three)
        )
        grad_mod = jnp.stack(
            [
                columns_one[..., 0],
                columns_one[..., 1],
                columns_two[..., 0],
                columns_two[..., 1],
                columns_two[..., 2],
                columns_three[..., 0],
            ]
        ).astype(BF16)
        gain_sums = sum(each(lambda s: s.gain_sums)).reshape(1, -1)
        high = gain_sums.astype(BF16)
        gain_row = jnp.concatenate([high, (gain_sums - high.astype(F32)).astype(BF16)], axis=1)
        sent = jnp.concatenate([grad_mod.reshape(6 * IMG_DEV, width), gain_row])[None]
        done.message = sent
        done.bits = bits_of("dp")
        modulation_send()

    def modulation_send():
        done.other = exchange(done.message, "dp", done.bits[0])

    def modulation_step():
        later = has_bit("dp", done.bits.pop(0))
        done.message = order(lambda a, b: in_order(a, b, later, 0, jnp.concatenate), done.message, done.other)
        if done.bits:
            modulation_send()

    def ada_back():
        while done.bits:
            modulation_step()
        sent = done.message
        mod_share = sent[:, : 6 * IMG_DEV].reshape(devices, 6, IMG_DEV, width).transpose(1, 0, 2, 3)
        mod_share = mod_share.reshape(6, devices * IMG_DEV, width)
        gain_sums = jnp.sum(sent[:, 6 * IMG_DEV].astype(F32), axis=0).reshape(2, 2, HEAD)
        done.gains = sum_small(gain_sums[0] + gain_sums[1], "mp")
        silu_all = gather_small(message[:, :slots], "mp", 2).reshape(devices * slots, -1)
        silu_share = jnp.take(silu_all, share_ids, axis=0)
        done.ada = order(lambda a, b: einsum("kbf,bd->kfd", a, b), mod_share, silu_share)
        done.bias = jnp.sum(mod_share.astype(F32), axis=1)

        slot = jnp.arange(slots)
        stays = slot < IMG_DEV - came_here[0]
        away_place = jnp.clip(slot - own_count + IMG_DEV, 0, IMG_DEV - 1)
        share_place = jnp.where(stays, device * IMG_DEV + slot, (device + 1) * IMG_DEV + away_place)
        share_place = jnp.clip(share_place, 0, devices * IMG_DEV - 1)
        live_here = (slot < own_count).astype(BF16)
        mod_slots = jnp.take(mod_share, share_place, axis=1) * live_here[None, :, None]
        grad_silu = sum_small(einsum("kbf,dkf->bd", mod_slots, ada_weight), "mp")
        grad_silu = lax.dynamic_slice_in_dim(grad_silu, part * width, width, 1)
        sigmoid_cond = jax.nn.sigmoid(condition)
        done.cond = grad_silu * sigmoid_cond * (1.0 + condition * (1.0 - sigmoid_cond))

    def home_result():
        done.output = order(
            lambda *a: home(home_facts, slots, a[:count], a[count:]), *each(lambda s: s.result), *each(lambda s: s.result_back)
        )

    def home_latent():
        done.latent = order(
            lambda *a: home(home_facts, slots, a[:count], a[count:]), *each(lambda s: s.grad_latent), *each(lambda s: s.latent_back)
        )

    prepare()
    choose_rows(0)
    choose_cot(0)
    attention(0)
    relay_one(0)
    prepare_up()
    middle(0)
    mlp(0)
    relay_three(0)
    begin(up1)
    begin(down)
    begin(up2)
    middle_back(0)
    halve(up1, 1)
    result_core(0)
    halve(down, 1)
    relay_two(0)
    halve(up2, 1)
    halve(up1, 2)
    attention_back(0)
    join(up1)
    halve(down, 2)
    attention_weights()
    halve(up2, 2)
    relay_four(0)
    double(up1, 0)
    result(0)
    send_result(0)
    join(down)
    halve(attn1, 1)
    halve(attn2, 1)
    last(0)
    send_latent(0)
    join(up2)
    double(up1, 1)
    modulation_back()
    home_result()
    halve(attn1, 2)
    double(down, 0)
    halve(attn2, 2)
    home_latent()
    double(up2, 0)
    join(attn1)
    modulation_step()
    join(attn2)
    double(down, 1)
    double(up2, 1)
    modulation_step()
    double(attn1, 0)
    double(attn2, 0)
    finish_down()
    finish_up()
    double(attn1, 1)
    double(attn2, 1)
    modulation_step()
    ada_back()
    finish_attention()
    return (
        done.output.transpose(0, 2, 1),
        done.latent.transpose(0, 2, 1),
        done.cond,
        done.ada.transpose(2, 0, 1),
        done.bias,
        done.qkv[0].transpose(2, 0, 1),
        done.gains,
        done.qkv[1],
        done.up,
        done.down,
    )


def solution(mesh):
    return jax.shard_map(
        local,
        mesh=mesh,
        in_specs=(
            P("dp", None, "mp"),
            P("dp", "mp"),
            P("dp", None, "mp"),
            P("dp"),
            P("dp"),
            P(None, None, "mp"),
            P(None, "mp"),
            P(None, None, "mp"),
            P(),
            P("mp", None),
            P(None, None, "mp"),
            P("mp", None),
        ),
        out_specs=(
            P("dp", None, "mp"),
            P("dp", None, "mp"),
            P("dp", "mp"),
            P(None, None, "mp"),
            P(None, "mp"),
            P(None, None, "mp"),
            P(),
            P("mp", None),
            P(None, None, "mp"),
            P("mp", None),
        ),
        check_vma=False,
    )
```

```python
import functools
import types

import jax
import jax.numpy as jnp
import numpy as np
from jax import lax
from jax.experimental import pallas as pl
from jax.experimental.pallas import tpu as pltpu
from jax.sharding import PartitionSpec as P

HEAD = 72
P_SIZE = 256
GRID = 16
IMG_DEV = 4
NBINS = 8

EPSILON = 1e-06
F32 = jnp.float32
BF16 = jnp.bfloat16
MIB = 1 << 20
WEIGHT = 0.1 * 1e9


def exchange(value, axis, bit):
    pairs = [(i, i ^ bit) for i in range(lax.axis_size(axis))]
    return lax.ppermute(value, axis, pairs)


def shifted(value, axis, by):
    devices = lax.axis_size(axis)
    pairs = [(i, i + by) for i in range(devices) if 0 <= i + by < devices]
    return lax.ppermute(value, axis, pairs)


def bits_of(axis):
    bits, bit = [], 1
    while bit < lax.axis_size(axis):
        bits.append(bit)
        bit *= 2
    return bits


def has_bit(axis, bit):
    return (lax.axis_index(axis) & bit) != 0


def in_order(mine, other, later, axis, join):
    return jnp.where(later, join([other, mine], axis=axis), join([mine, other], axis=axis))


def gather_small(value, axis, dim):
    for bit in bits_of(axis):
        other = exchange(value, axis, bit)
        value = in_order(value, other, has_bit(axis, bit), dim, jnp.concatenate)
    return value


def sum_small(value, axis):
    for bit in bits_of(axis):
        value = value + exchange(value, axis, bit)
    return value


def pick(value, index, dim):
    return lax.dynamic_index_in_dim(value, index, dim, keepdims=False)


def spread(piece):
    core = exchange(piece, "mp", 1)
    over = exchange(piece, "mp", 2)
    both = exchange(over, "mp", 1)
    return [piece, core, over, both]


def call(kernel, grid, scalars, ins, outs, scratch=(), vmem=24, us=3.0):
    in_specs = [
        pl.BlockSpec(block, index, pipeline_mode=pl.Buffered(1)) if whole else pl.BlockSpec(block, index)
        for _, block, index, whole in ins
    ]
    return pl.pallas_call(
        kernel,
        grid_spec=pltpu.PrefetchScalarGridSpec(
            num_scalar_prefetch=1,
            grid=grid,
            in_specs=in_specs,
            out_specs=[pl.BlockSpec(block, index) for _, _, block, index in outs],
            scratch_shapes=list(scratch),
        ),
        out_shape=[jax.ShapeDtypeStruct(shape, kind) for shape, kind, _, _ in outs],
        compiler_params=pltpu.CompilerParams(
            dimension_semantics=("arbitrary",) * len(grid), vmem_limit_bytes=vmem * MIB
        ),
        cost_estimate=pl.CostEstimate(flops=int(us * WEIGHT), bytes_accessed=1000, transcendentals=0),
    )(scalars, *(a for a, _, _, _ in ins))


def by_image(array):
    rest = array.shape[1:]
    return (array, (1,) + rest, lambda i, s: (i,) + (0,) * len(rest), False)


def entire(array):
    return (array, array.shape, lambda i, s: (0,) * array.ndim, True)


def image_out(images, rest, kind):
    return ((images,) + rest, kind, (1,) + rest, lambda i, s: (i,) + (0,) * len(rest))


def flat_out(images, rows):
    return ((rows, images * P_SIZE), BF16, (rows, P_SIZE), lambda i, s: (0, i))


def dot(a, b, over=(1, 0)):
    return lax.dot_general(a, b, (((over[0],), (over[1],)), ((), ())), preferred_element_type=F32)


def span(me, relative, width):
    return pl.ds(pl.multiple_of((me ^ relative) * width, 32), width)


def assemble(pieces, full, me):
    width = pieces[0].shape[1]
    for relative, piece in enumerate(pieces):
        full[span(me, relative, width), :] = piece[0]


def inverse_rms(rows):
    return lax.rsqrt(jnp.mean(rows * rows, axis=0, keepdims=True) + EPSILON)


def swap_quarters(v):
    rows = lax.broadcasted_iota(jnp.int32, v.shape, 0)
    quarter = HEAD // 4
    first = (rows % (2 * quarter)) < quarter
    return jnp.where(first, pltpu.roll(v, HEAD - quarter, 0), pltpu.roll(v, quarter, 0))


def head_parts(raw, gain, cos, sin):
    inverse = inverse_rms(raw)
    hat = raw * inverse
    scaled = hat * gain
    return hat, inverse, (scaled * cos + swap_quarters(scaled) * sin).astype(BF16)


def probabilities(queries, keys):
    scores = dot(keys, queries, (0, 0)) * HEAD ** (-0.5)
    weights = jnp.exp(scores - jnp.max(scores, axis=0, keepdims=True))
    return weights * (1.0 / jnp.sum(weights, axis=0, keepdims=True))


def split_out(me, weight, rows, width, near, far, keep, over, weights=None):
    inner = 0.0
    for relative, out in ((3, far), (1, near), (0, keep), (2, over)):
        product = dot(weight[span(me, relative, width), :], rows)
        out[0, :width] = product.astype(out.dtype)
        if weights is not None:
            inner += jnp.sum(product * weights(relative), axis=0, keepdims=True)
    if weights is not None:
        far[0, width:] = two_parts(jnp.broadcast_to(inner, (8, inner.shape[1])))


def two_parts(values):
    high = values.astype(BF16)
    return jnp.concatenate([high.astype(F32), values - high.astype(F32)], axis=0).astype(BF16)


def attention_kernel(
    me_ref, p0, p1, p2, p3, mods, wqkv, wproj, gains, cos_ref, sin_ref,
    near, far, keep, over, attn_out, raw_out, heads_out, inverse_out,
    full, heads,
):
    me = me_ref[0]
    width = p0.shape[1]
    assemble((p0, p1, p2, p3), full, me)
    rows = full[...].astype(F32)
    inverse = inverse_rms(rows)
    inverse_out[0] = inverse
    columns_in = mods[0].T
    attn = (rows * inverse * (1.0 + columns_in[:, 1:2]) + columns_in[:, 0:1]).astype(BF16)
    attn_out[...] = attn
    raw_out[0] = dot(wqkv[...], attn)
    cos, sin = cos_ref[...], sin_ref[...]
    for head in range(width // HEAD):
        low = head * HEAD
        _, _, queries = head_parts(raw_out[0, low : low + HEAD], gains[:, 0:1], cos, sin)
        low += width
        _, _, keys = head_parts(raw_out[0, low : low + HEAD], gains[:, 1:2], cos, sin)
        low += width
        values = raw_out[0, low : low + HEAD].astype(BF16)
        attention = probabilities(queries, keys).astype(BF16)
        heads[head * HEAD : (head + 1) * HEAD] = dot(values, attention)
    out = heads[...].astype(BF16)
    heads_out[...] = out
    split_out(me, wproj, out, width, near, far, keep, over)


def mlp_kernel(
    me_ref, p0, p1, p2, p3, g0, g1, g2, g3, mods, wup_t, wup, wdown_t, wdown,
    near_a, far_a, keep_a, over_a, near_b, far_b, keep_b, over_b, mlp_out, hidden_out, rows_out, grad_out, inverse_out,
    full, modulated,
):
    me = me_ref[0]
    width = p0.shape[1]
    units = wdown.shape[0]
    assemble((p0, p1, p2, p3), full, me)
    rows = full[...].astype(F32)
    inverse = inverse_rms(rows)
    inverse_out[0] = inverse
    columns_in = mods[0].T
    scaled = rows * inverse * (1.0 + columns_in[:, 3:4])
    modulated[...] = scaled
    mlp = (scaled + columns_in[:, 2:3]).astype(BF16)
    mlp_out[...] = mlp
    gate = dot(wup_t[:units], mlp)
    up = dot(wup_t[units:], mlp)
    sigmoid = jax.nn.sigmoid(gate)
    silu = gate * sigmoid
    hidden = (silu * up).astype(BF16)
    hidden_out[...] = hidden
    assemble((g0, g1, g2, g3), full, me)
    grad_out[...] = full[...]
    grad_hidden = dot(wdown[...], full[...])
    rows_out[:units] = (grad_hidden * up * sigmoid * (1.0 + gate * (1.0 - sigmoid))).astype(BF16)
    rows_out[units:] = (grad_hidden * silu).astype(BF16)
    split_out(
        me, wup, rows_out[...], width, near_b, far_b, keep_b, over_b, lambda r: modulated[span(me, r, width), :]
    )
    split_out(me, wdown_t, hidden, width, near_a, far_a, keep_a, over_a)


def attention_back_kernel(
    me_ref, p0, p1, p2, p3, r0, r1, r2, r3, inverse_ref, mods, raw, wproj, wqkv_t, gains, cos_ref, sin_ref,
    near, far, keep, over, rows_out, grad_out, gains_out,
    full, heads, rows, scales, gains_sum,
):
    me = me_ref[0]
    width = p0.shape[1]
    assemble((p0, p1, p2, p3), full, me)
    grad_out[...] = full[...]
    heads[...] = dot(wproj[...], full[...])
    cos, sin = cos_ref[...], sin_ref[...]
    scale = HEAD ** (-0.5)

    @pl.when(pl.program_id(0) == 0)
    def _():
        gains_sum[...] = jnp.zeros_like(gains_sum)

    for head in range(width // HEAD):
        low = head * HEAD
        gain_q, gain_k = gains[:, 0:1], gains[:, 1:2]
        hat_q, inverse_q, queries = head_parts(raw[0, low : low + HEAD], gain_q, cos, sin)
        hat_k, inverse_k, keys = head_parts(raw[0, width + low : width + low + HEAD], gain_k, cos, sin)
        values = raw[0, 2 * width + low : 2 * width + low + HEAD].astype(BF16)
        grad_heads = heads[low : low + HEAD].astype(BF16)
        probability = probabilities(queries, keys)
        grad_attention = dot(values, grad_heads, (0, 0))
        rows[2 * width + low : 2 * width + low + HEAD] = dot(grad_heads, probability.astype(BF16), (1, 1))
        inner = jnp.sum(probability * grad_attention, axis=0, keepdims=True)
        grad_scores = (probability * (grad_attention - inner)).astype(BF16)
        grad_q = dot(keys, grad_scores) * scale
        grad_k = dot(queries, grad_scores, (1, 1)) * scale
        for index, grad, hat, inverse, gain in (
            (0, grad_q, hat_q, inverse_q, gain_q),
            (1, grad_k, hat_k, inverse_k, gain_k),
        ):
            grad = grad * cos - swap_quarters(grad) * sin
            product = grad * hat
            gains_sum[index] += product
            grad = grad * gain
            middle = jnp.mean(product * gain, axis=0, keepdims=True)
            start = index * width + low
            rows[start : start + HEAD] = inverse * (grad - hat * middle)
    rows_out[...] = rows[...].astype(BF16)
    inverse = inverse_ref[0]
    pieces = (r0, r1, r2, r3)
    scales[...] = mods[0].T

    def weights(relative):
        scale = 1.0 + scales[span(me, relative, width), 1:2]
        return pieces[relative][0].astype(F32) * inverse * scale

    split_out(me, wqkv_t, rows_out[...], width, near, far, keep, over, weights)

    @pl.when(pl.program_id(0) == pl.num_programs(0) - 1)
    def _():
        for index in range(2):
            gains_out[index : index + 1] = jnp.sum(gains_sum[index].T, axis=0, keepdims=True)


def columns_of(mods, width):
    return mods[0].T[:width]


def columns(values):
    lanes = lax.broadcasted_iota(jnp.int32, (values[0].shape[0], 128), 1)
    out = jnp.zeros((values[0].shape[0], 128), F32)
    for index, value in enumerate(values):
        out = jnp.where(lanes == index, value, out)
    return out


def sum_parts(values, width):
    return values[0, width : width + 1].astype(F32) + values[0, width + 8 : width + 9].astype(F32)


def total_inner(far, far_core, across, width):
    return (sum_parts(far, width) + sum_parts(far_core, width) + sum_parts(across, width)) / (4 * width)


def middle_back_kernel(
    s_ref, far, far_core, keep, core, across, cot, middle, branch, inverse_ref, mods,
    grad_out, piece_out, sums_out,
):
    width = keep.shape[1]
    modulation = columns_of(mods, width)
    inverse = inverse_ref[0]
    grad = keep[0] + core[0].astype(F32) + across[0, :width].astype(F32)
    normed = middle[0] * inverse
    inner = total_inner(far, far_core, across, width)
    grad_middle = cot[0] + inverse * (grad * (1.0 + modulation[:, 4:5]) - normed * inner)
    grad_out[0] = grad_middle
    piece_out[0] = (grad_middle * modulation[:, 2:3]).astype(BF16)
    sums_out[0] = columns(
        [
            jnp.sum(grad_middle * branch[0], axis=1, keepdims=True),
            jnp.sum(grad, axis=1, keepdims=True),
            jnp.sum(grad * normed, axis=1, keepdims=True),
        ]
    )


def last_kernel(
    s_ref, far, far_core, keep, core, across, grad_middle, latents, inverse_ref, mods,
    grad_out, back_out, sums_out,
):
    width = keep.shape[1]
    modulation = columns_of(mods, width)
    inverse = inverse_ref[0]
    grad = keep[0] + core[0].astype(F32) + across[0, :width].astype(F32)
    normed = latents[0] * inverse
    inner = total_inner(far, far_core, across, width)
    result = grad_middle[0] + inverse * (grad * (1.0 + modulation[:, 1:2]) - normed * inner)
    grad_out[0] = result
    back_out[0] = result.astype(BF16)
    sums_out[0] = columns(
        [jnp.sum(grad, axis=1, keepdims=True), jnp.sum(grad * normed, axis=1, keepdims=True)]
    )


def relay_kernel(s_ref, far, far_core, over, out):
    width = over.shape[1]
    out[0, :width] = (over[0] + far_core[0, :width].astype(F32)).astype(BF16)
    if out.shape[1] > width:
        inner = sum_parts(far, width) + sum_parts(far_core, width)
        out[0, width:] = two_parts(jnp.broadcast_to(inner, (8, inner.shape[1])))


def relay(scalars, far, far_core, over):
    images = over.shape[0]
    return call(
        relay_kernel, (images,), scalars,
        [by_image(far), by_image(far_core), by_image(over)],
        [image_out(images, far.shape[1:], BF16)],
    )[0]


def accumulate(lefts, rights, out):
    total = dot(lefts[0][...], rights[0][...], (1, 1))
    for left, right in zip(lefts[1:], rights[1:]):
        total += dot(left[...], right[...], (1, 1))
    out[...] = total.astype(out.dtype).reshape(out.shape)


def half_kernel(s_ref, *refs):
    parts = len(refs) // 2 - 1
    lefts, rights, out, kept = refs[:parts], refs[parts : 2 * parts], refs[-2], refs[-1]

    @pl.when(pl.program_id(0) == 0)
    def _():
        accumulate(lefts, rights, out)

    @pl.when(pl.program_id(0) == 1)
    def _():
        accumulate(lefts, rights, kept)


def weight_halves(index, lefts, rights, first, rows):
    half = rows // 2
    outer = rights[0].shape[0]
    place = lambda b, s: (first // half + b * s[0] + (1 - b) * (1 - s[0]), 0)
    ins = [(left, (half, left.shape[1]), place, False) for left in lefts] + [entire(right) for right in rights]
    block = (1, half, outer)
    outs = [(block, kind, block, lambda b, s: (0, 0, 0)) for kind in (BF16, F32)]
    return call(half_kernel, (2,), index, ins, outs)


def attention_weight_kernel(s_ref, *refs):
    parts = len(refs) // 4 - 1
    rows, heads, inputs, grads = (refs[i * parts : (i + 1) * parts] for i in range(4))
    out1, kept1, out2, kept2, total = refs[4 * parts :]
    group = pl.program_id(0)
    half = total.shape[0] // 2

    @pl.when(group < 3)
    def _():
        accumulate(rows, inputs, total)

    @pl.when(group == 3)
    def _():
        accumulate(heads, grads, total)

    def store(index, out, kept):
        out[0] = total[pl.ds(pl.multiple_of((1 - index) * half, 16), half)].astype(BF16)
        kept[0] = total[pl.ds(pl.multiple_of(index * half, 16), half)]

    @pl.when(group < 2)
    def _():
        store(s_ref[0], out1, kept1)

    @pl.when(group >= 2)
    def _():
        store(s_ref[1], out2, kept2)


def attention_weight_halves(indices, rows, heads, inputs, grads):
    size = heads[0].shape[0]
    outer = inputs[0].shape[0]
    ins = [(left, (size, left.shape[1]), lambda g, s: (jnp.minimum(g, 2), 0), False) for left in rows]
    ins += [entire(array) for array in heads + inputs + grads]
    shape, block = (2, size // 2, outer), (1, size // 2, outer)
    outs = []
    for place in (lambda g, s: (jnp.minimum(g, 1), 0, 0), lambda g, s: (jnp.maximum(g - 2, 0), 0, 0)):
        outs += [(shape, BF16, block, place), (shape, F32, block, place)]
    return call(attention_weight_kernel, (4,), indices, ins, outs, scratch=[pltpu.VMEM((size, outer), F32)])


def paired_kernel(s_ref, *refs):
    out = refs[-1]
    blocks = pl.num_programs(0) // 4
    units = out.shape[2]
    for index, source in enumerate(refs[:-1]):

        @pl.when(pl.program_id(0) // blocks == index)
        def _():
            values = source[0].astype(F32)
            for pair in range(out.shape[1]):
                out[:, pair, :] = values[:, pair * units : (pair + 1) * units]


def paired(indices, sources, pairs, size):
    _, half, outer = sources[0].shape
    blocks = half // size
    ins = [
        (a, (1, size, outer), lambda b, s, f=i * blocks: (0, jnp.clip(b - f, 0, blocks - 1), 0), False)
        for i, a in enumerate(sources)
    ]
    shape = (4 * half, pairs, outer // pairs)

    def place(b, s):
        chunk, within = b // (2 * blocks), b % (2 * blocks)
        own = jnp.where(chunk == 0, s[0], s[1])
        return (chunk * 2 * blocks + ((within // blocks) ^ own) * blocks + within % blocks, 0, 0)

    return call(paired_kernel, (4 * blocks,), indices, ins, [(shape, F32, (size,) + shape[1:], place)])[0]


def add_split_kernel(s_ref, own_a, got_a, own_b, got_b, out, kept):
    out[...] = (own_a[...] + got_a[...].astype(F32)).astype(BF16)
    kept[...] = own_b[...] + got_b[...].astype(F32)


def add_split(index, own, received, axis):
    groups, rows, outer = own.shape
    cut = 3 if outer % 384 == 0 else 1
    size = outer // cut
    if axis == 1:
        shape = (groups, rows // 2, outer)
        block = (1, rows // 2, size)
        here = lambda g, c, s: (g, s[0], c)
        there = lambda g, c, s: (g, 1 - s[0], c)
    else:
        half = groups // 2
        shape = (half, rows, outer)
        block = (1, rows, size)
        here = lambda g, c, s: (s[0] * half + g, 0, c)
        there = lambda g, c, s: ((1 - s[0]) * half + g, 0, c)
    plain = lambda g, c, s: (g, 0, c)
    ins = [
        (own, block, there, False),
        (received, block, there, False),
        (own, block, here, False),
        (received, block, here, False),
    ]
    outs = [(shape, BF16, block, plain), (shape, F32, block, plain)]
    return call(add_split_kernel, (shape[0], cut), index, ins, outs)


def unfold_kernel(s_ref, *refs):
    out = refs[-1]
    blocks = pl.num_programs(0) // (len(refs) - 1)
    for index, source in enumerate(refs[:-1]):

        @pl.when(pl.program_id(0) // blocks == index)
        def _():
            out[0] = source[0].astype(F32)


def unfold(index, segments):
    rows, outer = segments[0][0].shape[1:]
    ins = []
    for mine, other, group in segments:
        for half in (mine, other):
            ins.append((half, (1, rows, outer), lambda b, s, g=group: (g, 0, 0), False))
    place = lambda b, s: (b // 2, (b % 2) ^ s[0], 0)
    outs = [((len(segments), 2 * rows, outer), F32, (1, rows, outer), place)]
    return call(unfold_kernel, (len(ins),), index, ins, outs)[0]


def unfold_pair_kernel(s_ref, mine1, other1, mine2, other2, qkv, proj):
    step = pl.program_id(0)
    for index, source in enumerate((mine1, other1, mine2, other2)):

        @pl.when((step // 4) * 2 + step % 2 == index)
        def _():
            values = source[0].astype(F32)

            @pl.when(step < 6)
            def _():
                qkv[0] = values

            @pl.when(step >= 6)
            def _():
                proj[...] = values


def unfold_pair(indices, sources):
    _, half, outer = sources[0].shape
    block = (1, half, outer)
    first = lambda b, s: (jnp.minimum(b // 2, 1), 0, 0)
    second = lambda b, s: (jnp.maximum(b // 2 - 2, 0), 0, 0)
    ins = [(a, block, first if i < 2 else second, False) for i, a in enumerate(sources)]

    def row(b, s):
        return (b % 2) ^ jnp.where(b < 4, s[0], s[1])

    outs = [
        (
            (3, 2 * half, outer), F32, block,
            lambda b, s: (jnp.minimum(b // 2, 2), row(jnp.minimum(b, 5), s), 0),
        ),
        ((2 * half, outer), F32, block[1:], lambda b, s: (row(jnp.maximum(b, 6), s), 0)),
    ]
    return call(unfold_pair_kernel, (8,), indices, ins, outs)


class Order:
    def __init__(self):
        self.last = None

    def __call__(self, step, *args):
        if self.last is not None:
            args = lax.optimization_barrier((self.last, *args))[1:]
        result = step(*args)
        self.last = jax.tree.leaves(result)
        return result


class Reduction:
    def __init__(self, order, second_first=False):
        self.order = order
        self.bits = bits_of("dp")
        if second_first and len(self.bits) > 1:
            self.bits[:2] = self.bits[1::-1]
        self.levels = []

    def index(self, bit):
        return has_bit("dp", bit).astype(jnp.int32)[None]

    def first(self):
        return self.index(self.bits[0])

    def begin(self, out, own):
        self.own = own
        self.received = exchange(out, "dp", self.bits[0])

    def halve(self, level):
        if level >= len(self.bits):
            return
        bit = self.bits[level]
        groups, rows, _ = self.own.shape
        if rows % 16 == 0:
            axis = 1
        elif groups % 2 == 0:
            axis = 0
        else:
            axis = None
        if axis is None:
            self.own = self.order(lambda a, b: a + b.astype(F32), self.own, self.received)
            self.received = exchange(self.own.astype(BF16), "dp", bit)
            return
        index = self.index(bit)
        out, self.own = self.order(lambda a, b: add_split(index, a, b, axis), self.own, self.received)
        self.received = exchange(out, "dp", bit)
        self.levels.append((bit, axis))

    def join(self):
        self.own = self.order(lambda a, b: (a + b.astype(F32)).astype(BF16), self.own, self.received)
        bit = self.levels[-1][0] if self.levels else self.bits[0]
        self.received = exchange(self.own, "dp", bit)

    def double(self, level):
        if level >= len(self.levels):
            return
        bit, axis = self.levels[-1 - level]
        later = has_bit("dp", bit)
        self.own = self.order(lambda a, b: in_order(a, b, later, axis, jnp.concatenate), self.own, self.received)
        outer = self.levels[-2 - level][0] if level + 1 < len(self.levels) else self.bits[0]
        self.received = exchange(self.own, "dp", outer)


def rope_tables():
    quarter = HEAD // 4
    frequency = 10000.0 ** (-np.arange(quarter, dtype=np.float32) / quarter)
    patches = np.arange(P_SIZE)
    row = (patches // GRID).astype(np.float32)[None, :] * frequency[:, None]
    col = (patches % GRID).astype(np.float32)[None, :] * frequency[:, None]
    cos = np.concatenate([np.cos(row), np.cos(row), np.cos(col), np.cos(col)])
    sin = np.concatenate([-np.sin(row), np.sin(row), -np.sin(col), np.sin(col)])
    return jnp.asarray(cos, F32), jnp.asarray(sin, F32)


def einsum(spec, *operands):
    return jnp.einsum(spec, *operands, preferred_element_type=F32)


PARTS = ((0, 4),)


def pack_kernel(s_ref, rows, out):
    out[...] = rows[...].astype(BF16)


def last_slots(count, rows):
    slots = rows.shape[0]
    place = lambda i, s: (lax.rem(s[0] - IMG_DEV + i + slots, slots), 0, 0)
    ins = [(rows, (1,) + rows.shape[1:], place, False)]
    return call(pack_kernel, (IMG_DEV,), count, ins, [image_out(IMG_DEV, rows.shape[1:], BF16)])[0]


def transpose_kernel(s_ref, values, out):
    out[...] = values[...].T


def transposed(scalars, array):
    rows, outer = array.shape
    ins = [(array, (rows, 128), lambda i, s: (0, i), False)]
    return call(transpose_kernel, (outer // 128,), scalars, ins, [((outer, rows), array.dtype, (128, rows), lambda i, s: (i, 0))])[0]


def share_kernel(device_ref, facts, ids_out, own_out, load_out, histogram):
    devices, slots = facts.shape[0], facts.shape[1] - 1
    for b in range(NBINS):
        histogram[b] = 0

    def count(i, carry):
        for j in range(slots):
            b = facts[i, j]
            histogram[b] = histogram[b] + jnp.where(j < facts[i, slots], 1, 0)
        return carry

    lax.fori_loop(0, devices, count, 0)

    def place(i, carry):
        came, before = carry
        for k in range(IMG_DEV):
            moved = (i - 1) * slots + lax.rem(before - IMG_DEV + k + slots, slots)
            ids_out[i * IMG_DEV + k] = jnp.where(k >= IMG_DEV - came, moved, i * slots + k)

        @pl.when(i == device_ref[0])
        def _():
            own_out[0] = came

        return came + facts[i, slots] - IMG_DEV, facts[i, slots]

    lax.fori_loop(0, devices, place, (0, 0))
    for k in range(IMG_DEV):
        slot = ids_out[device_ref[0] * IMG_DEV + k]
        owner, j = lax.div(slot, slots), lax.rem(slot, slots)
        load_out[k] = histogram[facts[owner, j]]
        load_out[IMG_DEV + k] = jnp.where(j < facts[owner, slots], 1, 0)


def share(device, facts):
    smem = pl.BlockSpec(memory_space=pltpu.SMEM)
    return pl.pallas_call(
        share_kernel,
        grid_spec=pltpu.PrefetchScalarGridSpec(
            num_scalar_prefetch=1, grid=(), in_specs=[smem], out_specs=[smem] * 3,
            scratch_shapes=[pltpu.SMEM((NBINS,), jnp.int32)],
        ),
        out_shape=[jax.ShapeDtypeStruct((n,), jnp.int32) for n in (facts.shape[0] * IMG_DEV, 8, 2 * IMG_DEV)],
        cost_estimate=pl.CostEstimate(flops=1000, bytes_accessed=1000, transcendentals=0),
    )(device, facts)


def choose(s_ref, start, own, came):
    moved = pl.program_id(0) + start >= IMG_DEV - s_ref[0]
    return jnp.where(moved, came[0].astype(F32), own[0])


def rows_kernel(start, s_ref, own, came, rows_out, piece_out):
    rows = choose(s_ref, start, own, came)
    rows_out[0] = rows
    piece_out[0] = rows.astype(BF16)


def cot_kernel(start, s_ref, own, came, mods, rows_out, piece_out):
    modulation = columns_of(mods, own.shape[1])
    rows = choose(s_ref, start, own, came) * modulation[:, 6:7]
    rows_out[0] = rows
    piece_out[0] = (rows * modulation[:, 5:6]).astype(BF16)


def from_image(array, start):
    rest = array.shape[1:]
    return (array, (1,) + rest, lambda i, s: (i + start,) + (0,) * len(rest), False)


def middle_kernel(s_ref, keep, core, across, rows, mods, branch_out, middle_out, piece_out):
    branch = keep[0] + core[0].astype(F32) + across[0].astype(F32)
    branch_out[0] = branch
    middle = rows[0] + columns_of(mods, rows.shape[1])[:, 2:3] * branch
    middle_out[0] = middle
    piece_out[0] = middle.astype(BF16)


def result_kernel(s_ref, keep, core, across, middle, cot, mods, result_out, back_out, sums_out):
    branch = keep[0] + core[0].astype(F32) + across[0].astype(F32)
    result = middle[0] + columns_of(mods, middle.shape[1])[:, 5:6] * branch
    result_out[0] = result
    back_out[0] = result.astype(BF16)
    sums_out[0] = columns([jnp.sum(cot[0] * branch, axis=1, keepdims=True)])


def home_kernel(starts, s_ref, *refs):
    out = refs[-1]
    parts = len(starts)
    slot = pl.program_id(0)
    came, count = s_ref[0], s_ref[1]
    kept, away = refs[0][0], refs[parts][0].astype(F32)
    for part in range(1, parts):
        kept = jnp.where(slot >= starts[part], refs[part][0], kept)
        place = slot - count + IMG_DEV
        away = jnp.where(place >= starts[part], refs[parts + part][0].astype(F32), away)
    chosen = jnp.where(slot < IMG_DEV - came, kept, away)
    out[0] = jnp.where(slot < count, chosen, 0.0)


def home(scalars, slots, here, back):
    starts, start = [], 0
    for part in here:
        starts.append(start)
        start += part.shape[0]
    block = (1,) + here[0].shape[1:]
    ins = []
    for part, first in zip(here, starts):
        end = part.shape[0] - 1
        ins.append((part, block, lambda i, s, f=first, e=end: (jnp.clip(i - f, 0, e), 0, 0), False))
    for part, first in zip(back, starts):
        end = part.shape[0] - 1
        ins.append(
            (part, block, lambda i, s, f=first, e=end: (jnp.clip(i - s[1] + IMG_DEV - f, 0, e), 0, 0), False)
        )
    outs = [image_out(slots, block[1:], F32)]
    return call(functools.partial(home_kernel, starts), (slots,), scalars, ins, outs)[0]


def local(
    latents,
    condition,
    cotangent,
    noise_bins,
    image_counts,
    ada_weight,
    ada_bias,
    qkv_weight,
    norm_gains,
    proj_weight,
    gate_up_weight,
    down_weight,
):
    slots = latents.shape[0]
    devices = lax.axis_size("dp")
    device = lax.axis_index("dp").astype(jnp.int32)
    part = lax.axis_index("mp")
    me = part.astype(jnp.int32)[None]
    width = latents.shape[2]
    features = qkv_weight.shape[0]
    units = down_weight.shape[0]
    rows_in = latents.transpose(0, 2, 1)
    cot_in = cotangent.transpose(0, 2, 1)
    cos, sin = rope_tables()
    gains = norm_gains.astype(F32).T
    order = Order()

    own_count = image_counts[0]
    silu = jax.nn.silu(condition)
    facts = jnp.concatenate([noise_bins, image_counts]).astype(F32)
    facts = jnp.pad(facts, (0, width - slots - 1))[None]
    message = jnp.concatenate([silu, facts]).astype(BF16)[None]
    latest = (own_count - IMG_DEV + jnp.arange(IMG_DEV)) % slots
    silu_came = shifted(jnp.take(silu, latest, axis=0).astype(BF16), "dp", 1)
    message = gather_small(message, "dp", 0)
    facts = message[:, slots, : slots + 1].astype(jnp.int32)
    rows_last = order(last_slots, image_counts, rows_in)
    share_ids, own_facts, loads = order(lambda f: share(device[None], f), facts)
    came_here = own_facts[:1]
    home_facts = jnp.concatenate([came_here, image_counts])
    rows_last, _ = lax.optimization_barrier((rows_last, own_facts))
    rows_came = shifted(rows_last, "dp", 1)
    came = types.SimpleNamespace()

    silu_near = jnp.concatenate([silu[:IMG_DEV].astype(BF16), silu_came])
    silu_near = gather_small(silu_near, "mp", 1)
    modulation = einsum("bd,dkf->bkf", silu_near, ada_weight) + ada_bias.astype(F32)
    spread_mods = jnp.concatenate([modulation[:, 0:2], modulation[:, 3:5]], axis=1)
    spread_mods = gather_small(spread_mods, "mp", 2)

    parts = PARTS
    count = len(parts)
    state = [types.SimpleNamespace() for _ in parts]
    wqkv = qkv_weight.transpose(1, 2, 0).reshape(3 * width, features)
    weights = types.SimpleNamespace()

    def prepare():
        up = order(lambda w: w.reshape(features, 2 * units), gate_up_weight)
        weights.up = up
        weights.proj_t, weights.qkv_t, weights.down_t = (
            order(lambda w: transposed(me, w), array) for array in (proj_weight, wqkv, down_weight)
        )
        cot_last = order(last_slots, image_counts, cot_in)
        cot_ready, _ = lax.optimization_barrier((cot_last, weights.down_t))
        came.cot = shifted(cot_ready, "dp", 1)

    def prepare_up():
        weights.up_t = order(lambda w: transposed(me, w), weights.up)

    def choose_rows(p):
        start, images = parts[p]
        st = state[p]
        rest = rows_in.shape[1:]
        st.rows, piece = order(
            lambda own, came: call(
                functools.partial(rows_kernel, start), (images,), came_here,
                [from_image(own, start), from_image(came, start)],
                [image_out(images, rest, F32), image_out(images, rest, BF16)],
            ),
            rows_in, rows_came,
        )
        st.pieces_one = spread(piece)

    moved = (jnp.arange(IMG_DEV) >= IMG_DEV - came_here[0])[:, None, None]
    spread_mods = jnp.where(moved, spread_mods[IMG_DEV:], spread_mods[:IMG_DEV])
    spread_mods = jnp.pad(spread_mods, ((0, 0), (0, 4), (0, 0)))
    modulation = jnp.where(moved, modulation[IMG_DEV:], modulation[:IMG_DEV])
    load, live = loads[:IMG_DEV].astype(F32), loads[IMG_DEV:].astype(F32)
    scaling = live * (IMG_DEV * devices) / (NBINS * (load + 1.0 - live))
    scaling = jnp.broadcast_to(scaling[:, None, None], (IMG_DEV, 2, width))
    mods_all = jnp.concatenate([modulation, scaling], axis=1)
    mods_all = jnp.pad(mods_all, ((0, 0), (0, 0), (0, -width % 128)))
    for p, (start, images) in enumerate(parts):
        state[p].mods_full = spread_mods[start : start + images]
        state[p].mods = mods_all[start : start + images]

    def attention(p):
        st = state[p]
        images = parts[p][1]
        st.near, st.far, st.keep, st.over, st.attn, st.raw, st.heads, st.inverse_one = order(
            lambda *a: call(
                attention_kernel, (images,), me,
                [by_image(x) for x in a[:5]] + [entire(x) for x in a[5:]],
                [
                    image_out(images, (width, P_SIZE), BF16),
                    image_out(images, (width, P_SIZE), BF16),
                    image_out(images, (width, P_SIZE), F32),
                    image_out(images, (width, P_SIZE), F32),
                    flat_out(images, features),
                    image_out(images, (3 * width, P_SIZE), F32),
                    flat_out(images, width),
                    image_out(images, (1, P_SIZE), F32),
                ],
                scratch=[pltpu.VMEM((features, P_SIZE), BF16), pltpu.VMEM((width, P_SIZE), F32)],
                us=4.5 * images,
                vmem=48,
            ),
            *st.pieces_one, st.mods_full, wqkv, weights.proj_t, gains, cos, sin,
        )
        far, near, _ = lax.optimization_barrier((st.far, st.near, st.pieces_grad_two[2]))
        st.far_core = exchange(far, "mp", 1)
        st.core = exchange(near, "mp", 1)

    def choose_cot(p):
        start, images = parts[p]
        st = state[p]
        rest = rows_in.shape[1:]
        st.cot, piece = order(
            lambda own, came, mods: call(
                functools.partial(cot_kernel, start), (images,), came_here,
                [from_image(own, start), from_image(came, start), by_image(mods)],
                [image_out(images, rest, F32), image_out(images, rest, BF16)],
            ),
            cot_in, came.cot, st.mods,
        )
        st.pieces_grad_two = spread(piece)

    def relay_one(p):
        st = state[p]
        out = order(lambda *a: relay(me, *a), st.far, st.far_core, st.over)
        st.across = exchange(out, "mp", 2)

    def middle(p):
        st = state[p]
        images = parts[p][1]
        rest = (width, P_SIZE)
        st.branch_one, st.middle, piece = order(
            lambda keep, core, *a: call(
                middle_kernel, (images,), me,
                [by_image(keep), by_image(core)] + [by_image(x) for x in a],
                [image_out(images, rest, F32), image_out(images, rest, F32), image_out(images, rest, BF16)],
            ),
            st.keep, st.core, st.across, st.rows, st.mods,
        )
        st.pieces_two = spread(piece)

    def mlp(p):
        st = state[p]
        images = parts[p][1]
        (
            st.near_a, st.far_a, st.keep_a, st.over_a,
            st.near_b, st.far_b, st.keep_b, st.over_b,
            st.mlp, st.hidden, st.grad_rows_two, st.grad_two, st.inverse_two,
        ) = order(
            lambda *a: call(
                mlp_kernel, (images,), me,
                [by_image(x) for x in a[:9]] + [entire(x) for x in a[9:]],
                [
                    image_out(images, (width, P_SIZE), BF16),
                    image_out(images, (width, P_SIZE), BF16),
                    image_out(images, (width, P_SIZE), F32),
                    image_out(images, (width, P_SIZE), F32),
                    image_out(images, (width, P_SIZE), BF16),
                    image_out(images, (width + 16, P_SIZE), BF16),
                    image_out(images, (width, P_SIZE), F32),
                    image_out(images, (width, P_SIZE), F32),
                    flat_out(images, features),
                    flat_out(images, units),
                    flat_out(images, 2 * units),
                    flat_out(images, features),
                    image_out(images, (1, P_SIZE), F32),
                ],
                scratch=[pltpu.VMEM((features, P_SIZE), BF16), pltpu.VMEM((features, P_SIZE), F32)],
                us=6.0 * images,
                vmem=48,
            ),
            *st.pieces_two, *st.pieces_grad_two, st.mods_full,
            weights.up_t, weights.up, weights.down_t, down_weight,
        )
        st.far_core_b = exchange(st.far_b, "mp", 1)
        st.core_b = exchange(st.near_b, "mp", 1)

    def relay_three(p):
        st = state[p]
        out = order(lambda *a: relay(me, *a), st.far_b, st.far_core_b, st.over_b)
        st.across_b = exchange(out, "mp", 2)

    def middle_back(p):
        st = state[p]
        images = parts[p][1]
        st.grad_middle, piece, st.sums_two = order(
            lambda *a: call(
                middle_back_kernel, (images,), me, [by_image(x) for x in a],
                [
                    image_out(images, (width, P_SIZE), F32),
                    image_out(images, (width, P_SIZE), BF16),
                    image_out(images, (width, 128), F32),
                ],
            ),
            st.far_b, st.far_core_b, st.keep_b, st.core_b, st.across_b, st.cot, st.middle,
            st.branch_one, st.inverse_two, st.mods,
        )
        st.pieces_grad_one = spread(piece)

    def result_core(p):
        st = state[p]
        far, near, _ = lax.optimization_barrier((st.far_a, st.near_a, order.last))
        st.far_core_a = exchange(far, "mp", 1)
        st.core_a = exchange(near, "mp", 1)

    def relay_two(p):
        st = state[p]
        out = order(lambda *a: relay(me, *a), st.far_a, st.far_core_a, st.over_a)
        st.across_a = exchange(out, "mp", 2)

    def result(p):
        st = state[p]
        images = parts[p][1]
        st.result, back, st.sums_three = order(
            lambda keep, core, *a: call(
                result_kernel, (images,), me,
                [by_image(keep), by_image(core)] + [by_image(x) for x in a],
                [
                    image_out(images, (width, P_SIZE), F32),
                    image_out(images, (width, P_SIZE), BF16),
                    image_out(images, (width, 128), F32),
                ],
            ),
            st.keep_a, st.core_a, st.across_a, st.middle, st.cot, st.mods,
        )
        st.result_out = back

    def attention_back(p):
        st = state[p]
        images = parts[p][1]
        st.near_c, st.far_c, st.keep_c, st.over_c, st.grad_rows_one, st.grad_one, st.gain_sums = order(
            lambda *a: call(
                attention_back_kernel, (images,), me,
                [by_image(x) for x in a[:11]] + [entire(x) for x in a[11:]],
                [
                    image_out(images, (width, P_SIZE), BF16),
                    image_out(images, (width + 16, P_SIZE), BF16),
                    image_out(images, (width, P_SIZE), F32),
                    image_out(images, (width, P_SIZE), F32),
                    flat_out(images, 3 * width),
                    flat_out(images, features),
                    ((2, HEAD), F32, (2, HEAD), lambda i, s: (0, 0)),
                ],
                scratch=[
                    pltpu.VMEM((features, P_SIZE), BF16),
                    pltpu.VMEM((width, P_SIZE), F32),
                    pltpu.VMEM((3 * width, P_SIZE), F32),
                    pltpu.VMEM((features, 8), F32),
                    pltpu.VMEM((2, HEAD, P_SIZE), F32),
                ],
                us=4.5 * images,
                vmem=48,
            ),
            *st.pieces_grad_one, *st.pieces_one, st.inverse_one, st.mods_full, st.raw,
            proj_weight, weights.qkv_t, gains, cos, sin,
        )
        st.far_core_c = exchange(st.far_c, "mp", 1)
        st.core_c = exchange(st.near_c, "mp", 1)

    def relay_four(p):
        st = state[p]
        out = order(lambda *a: relay(me, *a), st.far_c, st.far_core_c, st.over_c)
        st.across_c = exchange(out, "mp", 2)

    def last(p):
        st = state[p]
        images = parts[p][1]
        st.grad_latent, back, st.sums_one = order(
            lambda *a: call(
                last_kernel, (images,), me, [by_image(x) for x in a],
                [
                    image_out(images, (width, P_SIZE), F32),
                    image_out(images, (width, P_SIZE), BF16),
                    image_out(images, (width, 128), F32),
                ],
            ),
            st.far_c, st.far_core_c, st.keep_c, st.core_c, st.across_c, st.grad_middle, st.rows,
            st.inverse_one, st.mods,
        )
        st.latent_out = back

    def each(field):
        return [field(st) for st in state]

    attn1 = Reduction(order, True)
    attn2 = Reduction(order, False)
    up1 = Reduction(order, False)
    up2 = Reduction(order, False)
    down = Reduction(order, True)

    def attention_weights():
        indices = jnp.concatenate([attn1.first(), attn2.first()])
        out1, own1, out2, own2 = order(
            lambda *a: attention_weight_halves(indices, *(a[i * count : (i + 1) * count] for i in range(4))),
            *each(lambda s: s.grad_rows_one), *each(lambda s: s.heads),
            *each(lambda s: s.attn), *each(lambda s: s.grad_one),
        )
        attn1.begin(out1, own1)
        attn2.begin(out2, own2)

    def begin(reduction):
        if reduction is down:
            lefts, rights, first, rows = each(lambda s: s.hidden), each(lambda s: s.grad_two), 0, units
        else:
            lefts, rights, rows = each(lambda s: s.mlp), each(lambda s: s.grad_rows_two), features // 2
            first = 0 if reduction is up1 else rows
        index = reduction.first()
        reduction.begin(
            *order(lambda *a: weight_halves(index, a[:count], a[count:], first, rows), *lefts, *rights)
        )

    def halve(reduction, level):
        reduction.halve(level)

    def join(reduction):
        for level in range(3, len(reduction.bits)):
            reduction.halve(level)
        reduction.join()
        for level in range(0, len(reduction.levels) - 2):
            reduction.double(level)

    def double(reduction, step):
        reduction.double(max(0, len(reduction.levels) - 2) + step)

    def unfolded(reduction, groups):
        index = reduction.first()
        return order(lambda a, b: unfold(index, [(a, b, g) for g in groups]), reduction.own, reduction.received)

    def finish_attention():
        done.qkv = order(
            lambda *a: unfold_pair(jnp.concatenate([attn1.first(), attn2.first()]), a),
            attn1.own, attn1.received, attn2.own, attn2.received,
        )

    def finish_down():
        done.down = unfolded(down, (0,))[0]

    def finish_up():
        indices = jnp.concatenate([up1.first(), up2.first()])
        done.up = order(
            lambda *a: paired(indices, a, 2, features // 8), up1.own, up1.received, up2.own, up2.received
        )

    done = types.SimpleNamespace()

    def send_result(p):
        out, _ = lax.optimization_barrier((state[p].result_out, order.last))
        state[p].result_back = shifted(out, "dp", -1)

    def send_latent(p):
        out, _ = lax.optimization_barrier((state[p].latent_out, order.last))
        state[p].latent_back = shifted(out, "dp", -1)

    def modulation_back():
        columns_one, columns_two, columns_three = (
            jnp.concatenate(each(field))
            for field in (lambda s: s.sums_one, lambda s: s.sums_two, lambda s: s.sums_three)
        )
        grad_mod = jnp.stack(
            [
                columns_one[..., 0],
                columns_one[..., 1],
                columns_two[..., 0],
                columns_two[..., 1],
                columns_two[..., 2],
                columns_three[..., 0],
            ]
        ).astype(BF16)
        gain_sums = sum(each(lambda s: s.gain_sums)).reshape(1, -1)
        high = gain_sums.astype(BF16)
        gain_row = jnp.concatenate([high, (gain_sums - high.astype(F32)).astype(BF16)], axis=1)
        sent = jnp.concatenate([grad_mod.reshape(6 * IMG_DEV, width), gain_row])[None]
        done.message = sent
        done.bits = bits_of("dp")
        modulation_send()

    def modulation_send():
        done.other = exchange(done.message, "dp", done.bits[0])

    def modulation_step():
        later = has_bit("dp", done.bits.pop(0))
        done.message = order(lambda a, b: in_order(a, b, later, 0, jnp.concatenate), done.message, done.other)
        if done.bits:
            modulation_send()

    def ada_back():
        while done.bits:
            modulation_step()
        sent = done.message
        mod_share = sent[:, : 6 * IMG_DEV].reshape(devices, 6, IMG_DEV, width).transpose(1, 0, 2, 3)
        mod_share = mod_share.reshape(6, devices * IMG_DEV, width)
        gain_sums = jnp.sum(sent[:, 6 * IMG_DEV].astype(F32), axis=0).reshape(2, 2, HEAD)
        done.gains = sum_small(gain_sums[0] + gain_sums[1], "mp")
        silu_all = gather_small(message[:, :slots], "mp", 2).reshape(devices * slots, -1)
        silu_share = jnp.take(silu_all, share_ids, axis=0)
        done.ada = order(lambda a, b: einsum("kbf,bd->kfd", a, b), mod_share, silu_share)
        done.bias = jnp.sum(mod_share.astype(F32), axis=1)

        slot = jnp.arange(slots)
        stays = slot < IMG_DEV - came_here[0]
        away_place = jnp.clip(slot - own_count + IMG_DEV, 0, IMG_DEV - 1)
        share_place = jnp.where(stays, device * IMG_DEV + slot, (device + 1) * IMG_DEV + away_place)
        share_place = jnp.clip(share_place, 0, devices * IMG_DEV - 1)
        live_here = (slot < own_count).astype(BF16)
        mod_slots = jnp.take(mod_share, share_place, axis=1) * live_here[None, :, None]
        grad_silu = sum_small(einsum("kbf,dkf->bd", mod_slots, ada_weight), "mp")
        grad_silu = lax.dynamic_slice_in_dim(grad_silu, part * width, width, 1)
        sigmoid_cond = jax.nn.sigmoid(condition)
        done.cond = grad_silu * sigmoid_cond * (1.0 + condition * (1.0 - sigmoid_cond))

    def home_result():
        done.output = order(
            lambda *a: home(home_facts, slots, a[:count], a[count:]), *each(lambda s: s.result), *each(lambda s: s.result_back)
        )

    def home_latent():
        done.latent = order(
            lambda *a: home(home_facts, slots, a[:count], a[count:]), *each(lambda s: s.grad_latent), *each(lambda s: s.latent_back)
        )

    prepare()
    choose_rows(0)
    choose_cot(0)
    attention(0)
    relay_one(0)
    prepare_up()
    middle(0)
    mlp(0)
    relay_three(0)
    begin(up1)
    begin(down)
    begin(up2)
    middle_back(0)
    halve(up1, 1)
    result_core(0)
    halve(down, 1)
    relay_two(0)
    halve(up2, 1)
    halve(up1, 2)
    attention_back(0)
    join(up1)
    halve(down, 2)
    attention_weights()
    halve(up2, 2)
    relay_four(0)
    double(up1, 0)
    result(0)
    send_result(0)
    join(down)
    halve(attn1, 1)
    halve(attn2, 1)
    last(0)
    send_latent(0)
    join(up2)
    double(up1, 1)
    modulation_back()
    home_result()
    halve(attn1, 2)
    double(down, 0)
    halve(attn2, 2)
    double(up2, 0)
    join(attn1)
    modulation_step()
    join(attn2)
    home_latent()
    double(down, 1)
    double(up2, 1)
    modulation_step()
    double(attn1, 0)
    double(attn2, 0)
    finish_down()
    finish_up()
    double(attn1, 1)
    double(attn2, 1)
    modulation_step()
    ada_back()
    finish_attention()
    return (
        done.output.transpose(0, 2, 1),
        done.latent.transpose(0, 2, 1),
        done.cond,
        done.ada.transpose(2, 0, 1),
        done.bias,
        done.qkv[0].transpose(2, 0, 1),
        done.gains,
        done.qkv[1],
        done.up,
        done.down,
    )


def solution(mesh):
    return jax.shard_map(
        local,
        mesh=mesh,
        in_specs=(
            P("dp", None, "mp"),
            P("dp", "mp"),
            P("dp", None, "mp"),
            P("dp"),
            P("dp"),
            P(None, None, "mp"),
            P(None, "mp"),
            P(None, None, "mp"),
            P(),
            P("mp", None),
            P(None, None, "mp"),
            P("mp", None),
        ),
        out_specs=(
            P("dp", None, "mp"),
            P("dp", None, "mp"),
            P("dp", "mp"),
            P(None, None, "mp"),
            P(None, "mp"),
            P(None, None, "mp"),
            P(),
            P("mp", None),
            P(None, None, "mp"),
            P("mp", None),
        ),
        check_vma=False,
    )
```

```python
import functools
import types

import jax
import jax.numpy as jnp
import numpy as np
from jax import lax
from jax.experimental import pallas as pl
from jax.experimental.pallas import tpu as pltpu
from jax.sharding import PartitionSpec as P

HEAD = 72
P_SIZE = 256
GRID = 16
IMG_DEV = 4
NBINS = 8

EPSILON = 1e-06
F32 = jnp.float32
BF16 = jnp.bfloat16
MIB = 1 << 20
WEIGHT = 0.1 * 1e9


def exchange(value, axis, bit):
    pairs = [(i, i ^ bit) for i in range(lax.axis_size(axis))]
    return lax.ppermute(value, axis, pairs)


def shifted(value, axis, by):
    devices = lax.axis_size(axis)
    pairs = [(i, i + by) for i in range(devices) if 0 <= i + by < devices]
    return lax.ppermute(value, axis, pairs)


def bits_of(axis):
    bits, bit = [], 1
    while bit < lax.axis_size(axis):
        bits.append(bit)
        bit *= 2
    return bits


def has_bit(axis, bit):
    return (lax.axis_index(axis) & bit) != 0


def in_order(mine, other, later, axis, join):
    return jnp.where(later, join([other, mine], axis=axis), join([mine, other], axis=axis))


def gather_small(value, axis, dim):
    for bit in bits_of(axis):
        other = exchange(value, axis, bit)
        value = in_order(value, other, has_bit(axis, bit), dim, jnp.concatenate)
    return value


def sum_small(value, axis):
    for bit in bits_of(axis):
        value = value + exchange(value, axis, bit)
    return value


def pick(value, index, dim):
    return lax.dynamic_index_in_dim(value, index, dim, keepdims=False)


def spread(piece):
    core = exchange(piece, "mp", 1)
    over = exchange(piece, "mp", 2)
    both = exchange(over, "mp", 1)
    return [piece, core, over, both]


def call(kernel, grid, scalars, ins, outs, scratch=(), vmem=24, us=3.0):
    in_specs = [
        pl.BlockSpec(block, index, pipeline_mode=pl.Buffered(1)) if whole else pl.BlockSpec(block, index)
        for _, block, index, whole in ins
    ]
    return pl.pallas_call(
        kernel,
        grid_spec=pltpu.PrefetchScalarGridSpec(
            num_scalar_prefetch=1,
            grid=grid,
            in_specs=in_specs,
            out_specs=[pl.BlockSpec(block, index) for _, _, block, index in outs],
            scratch_shapes=list(scratch),
        ),
        out_shape=[jax.ShapeDtypeStruct(shape, kind) for shape, kind, _, _ in outs],
        compiler_params=pltpu.CompilerParams(
            dimension_semantics=("arbitrary",) * len(grid), vmem_limit_bytes=vmem * MIB
        ),
        cost_estimate=pl.CostEstimate(flops=int(us * WEIGHT), bytes_accessed=1000, transcendentals=0),
    )(scalars, *(a for a, _, _, _ in ins))


def by_image(array):
    rest = array.shape[1:]
    return (array, (1,) + rest, lambda i, s: (i,) + (0,) * len(rest), False)


def entire(array):
    return (array, array.shape, lambda i, s: (0,) * array.ndim, True)


def image_out(images, rest, kind):
    return ((images,) + rest, kind, (1,) + rest, lambda i, s: (i,) + (0,) * len(rest))


def flat_out(images, rows):
    return ((rows, images * P_SIZE), BF16, (rows, P_SIZE), lambda i, s: (0, i))


def dot(a, b, over=(1, 0)):
    return lax.dot_general(a, b, (((over[0],), (over[1],)), ((), ())), preferred_element_type=F32)


def span(me, relative, width):
    return pl.ds(pl.multiple_of((me ^ relative) * width, 32), width)


def assemble(pieces, full, me):
    width = pieces[0].shape[1]
    for relative, piece in enumerate(pieces):
        full[span(me, relative, width), :] = piece[0]


def inverse_rms(rows):
    return lax.rsqrt(jnp.mean(rows * rows, axis=0, keepdims=True) + EPSILON)


def swap_quarters(v):
    rows = lax.broadcasted_iota(jnp.int32, v.shape, 0)
    quarter = HEAD // 4
    first = (rows % (2 * quarter)) < quarter
    return jnp.where(first, pltpu.roll(v, HEAD - quarter, 0), pltpu.roll(v, quarter, 0))


def head_parts(raw, gain, cos, sin):
    inverse = inverse_rms(raw)
    hat = raw * inverse
    scaled = hat * gain
    return hat, inverse, (scaled * cos + swap_quarters(scaled) * sin).astype(BF16)


def probabilities(queries, keys):
    scores = dot(keys, queries, (0, 0)) * HEAD ** (-0.5)
    weights = jnp.exp(scores - jnp.max(scores, axis=0, keepdims=True))
    return weights * (1.0 / jnp.sum(weights, axis=0, keepdims=True))


def split_out(me, weight, rows, width, near, far, keep, over, weights=None):
    inner = 0.0
    for relative, out in ((3, far), (1, near), (0, keep), (2, over)):
        product = dot(weight[span(me, relative, width), :], rows)
        out[0, :width] = product.astype(out.dtype)
        if weights is not None:
            inner += jnp.sum(product * weights(relative), axis=0, keepdims=True)
    if weights is not None:
        far[0, width:] = two_parts(jnp.broadcast_to(inner, (8, inner.shape[1])))


def two_parts(values):
    high = values.astype(BF16)
    return jnp.concatenate([high.astype(F32), values - high.astype(F32)], axis=0).astype(BF16)


def attention_kernel(
    me_ref, p0, p1, p2, p3, mods, wqkv, wproj, gains, cos_ref, sin_ref,
    near, far, keep, over, attn_out, raw_out, heads_out, inverse_out,
    full, heads,
):
    me = me_ref[0]
    width = p0.shape[1]
    assemble((p0, p1, p2, p3), full, me)
    rows = full[...].astype(F32)
    inverse = inverse_rms(rows)
    inverse_out[0] = inverse
    columns_in = mods[0].T
    attn = (rows * inverse * (1.0 + columns_in[:, 1:2]) + columns_in[:, 0:1]).astype(BF16)
    attn_out[...] = attn
    raw_out[0] = dot(wqkv[...], attn)
    cos, sin = cos_ref[...], sin_ref[...]
    for head in range(width // HEAD):
        low = head * HEAD
        _, _, queries = head_parts(raw_out[0, low : low + HEAD], gains[:, 0:1], cos, sin)
        low += width
        _, _, keys = head_parts(raw_out[0, low : low + HEAD], gains[:, 1:2], cos, sin)
        low += width
        values = raw_out[0, low : low + HEAD].astype(BF16)
        attention = probabilities(queries, keys).astype(BF16)
        heads[head * HEAD : (head + 1) * HEAD] = dot(values, attention)
    out = heads[...].astype(BF16)
    heads_out[...] = out
    split_out(me, wproj, out, width, near, far, keep, over)


def mlp_kernel(
    me_ref, p0, p1, p2, p3, g0, g1, g2, g3, mods, wup_t, wup, wdown_t, wdown,
    near_a, far_a, keep_a, over_a, near_b, far_b, keep_b, over_b, mlp_out, hidden_out, rows_out, grad_out, inverse_out,
    full, modulated,
):
    me = me_ref[0]
    width = p0.shape[1]
    units = wdown.shape[0]
    assemble((p0, p1, p2, p3), full, me)
    rows = full[...].astype(F32)
    inverse = inverse_rms(rows)
    inverse_out[0] = inverse
    columns_in = mods[0].T
    scaled = rows * inverse * (1.0 + columns_in[:, 3:4])
    modulated[...] = scaled
    mlp = (scaled + columns_in[:, 2:3]).astype(BF16)
    mlp_out[...] = mlp
    gate = dot(wup_t[:units], mlp)
    up = dot(wup_t[units:], mlp)
    sigmoid = jax.nn.sigmoid(gate)
    silu = gate * sigmoid
    hidden = (silu * up).astype(BF16)
    hidden_out[...] = hidden
    assemble((g0, g1, g2, g3), full, me)
    grad_out[...] = full[...]
    grad_hidden = dot(wdown[...], full[...])
    rows_out[:units] = (grad_hidden * up * sigmoid * (1.0 + gate * (1.0 - sigmoid))).astype(BF16)
    rows_out[units:] = (grad_hidden * silu).astype(BF16)
    split_out(
        me, wup, rows_out[...], width, near_b, far_b, keep_b, over_b, lambda r: modulated[span(me, r, width), :]
    )
    split_out(me, wdown_t, hidden, width, near_a, far_a, keep_a, over_a)


def attention_back_kernel(
    me_ref, p0, p1, p2, p3, r0, r1, r2, r3, inverse_ref, mods, raw, wproj, wqkv_t, gains, cos_ref, sin_ref,
    near, far, keep, over, rows_out, grad_out, gains_out,
    full, heads, rows, scales, gains_sum,
):
    me = me_ref[0]
    width = p0.shape[1]
    assemble((p0, p1, p2, p3), full, me)
    grad_out[...] = full[...]
    heads[...] = dot(wproj[...], full[...])
    cos, sin = cos_ref[...], sin_ref[...]
    scale = HEAD ** (-0.5)

    @pl.when(pl.program_id(0) == 0)
    def _():
        gains_sum[...] = jnp.zeros_like(gains_sum)

    for head in range(width // HEAD):
        low = head * HEAD
        gain_q, gain_k = gains[:, 0:1], gains[:, 1:2]
        hat_q, inverse_q, queries = head_parts(raw[0, low : low + HEAD], gain_q, cos, sin)
        hat_k, inverse_k, keys = head_parts(raw[0, width + low : width + low + HEAD], gain_k, cos, sin)
        values = raw[0, 2 * width + low : 2 * width + low + HEAD].astype(BF16)
        grad_heads = heads[low : low + HEAD].astype(BF16)
        probability = probabilities(queries, keys)
        grad_attention = dot(values, grad_heads, (0, 0))
        rows[2 * width + low : 2 * width + low + HEAD] = dot(grad_heads, probability.astype(BF16), (1, 1))
        inner = jnp.sum(probability * grad_attention, axis=0, keepdims=True)
        grad_scores = (probability * (grad_attention - inner)).astype(BF16)
        grad_q = dot(keys, grad_scores) * scale
        grad_k = dot(queries, grad_scores, (1, 1)) * scale
        for index, grad, hat, inverse, gain in (
            (0, grad_q, hat_q, inverse_q, gain_q),
            (1, grad_k, hat_k, inverse_k, gain_k),
        ):
            grad = grad * cos - swap_quarters(grad) * sin
            product = grad * hat
            gains_sum[index] += product
            grad = grad * gain
            middle = jnp.mean(product * gain, axis=0, keepdims=True)
            start = index * width + low
            rows[start : start + HEAD] = inverse * (grad - hat * middle)
    rows_out[...] = rows[...].astype(BF16)
    inverse = inverse_ref[0]
    pieces = (r0, r1, r2, r3)
    scales[...] = mods[0].T

    def weights(relative):
        scale = 1.0 + scales[span(me, relative, width), 1:2]
        return pieces[relative][0].astype(F32) * inverse * scale

    split_out(me, wqkv_t, rows_out[...], width, near, far, keep, over, weights)

    @pl.when(pl.program_id(0) == pl.num_programs(0) - 1)
    def _():
        for index in range(2):
            gains_out[index : index + 1] = jnp.sum(gains_sum[index].T, axis=0, keepdims=True)


def columns_of(mods, width):
    return mods[0].T[:width]


def columns(values):
    lanes = lax.broadcasted_iota(jnp.int32, (values[0].shape[0], 128), 1)
    out = jnp.zeros((values[0].shape[0], 128), F32)
    for index, value in enumerate(values):
        out = jnp.where(lanes == index, value, out)
    return out


def sum_parts(values, width):
    return values[0, width : width + 1].astype(F32) + values[0, width + 8 : width + 9].astype(F32)


def total_inner(far, far_core, across, width):
    return (sum_parts(far, width) + sum_parts(far_core, width) + sum_parts(across, width)) / (4 * width)


def middle_back_kernel(
    s_ref, far, far_core, keep, core, across, cot, middle, branch, inverse_ref, mods,
    grad_out, piece_out, sums_out,
):
    width = keep.shape[1]
    modulation = columns_of(mods, width)
    inverse = inverse_ref[0]
    grad = keep[0] + core[0].astype(F32) + across[0, :width].astype(F32)
    normed = middle[0] * inverse
    inner = total_inner(far, far_core, across, width)
    grad_middle = cot[0] + inverse * (grad * (1.0 + modulation[:, 4:5]) - normed * inner)
    grad_out[0] = grad_middle
    piece_out[0] = (grad_middle * modulation[:, 2:3]).astype(BF16)
    sums_out[0] = columns(
        [
            jnp.sum(grad_middle * branch[0], axis=1, keepdims=True),
            jnp.sum(grad, axis=1, keepdims=True),
            jnp.sum(grad * normed, axis=1, keepdims=True),
        ]
    )


def last_kernel(
    s_ref, far, far_core, keep, core, across, grad_middle, latents, inverse_ref, mods,
    grad_out, back_out, sums_out,
):
    width = keep.shape[1]
    modulation = columns_of(mods, width)
    inverse = inverse_ref[0]
    grad = keep[0] + core[0].astype(F32) + across[0, :width].astype(F32)
    normed = latents[0] * inverse
    inner = total_inner(far, far_core, across, width)
    result = grad_middle[0] + inverse * (grad * (1.0 + modulation[:, 1:2]) - normed * inner)
    grad_out[0] = result
    back_out[0] = result.astype(BF16)
    sums_out[0] = columns(
        [jnp.sum(grad, axis=1, keepdims=True), jnp.sum(grad * normed, axis=1, keepdims=True)]
    )


def relay_kernel(s_ref, far, far_core, over, out):
    width = over.shape[1]
    out[0, :width] = (over[0] + far_core[0, :width].astype(F32)).astype(BF16)
    if out.shape[1] > width:
        inner = sum_parts(far, width) + sum_parts(far_core, width)
        out[0, width:] = two_parts(jnp.broadcast_to(inner, (8, inner.shape[1])))


def relay(scalars, far, far_core, over):
    images = over.shape[0]
    return call(
        relay_kernel, (images,), scalars,
        [by_image(far), by_image(far_core), by_image(over)],
        [image_out(images, far.shape[1:], BF16)],
    )[0]


def accumulate(lefts, rights, out):
    total = dot(lefts[0][...], rights[0][...], (1, 1))
    for left, right in zip(lefts[1:], rights[1:]):
        total += dot(left[...], right[...], (1, 1))
    out[...] = total.astype(out.dtype).reshape(out.shape)


def half_kernel(s_ref, *refs):
    parts = len(refs) // 2 - 1
    lefts, rights, out, kept = refs[:parts], refs[parts : 2 * parts], refs[-2], refs[-1]

    @pl.when(pl.program_id(0) == 0)
    def _():
        accumulate(lefts, rights, out)

    @pl.when(pl.program_id(0) == 1)
    def _():
        accumulate(lefts, rights, kept)


def weight_halves(index, lefts, rights, first, rows):
    half = rows // 2
    outer = rights[0].shape[0]
    place = lambda b, s: (first // half + b * s[0] + (1 - b) * (1 - s[0]), 0)
    ins = [(left, (half, left.shape[1]), place, False) for left in lefts] + [entire(right) for right in rights]
    block = (1, half, outer)
    outs = [(block, kind, block, lambda b, s: (0, 0, 0)) for kind in (BF16, F32)]
    return call(half_kernel, (2,), index, ins, outs)


def attention_weight_kernel(s_ref, *refs):
    parts = len(refs) // 4 - 1
    rows, heads, inputs, grads = (refs[i * parts : (i + 1) * parts] for i in range(4))
    out1, kept1, out2, kept2, total = refs[4 * parts :]
    group = pl.program_id(0)
    half = total.shape[0] // 2

    @pl.when(group < 3)
    def _():
        accumulate(rows, inputs, total)

    @pl.when(group == 3)
    def _():
        accumulate(heads, grads, total)

    def store(index, out, kept):
        out[0] = total[pl.ds(pl.multiple_of((1 - index) * half, 16), half)].astype(BF16)
        kept[0] = total[pl.ds(pl.multiple_of(index * half, 16), half)]

    @pl.when(group < 2)
    def _():
        store(s_ref[0], out1, kept1)

    @pl.when(group >= 2)
    def _():
        store(s_ref[1], out2, kept2)


def attention_weight_halves(indices, rows, heads, inputs, grads):
    size = heads[0].shape[0]
    outer = inputs[0].shape[0]
    ins = [(left, (size, left.shape[1]), lambda g, s: (jnp.minimum(g, 2), 0), False) for left in rows]
    ins += [entire(array) for array in heads + inputs + grads]
    shape, block = (2, size // 2, outer), (1, size // 2, outer)
    outs = []
    for place in (lambda g, s: (jnp.minimum(g, 1), 0, 0), lambda g, s: (jnp.maximum(g - 2, 0), 0, 0)):
        outs += [(shape, BF16, block, place), (shape, F32, block, place)]
    return call(attention_weight_kernel, (4,), indices, ins, outs, scratch=[pltpu.VMEM((size, outer), F32)])


def paired_kernel(s_ref, *refs):
    out = refs[-1]
    blocks = pl.num_programs(0) // 4
    units = out.shape[2]
    for index, source in enumerate(refs[:-1]):

        @pl.when(pl.program_id(0) // blocks == index)
        def _():
            values = source[0].astype(F32)
            for pair in range(out.shape[1]):
                out[:, pair, :] = values[:, pair * units : (pair + 1) * units]


def paired(indices, sources, pairs, size):
    _, half, outer = sources[0].shape
    blocks = half // size
    ins = [
        (a, (1, size, outer), lambda b, s, f=i * blocks: (0, jnp.clip(b - f, 0, blocks - 1), 0), False)
        for i, a in enumerate(sources)
    ]
    shape = (4 * half, pairs, outer // pairs)

    def place(b, s):
        chunk, within = b // (2 * blocks), b % (2 * blocks)
        own = jnp.where(chunk == 0, s[0], s[1])
        return (chunk * 2 * blocks + ((within // blocks) ^ own) * blocks + within % blocks, 0, 0)

    return call(paired_kernel, (4 * blocks,), indices, ins, [(shape, F32, (size,) + shape[1:], place)])[0]


def add_split_kernel(s_ref, own_a, got_a, own_b, got_b, out, kept):
    out[...] = (own_a[...] + got_a[...].astype(F32)).astype(BF16)
    kept[...] = own_b[...] + got_b[...].astype(F32)


def add_split(index, own, received, axis):
    groups, rows, outer = own.shape
    cut = 3 if outer % 384 == 0 else 1
    size = outer // cut
    if axis == 1:
        shape = (groups, rows // 2, outer)
        block = (1, rows // 2, size)
        here = lambda g, c, s: (g, s[0], c)
        there = lambda g, c, s: (g, 1 - s[0], c)
    else:
        half = groups // 2
        shape = (half, rows, outer)
        block = (1, rows, size)
        here = lambda g, c, s: (s[0] * half + g, 0, c)
        there = lambda g, c, s: ((1 - s[0]) * half + g, 0, c)
    plain = lambda g, c, s: (g, 0, c)
    ins = [
        (own, block, there, False),
        (received, block, there, False),
        (own, block, here, False),
        (received, block, here, False),
    ]
    outs = [(shape, BF16, block, plain), (shape, F32, block, plain)]
    return call(add_split_kernel, (shape[0], cut), index, ins, outs)


def unfold_kernel(s_ref, *refs):
    out = refs[-1]
    blocks = pl.num_programs(0) // (len(refs) - 1)
    for index, source in enumerate(refs[:-1]):

        @pl.when(pl.program_id(0) // blocks == index)
        def _():
            out[0] = source[0].astype(F32)


def unfold(index, segments):
    rows, outer = segments[0][0].shape[1:]
    ins = []
    for mine, other, group in segments:
        for half in (mine, other):
            ins.append((half, (1, rows, outer), lambda b, s, g=group: (g, 0, 0), False))
    place = lambda b, s: (b // 2, (b % 2) ^ s[0], 0)
    outs = [((len(segments), 2 * rows, outer), F32, (1, rows, outer), place)]
    return call(unfold_kernel, (len(ins),), index, ins, outs)[0]


def unfold_pair_kernel(s_ref, mine1, other1, mine2, other2, qkv, proj):
    step = pl.program_id(0)
    for index, source in enumerate((mine1, other1, mine2, other2)):

        @pl.when((step // 4) * 2 + step % 2 == index)
        def _():
            values = source[0].astype(F32)

            @pl.when(step < 6)
            def _():
                qkv[0] = values

            @pl.when(step >= 6)
            def _():
                proj[...] = values


def unfold_pair(indices, sources):
    _, half, outer = sources[0].shape
    block = (1, half, outer)
    first = lambda b, s: (jnp.minimum(b // 2, 1), 0, 0)
    second = lambda b, s: (jnp.maximum(b // 2 - 2, 0), 0, 0)
    ins = [(a, block, first if i < 2 else second, False) for i, a in enumerate(sources)]

    def row(b, s):
        return (b % 2) ^ jnp.where(b < 4, s[0], s[1])

    outs = [
        (
            (3, 2 * half, outer), F32, block,
            lambda b, s: (jnp.minimum(b // 2, 2), row(jnp.minimum(b, 5), s), 0),
        ),
        ((2 * half, outer), F32, block[1:], lambda b, s: (row(jnp.maximum(b, 6), s), 0)),
    ]
    return call(unfold_pair_kernel, (8,), indices, ins, outs)


class Order:
    def __init__(self):
        self.last = None

    def __call__(self, step, *args):
        if self.last is not None:
            args = lax.optimization_barrier((self.last, *args))[1:]
        result = step(*args)
        self.last = jax.tree.leaves(result)
        return result


class Reduction:
    def __init__(self, order, second_first=False):
        self.order = order
        self.bits = bits_of("dp")
        if second_first and len(self.bits) > 1:
            self.bits[:2] = self.bits[1::-1]
        self.levels = []

    def index(self, bit):
        return has_bit("dp", bit).astype(jnp.int32)[None]

    def first(self):
        return self.index(self.bits[0])

    def begin(self, out, own):
        self.own = own
        self.received = exchange(out, "dp", self.bits[0])

    def halve(self, level):
        if level >= len(self.bits):
            return
        bit = self.bits[level]
        groups, rows, _ = self.own.shape
        if rows % 16 == 0:
            axis = 1
        elif groups % 2 == 0:
            axis = 0
        else:
            axis = None
        if axis is None:
            self.own = self.order(lambda a, b: a + b.astype(F32), self.own, self.received)
            self.received = exchange(self.own.astype(BF16), "dp", bit)
            return
        index = self.index(bit)
        out, self.own = self.order(lambda a, b: add_split(index, a, b, axis), self.own, self.received)
        self.received = exchange(out, "dp", bit)
        self.levels.append((bit, axis))

    def join(self):
        self.own = self.order(lambda a, b: (a + b.astype(F32)).astype(BF16), self.own, self.received)
        bit = self.levels[-1][0] if self.levels else self.bits[0]
        self.received = exchange(self.own, "dp", bit)

    def double(self, level):
        if level >= len(self.levels):
            return
        bit, axis = self.levels[-1 - level]
        later = has_bit("dp", bit)
        self.own = self.order(lambda a, b: in_order(a, b, later, axis, jnp.concatenate), self.own, self.received)
        outer = self.levels[-2 - level][0] if level + 1 < len(self.levels) else self.bits[0]
        self.received = exchange(self.own, "dp", outer)


def rope_tables():
    quarter = HEAD // 4
    frequency = 10000.0 ** (-np.arange(quarter, dtype=np.float32) / quarter)
    patches = np.arange(P_SIZE)
    row = (patches // GRID).astype(np.float32)[None, :] * frequency[:, None]
    col = (patches % GRID).astype(np.float32)[None, :] * frequency[:, None]
    cos = np.concatenate([np.cos(row), np.cos(row), np.cos(col), np.cos(col)])
    sin = np.concatenate([-np.sin(row), np.sin(row), -np.sin(col), np.sin(col)])
    return jnp.asarray(cos, F32), jnp.asarray(sin, F32)


def einsum(spec, *operands):
    return jnp.einsum(spec, *operands, preferred_element_type=F32)


PARTS = ((0, 4),)


def pack_kernel(s_ref, rows, out):
    out[...] = rows[...].astype(BF16)


def last_slots(count, rows):
    slots = rows.shape[0]
    place = lambda i, s: (lax.rem(s[0] - IMG_DEV + i + slots, slots), 0, 0)
    ins = [(rows, (1,) + rows.shape[1:], place, False)]
    return call(pack_kernel, (IMG_DEV,), count, ins, [image_out(IMG_DEV, rows.shape[1:], BF16)])[0]


def transpose_kernel(s_ref, values, out):
    out[...] = values[...].T


def transposed(scalars, array):
    rows, outer = array.shape
    ins = [(array, (rows, 128), lambda i, s: (0, i), False)]
    return call(transpose_kernel, (outer // 128,), scalars, ins, [((outer, rows), array.dtype, (128, rows), lambda i, s: (i, 0))])[0]


def share_kernel(device_ref, facts, ids_out, own_out, load_out, histogram):
    devices, slots = facts.shape[0], facts.shape[1] - 1
    for b in range(NBINS):
        histogram[b] = 0

    def count(i, carry):
        for j in range(slots):
            b = facts[i, j]
            histogram[b] = histogram[b] + jnp.where(j < facts[i, slots], 1, 0)
        return carry

    lax.fori_loop(0, devices, count, 0)

    def place(i, carry):
        came, before = carry
        for k in range(IMG_DEV):
            moved = (i - 1) * slots + lax.rem(before - IMG_DEV + k + slots, slots)
            ids_out[i * IMG_DEV + k] = jnp.where(k >= IMG_DEV - came, moved, i * slots + k)

        @pl.when(i == device_ref[0])
        def _():
            own_out[0] = came

        return came + facts[i, slots] - IMG_DEV, facts[i, slots]

    lax.fori_loop(0, devices, place, (0, 0))
    for k in range(IMG_DEV):
        slot = ids_out[device_ref[0] * IMG_DEV + k]
        owner, j = lax.div(slot, slots), lax.rem(slot, slots)
        load_out[k] = histogram[facts[owner, j]]
        load_out[IMG_DEV + k] = jnp.where(j < facts[owner, slots], 1, 0)


def share(device, facts):
    smem = pl.BlockSpec(memory_space=pltpu.SMEM)
    return pl.pallas_call(
        share_kernel,
        grid_spec=pltpu.PrefetchScalarGridSpec(
            num_scalar_prefetch=1, grid=(), in_specs=[smem], out_specs=[smem] * 3,
            scratch_shapes=[pltpu.SMEM((NBINS,), jnp.int32)],
        ),
        out_shape=[jax.ShapeDtypeStruct((n,), jnp.int32) for n in (facts.shape[0] * IMG_DEV, 8, 2 * IMG_DEV)],
        cost_estimate=pl.CostEstimate(flops=1000, bytes_accessed=1000, transcendentals=0),
    )(device, facts)


def choose(s_ref, start, own, came):
    moved = pl.program_id(0) + start >= IMG_DEV - s_ref[0]
    return jnp.where(moved, came[0].astype(F32), own[0])


def rows_kernel(start, s_ref, own, came, rows_out, piece_out):
    rows = choose(s_ref, start, own, came)
    rows_out[0] = rows
    piece_out[0] = rows.astype(BF16)


def cot_kernel(start, s_ref, own, came, mods, rows_out, piece_out):
    modulation = columns_of(mods, own.shape[1])
    rows = choose(s_ref, start, own, came) * modulation[:, 6:7]
    rows_out[0] = rows
    piece_out[0] = (rows * modulation[:, 5:6]).astype(BF16)


def from_image(array, start):
    rest = array.shape[1:]
    return (array, (1,) + rest, lambda i, s: (i + start,) + (0,) * len(rest), False)


def middle_kernel(s_ref, keep, core, across, rows, mods, branch_out, middle_out, piece_out):
    branch = keep[0] + core[0].astype(F32) + across[0].astype(F32)
    branch_out[0] = branch
    middle = rows[0] + columns_of(mods, rows.shape[1])[:, 2:3] * branch
    middle_out[0] = middle
    piece_out[0] = middle.astype(BF16)


def result_kernel(s_ref, keep, core, across, middle, cot, mods, result_out, back_out, sums_out):
    branch = keep[0] + core[0].astype(F32) + across[0].astype(F32)
    result = middle[0] + columns_of(mods, middle.shape[1])[:, 5:6] * branch
    result_out[0] = result
    back_out[0] = result.astype(BF16)
    sums_out[0] = columns([jnp.sum(cot[0] * branch, axis=1, keepdims=True)])


def home_kernel(starts, s_ref, *refs):
    out = refs[-1]
    parts = len(starts)
    slot = pl.program_id(0)
    came, count = s_ref[0], s_ref[1]
    kept, away = refs[0][0], refs[parts][0].astype(F32)
    for part in range(1, parts):
        kept = jnp.where(slot >= starts[part], refs[part][0], kept)
        place = slot - count + IMG_DEV
        away = jnp.where(place >= starts[part], refs[parts + part][0].astype(F32), away)
    chosen = jnp.where(slot < IMG_DEV - came, kept, away)
    out[0] = jnp.where(slot < count, chosen, 0.0)


def home(scalars, slots, here, back):
    starts, start = [], 0
    for part in here:
        starts.append(start)
        start += part.shape[0]
    block = (1,) + here[0].shape[1:]
    ins = []
    for part, first in zip(here, starts):
        end = part.shape[0] - 1
        ins.append((part, block, lambda i, s, f=first, e=end: (jnp.clip(i - f, 0, e), 0, 0), False))
    for part, first in zip(back, starts):
        end = part.shape[0] - 1
        ins.append(
            (part, block, lambda i, s, f=first, e=end: (jnp.clip(i - s[1] + IMG_DEV - f, 0, e), 0, 0), False)
        )
    outs = [image_out(slots, block[1:], F32)]
    return call(functools.partial(home_kernel, starts), (slots,), scalars, ins, outs)[0]


def local(
    latents,
    condition,
    cotangent,
    noise_bins,
    image_counts,
    ada_weight,
    ada_bias,
    qkv_weight,
    norm_gains,
    proj_weight,
    gate_up_weight,
    down_weight,
):
    slots = latents.shape[0]
    devices = lax.axis_size("dp")
    device = lax.axis_index("dp").astype(jnp.int32)
    part = lax.axis_index("mp")
    me = part.astype(jnp.int32)[None]
    width = latents.shape[2]
    features = qkv_weight.shape[0]
    units = down_weight.shape[0]
    rows_in = latents.transpose(0, 2, 1)
    cot_in = cotangent.transpose(0, 2, 1)
    cos, sin = rope_tables()
    gains = norm_gains.astype(F32).T
    order = Order()

    own_count = image_counts[0]
    silu = jax.nn.silu(condition)
    facts = jnp.concatenate([noise_bins, image_counts]).astype(F32)
    facts = jnp.pad(facts, (0, width - slots - 1))[None]
    message = jnp.concatenate([silu, facts]).astype(BF16)[None]
    latest = (own_count - IMG_DEV + jnp.arange(IMG_DEV)) % slots
    silu_came = shifted(jnp.take(silu, latest, axis=0).astype(BF16), "dp", 1)
    message = gather_small(message, "dp", 0)
    facts = message[:, slots, : slots + 1].astype(jnp.int32)
    rows_last = order(last_slots, image_counts, rows_in)
    share_ids, own_facts, loads = order(lambda f: share(device[None], f), facts)
    came_here = own_facts[:1]
    home_facts = jnp.concatenate([came_here, image_counts])
    rows_last, _ = lax.optimization_barrier((rows_last, own_facts))
    rows_came = shifted(rows_last, "dp", 1)
    came = types.SimpleNamespace()

    silu_near = jnp.concatenate([silu[:IMG_DEV].astype(BF16), silu_came])
    silu_near = gather_small(silu_near, "mp", 1)
    modulation = einsum("bd,dkf->bkf", silu_near, ada_weight) + ada_bias.astype(F32)
    spread_mods = jnp.concatenate([modulation[:, 0:2], modulation[:, 3:5]], axis=1)
    spread_mods = gather_small(spread_mods, "mp", 2)

    parts = PARTS
    count = len(parts)
    state = [types.SimpleNamespace() for _ in parts]
    wqkv = qkv_weight.transpose(1, 2, 0).reshape(3 * width, features)
    weights = types.SimpleNamespace()

    def prepare():
        up = order(lambda w: w.reshape(features, 2 * units), gate_up_weight)
        weights.up = up
        weights.proj_t, weights.qkv_t, weights.down_t = (
            order(lambda w: transposed(me, w), array) for array in (proj_weight, wqkv, down_weight)
        )
        cot_last = order(last_slots, image_counts, cot_in)
        cot_ready, _ = lax.optimization_barrier((cot_last, weights.down_t))
        came.cot = shifted(cot_ready, "dp", 1)

    def prepare_up():
        weights.up_t = order(lambda w: transposed(me, w), weights.up)

    def choose_rows(p):
        start, images = parts[p]
        st = state[p]
        rest = rows_in.shape[1:]
        st.rows, piece = order(
            lambda own, came: call(
                functools.partial(rows_kernel, start), (images,), came_here,
                [from_image(own, start), from_image(came, start)],
                [image_out(images, rest, F32), image_out(images, rest, BF16)],
            ),
            rows_in, rows_came,
        )
        st.pieces_one = spread(piece)

    moved = (jnp.arange(IMG_DEV) >= IMG_DEV - came_here[0])[:, None, None]
    spread_mods = jnp.where(moved, spread_mods[IMG_DEV:], spread_mods[:IMG_DEV])
    spread_mods = jnp.pad(spread_mods, ((0, 0), (0, 4), (0, 0)))
    modulation = jnp.where(moved, modulation[IMG_DEV:], modulation[:IMG_DEV])
    load, live = loads[:IMG_DEV].astype(F32), loads[IMG_DEV:].astype(F32)
    scaling = live * (IMG_DEV * devices) / (NBINS * (load + 1.0 - live))
    scaling = jnp.broadcast_to(scaling[:, None, None], (IMG_DEV, 2, width))
    mods_all = jnp.concatenate([modulation, scaling], axis=1)
    mods_all = jnp.pad(mods_all, ((0, 0), (0, 0), (0, -width % 128)))
    for p, (start, images) in enumerate(parts):
        state[p].mods_full = spread_mods[start : start + images]
        state[p].mods = mods_all[start : start + images]

    def attention(p):
        st = state[p]
        images = parts[p][1]
        st.near, st.far, st.keep, st.over, st.attn, st.raw, st.heads, st.inverse_one = order(
            lambda *a: call(
                attention_kernel, (images,), me,
                [by_image(x) for x in a[:5]] + [entire(x) for x in a[5:]],
                [
                    image_out(images, (width, P_SIZE), BF16),
                    image_out(images, (width, P_SIZE), BF16),
                    image_out(images, (width, P_SIZE), F32),
                    image_out(images, (width, P_SIZE), F32),
                    flat_out(images, features),
                    image_out(images, (3 * width, P_SIZE), F32),
                    flat_out(images, width),
                    image_out(images, (1, P_SIZE), F32),
                ],
                scratch=[pltpu.VMEM((features, P_SIZE), BF16), pltpu.VMEM((width, P_SIZE), F32)],
                us=4.5 * images,
                vmem=48,
            ),
            *st.pieces_one, st.mods_full, wqkv, weights.proj_t, gains, cos, sin,
        )
        far, near, _ = lax.optimization_barrier((st.far, st.near, st.pieces_grad_two[2]))
        st.far_core = exchange(far, "mp", 1)
        st.core = exchange(near, "mp", 1)

    def choose_cot(p):
        start, images = parts[p]
        st = state[p]
        rest = rows_in.shape[1:]
        st.cot, piece = order(
            lambda own, came, mods: call(
                functools.partial(cot_kernel, start), (images,), came_here,
                [from_image(own, start), from_image(came, start), by_image(mods)],
                [image_out(images, rest, F32), image_out(images, rest, BF16)],
            ),
            cot_in, came.cot, st.mods,
        )
        st.pieces_grad_two = spread(piece)

    def relay_one(p):
        st = state[p]
        out = order(lambda *a: relay(me, *a), st.far, st.far_core, st.over)
        st.across = exchange(out, "mp", 2)

    def middle(p):
        st = state[p]
        images = parts[p][1]
        rest = (width, P_SIZE)
        st.branch_one, st.middle, piece = order(
            lambda keep, core, *a: call(
                middle_kernel, (images,), me,
                [by_image(keep), by_image(core)] + [by_image(x) for x in a],
                [image_out(images, rest, F32), image_out(images, rest, F32), image_out(images, rest, BF16)],
            ),
            st.keep, st.core, st.across, st.rows, st.mods,
        )
        st.pieces_two = spread(piece)

    def mlp(p):
        st = state[p]
        images = parts[p][1]
        (
            st.near_a, st.far_a, st.keep_a, st.over_a,
            st.near_b, st.far_b, st.keep_b, st.over_b,
            st.mlp, st.hidden, st.grad_rows_two, st.grad_two, st.inverse_two,
        ) = order(
            lambda *a: call(
                mlp_kernel, (images,), me,
                [by_image(x) for x in a[:9]] + [entire(x) for x in a[9:]],
                [
                    image_out(images, (width, P_SIZE), BF16),
                    image_out(images, (width, P_SIZE), BF16),
                    image_out(images, (width, P_SIZE), F32),
                    image_out(images, (width, P_SIZE), F32),
                    image_out(images, (width, P_SIZE), BF16),
                    image_out(images, (width + 16, P_SIZE), BF16),
                    image_out(images, (width, P_SIZE), F32),
                    image_out(images, (width, P_SIZE), F32),
                    flat_out(images, features),
                    flat_out(images, units),
                    flat_out(images, 2 * units),
                    flat_out(images, features),
                    image_out(images, (1, P_SIZE), F32),
                ],
                scratch=[pltpu.VMEM((features, P_SIZE), BF16), pltpu.VMEM((features, P_SIZE), F32)],
                us=6.0 * images,
                vmem=48,
            ),
            *st.pieces_two, *st.pieces_grad_two, st.mods_full,
            weights.up_t, weights.up, weights.down_t, down_weight,
        )
        st.far_core_b = exchange(st.far_b, "mp", 1)
        st.core_b = exchange(st.near_b, "mp", 1)

    def relay_three(p):
        st = state[p]
        out = order(lambda *a: relay(me, *a), st.far_b, st.far_core_b, st.over_b)
        st.across_b = exchange(out, "mp", 2)

    def middle_back(p):
        st = state[p]
        images = parts[p][1]
        st.grad_middle, piece, st.sums_two = order(
            lambda *a: call(
                middle_back_kernel, (images,), me, [by_image(x) for x in a],
                [
                    image_out(images, (width, P_SIZE), F32),
                    image_out(images, (width, P_SIZE), BF16),
                    image_out(images, (width, 128), F32),
                ],
            ),
            st.far_b, st.far_core_b, st.keep_b, st.core_b, st.across_b, st.cot, st.middle,
            st.branch_one, st.inverse_two, st.mods,
        )
        st.pieces_grad_one = spread(piece)

    def result_core(p):
        st = state[p]
        far, near, _ = lax.optimization_barrier((st.far_a, st.near_a, order.last))
        st.far_core_a = exchange(far, "mp", 1)
        st.core_a = exchange(near, "mp", 1)

    def relay_two(p):
        st = state[p]
        out = order(lambda *a: relay(me, *a), st.far_a, st.far_core_a, st.over_a)
        st.across_a = exchange(out, "mp", 2)

    def result(p):
        st = state[p]
        images = parts[p][1]
        st.result, back, st.sums_three = order(
            lambda keep, core, *a: call(
                result_kernel, (images,), me,
                [by_image(keep), by_image(core)] + [by_image(x) for x in a],
                [
                    image_out(images, (width, P_SIZE), F32),
                    image_out(images, (width, P_SIZE), BF16),
                    image_out(images, (width, 128), F32),
                ],
            ),
            st.keep_a, st.core_a, st.across_a, st.middle, st.cot, st.mods,
        )
        st.result_out = back

    def attention_back(p):
        st = state[p]
        images = parts[p][1]
        st.near_c, st.far_c, st.keep_c, st.over_c, st.grad_rows_one, st.grad_one, st.gain_sums = order(
            lambda *a: call(
                attention_back_kernel, (images,), me,
                [by_image(x) for x in a[:11]] + [entire(x) for x in a[11:]],
                [
                    image_out(images, (width, P_SIZE), BF16),
                    image_out(images, (width + 16, P_SIZE), BF16),
                    image_out(images, (width, P_SIZE), F32),
                    image_out(images, (width, P_SIZE), F32),
                    flat_out(images, 3 * width),
                    flat_out(images, features),
                    ((2, HEAD), F32, (2, HEAD), lambda i, s: (0, 0)),
                ],
                scratch=[
                    pltpu.VMEM((features, P_SIZE), BF16),
                    pltpu.VMEM((width, P_SIZE), F32),
                    pltpu.VMEM((3 * width, P_SIZE), F32),
                    pltpu.VMEM((features, 8), F32),
                    pltpu.VMEM((2, HEAD, P_SIZE), F32),
                ],
                us=4.5 * images,
                vmem=48,
            ),
            *st.pieces_grad_one, *st.pieces_one, st.inverse_one, st.mods_full, st.raw,
            proj_weight, weights.qkv_t, gains, cos, sin,
        )
        st.far_core_c = exchange(st.far_c, "mp", 1)
        st.core_c = exchange(st.near_c, "mp", 1)

    def relay_four(p):
        st = state[p]
        out = order(lambda *a: relay(me, *a), st.far_c, st.far_core_c, st.over_c)
        st.across_c = exchange(out, "mp", 2)

    def last(p):
        st = state[p]
        images = parts[p][1]
        st.grad_latent, back, st.sums_one = order(
            lambda *a: call(
                last_kernel, (images,), me, [by_image(x) for x in a],
                [
                    image_out(images, (width, P_SIZE), F32),
                    image_out(images, (width, P_SIZE), BF16),
                    image_out(images, (width, 128), F32),
                ],
            ),
            st.far_c, st.far_core_c, st.keep_c, st.core_c, st.across_c, st.grad_middle, st.rows,
            st.inverse_one, st.mods,
        )
        st.latent_out = back

    def each(field):
        return [field(st) for st in state]

    attn1 = Reduction(order, True)
    attn2 = Reduction(order, False)
    up1 = Reduction(order, False)
    up2 = Reduction(order, False)
    down = Reduction(order, True)

    def attention_weights():
        indices = jnp.concatenate([attn1.first(), attn2.first()])
        out1, own1, out2, own2 = order(
            lambda *a: attention_weight_halves(indices, *(a[i * count : (i + 1) * count] for i in range(4))),
            *each(lambda s: s.grad_rows_one), *each(lambda s: s.heads),
            *each(lambda s: s.attn), *each(lambda s: s.grad_one),
        )
        attn1.begin(out1, own1)
        attn2.begin(out2, own2)

    def begin(reduction):
        if reduction is down:
            lefts, rights, first, rows = each(lambda s: s.hidden), each(lambda s: s.grad_two), 0, units
        else:
            lefts, rights, rows = each(lambda s: s.mlp), each(lambda s: s.grad_rows_two), features // 2
            first = 0 if reduction is up1 else rows
        index = reduction.first()
        reduction.begin(
            *order(lambda *a: weight_halves(index, a[:count], a[count:], first, rows), *lefts, *rights)
        )

    def halve(reduction, level):
        reduction.halve(level)

    def join(reduction):
        for level in range(3, len(reduction.bits)):
            reduction.halve(level)
        reduction.join()
        for level in range(0, len(reduction.levels) - 2):
            reduction.double(level)

    def double(reduction, step):
        reduction.double(max(0, len(reduction.levels) - 2) + step)

    def unfolded(reduction, groups):
        index = reduction.first()
        return order(lambda a, b: unfold(index, [(a, b, g) for g in groups]), reduction.own, reduction.received)

    def finish_attention():
        done.qkv = order(
            lambda *a: unfold_pair(jnp.concatenate([attn1.first(), attn2.first()]), a),
            attn1.own, attn1.received, attn2.own, attn2.received,
        )

    def finish_down():
        done.down = unfolded(down, (0,))[0]

    def finish_up():
        indices = jnp.concatenate([up1.first(), up2.first()])
        done.up = order(
            lambda *a: paired(indices, a, 2, features // 4), up1.own, up1.received, up2.own, up2.received
        )

    done = types.SimpleNamespace()

    def send_result(p):
        out, _ = lax.optimization_barrier((state[p].result_out, order.last))
        state[p].result_back = shifted(out, "dp", -1)

    def send_latent(p):
        out, _ = lax.optimization_barrier((state[p].latent_out, order.last))
        state[p].latent_back = shifted(out, "dp", -1)

    def modulation_back():
        columns_one, columns_two, columns_three = (
            jnp.concatenate(each(field))
            for field in (lambda s: s.sums_one, lambda s: s.sums_two, lambda s: s.sums_three)
        )
        grad_mod = jnp.stack(
            [
                columns_one[..., 0],
                columns_one[..., 1],
                columns_two[..., 0],
                columns_two[..., 1],
                columns_two[..., 2],
                columns_three[..., 0],
            ]
        ).astype(BF16)
        gain_sums = sum(each(lambda s: s.gain_sums)).reshape(1, -1)
        high = gain_sums.astype(BF16)
        gain_row = jnp.concatenate([high, (gain_sums - high.astype(F32)).astype(BF16)], axis=1)
        sent = jnp.concatenate([grad_mod.reshape(6 * IMG_DEV, width), gain_row])[None]
        done.message = sent
        done.bits = bits_of("dp")
        modulation_send()

    def modulation_send():
        done.other = exchange(done.message, "dp", done.bits[0])

    def modulation_step():
        later = has_bit("dp", done.bits.pop(0))
        done.message = order(lambda a, b: in_order(a, b, later, 0, jnp.concatenate), done.message, done.other)
        if done.bits:
            modulation_send()

    def ada_back():
        while done.bits:
            modulation_step()
        sent = done.message
        mod_share = sent[:, : 6 * IMG_DEV].reshape(devices, 6, IMG_DEV, width).transpose(1, 0, 2, 3)
        mod_share = mod_share.reshape(6, devices * IMG_DEV, width)
        gain_sums = jnp.sum(sent[:, 6 * IMG_DEV].astype(F32), axis=0).reshape(2, 2, HEAD)
        done.gains = sum_small(gain_sums[0] + gain_sums[1], "mp")
        silu_all = gather_small(message[:, :slots], "mp", 2).reshape(devices * slots, -1)
        silu_share = jnp.take(silu_all, share_ids, axis=0)
        done.ada = order(lambda a, b: einsum("kbf,bd->kfd", a, b), mod_share, silu_share)
        done.bias = jnp.sum(mod_share.astype(F32), axis=1)

        slot = jnp.arange(slots)
        stays = slot < IMG_DEV - came_here[0]
        away_place = jnp.clip(slot - own_count + IMG_DEV, 0, IMG_DEV - 1)
        share_place = jnp.where(stays, device * IMG_DEV + slot, (device + 1) * IMG_DEV + away_place)
        share_place = jnp.clip(share_place, 0, devices * IMG_DEV - 1)
        live_here = (slot < own_count).astype(BF16)
        mod_slots = jnp.take(mod_share, share_place, axis=1) * live_here[None, :, None]
        grad_silu = sum_small(einsum("kbf,dkf->bd", mod_slots, ada_weight), "mp")
        grad_silu = lax.dynamic_slice_in_dim(grad_silu, part * width, width, 1)
        sigmoid_cond = jax.nn.sigmoid(condition)
        done.cond = grad_silu * sigmoid_cond * (1.0 + condition * (1.0 - sigmoid_cond))

    def home_result():
        done.output = order(
            lambda *a: home(home_facts, slots, a[:count], a[count:]), *each(lambda s: s.result), *each(lambda s: s.result_back)
        )

    def home_latent():
        done.latent = order(
            lambda *a: home(home_facts, slots, a[:count], a[count:]), *each(lambda s: s.grad_latent), *each(lambda s: s.latent_back)
        )

    prepare()
    choose_rows(0)
    choose_cot(0)
    attention(0)
    relay_one(0)
    prepare_up()
    middle(0)
    mlp(0)
    relay_three(0)
    begin(up1)
    begin(down)
    begin(up2)
    middle_back(0)
    halve(up1, 1)
    result_core(0)
    halve(down, 1)
    relay_two(0)
    halve(up2, 1)
    halve(up1, 2)
    attention_back(0)
    join(up1)
    halve(down, 2)
    attention_weights()
    halve(up2, 2)
    relay_four(0)
    double(up1, 0)
    result(0)
    send_result(0)
    join(down)
    halve(attn1, 1)
    halve(attn2, 1)
    last(0)
    send_latent(0)
    join(up2)
    double(up1, 1)
    modulation_back()
    home_result()
    halve(attn1, 2)
    double(down, 0)
    halve(attn2, 2)
    double(up2, 0)
    join(attn1)
    modulation_step()
    join(attn2)
    home_latent()
    double(down, 1)
    double(up2, 1)
    modulation_step()
    double(attn1, 0)
    double(attn2, 0)
    finish_down()
    finish_up()
    double(attn1, 1)
    double(attn2, 1)
    modulation_step()
    ada_back()
    finish_attention()
    return (
        done.output.transpose(0, 2, 1),
        done.latent.transpose(0, 2, 1),
        done.cond,
        done.ada.transpose(2, 0, 1),
        done.bias,
        done.qkv[0].transpose(2, 0, 1),
        done.gains,
        done.qkv[1],
        done.up,
        done.down,
    )


def solution(mesh):
    return jax.shard_map(
        local,
        mesh=mesh,
        in_specs=(
            P("dp", None, "mp"),
            P("dp", "mp"),
            P("dp", None, "mp"),
            P("dp"),
            P("dp"),
            P(None, None, "mp"),
            P(None, "mp"),
            P(None, None, "mp"),
            P(),
            P("mp", None),
            P(None, None, "mp"),
            P("mp", None),
        ),
        out_specs=(
            P("dp", None, "mp"),
            P("dp", None, "mp"),
            P("dp", "mp"),
            P(None, None, "mp"),
            P(None, "mp"),
            P(None, None, "mp"),
            P(),
            P("mp", None),
            P(None, None, "mp"),
            P("mp", None),
        ),
        check_vma=False,
    )
```
